128 devices in a mesh: experts: 16 (over y, z), dp: 8 (over x, core).
Axes of the slice: x: 4, y: 4, z: 4, core: 2. Of those that a mesh axis runs over, the one named last changes fastest.
Arguments:
- tokens: bfloat16 [384, 50, 512], P(('experts', 'dp')), may hold values from -6 to 6
- cotangent: bfloat16 [384, 50, 512], P(('experts', 'dp')), may hold values from -6 to 6
- norm_gain: bfloat16 [2, 2, 512], P(None, None, ('experts', 'dp')), may hold values from 0.25 to 1.75
- qkv_weight: bfloat16 [2, 512, 1536], P(None, ('experts', 'dp')), may hold values from -0.375 to 0.375
- proj_weight: bfloat16 [2, 512, 512], P(None, ('experts', 'dp')), may hold values from -0.5 to 0.5
- router_weight: bfloat16 [2, 512, 32], P(None, ('experts', 'dp')), may hold values from -0.1875 to 0.1875
- expert_in: bfloat16 [2, 32, 512, 2048], P(None, 'experts', None, 'dp'), may hold values from -0.25 to 0.25
- expert_out: bfloat16 [2, 32, 2048, 512], P(None, 'experts', 'dp'), may hold values from -0.1875 to 0.1875
- routes: int32 [2, 384, 50, 2], P(None, ('experts', 'dp')), may hold values from 0 to 31, all different within a row; in each aligned block of 150 rows (0 to 149, 150 to 299, ..., all dimensions but the last counted through in order) at most 12 rows name the same one
Outputs:
- output: bfloat16 [384, 50, 512], P(('experts', 'dp'))
- grad_tokens: float32 [384, 50, 512], P(('experts', 'dp'))
- grad_gain: float32 [2, 2, 512], P(None, None, ('experts', 'dp'))
- grad_qkv: float32 [2, 512, 1536], P(None, ('experts', 'dp'))
- grad_proj: float32 [2, 512, 512], P(None, ('experts', 'dp'))
- grad_router: float32 [2, 512, 32], P(None, ('experts', 'dp'))
- grad_in: float32 [2, 32, 512, 2048], P(None, 'experts', None, 'dp')
- grad_out: float32 [2, 32, 2048, 512], P(None, 'experts', 'dp')
The draws below stay inside these ranges and needn't reach their ends.
Inputs may be any that keep to these rules, and one draw needn't show every extreme that they name: `routes`: each token names 2 different experts. In the rows of one device (aligned blocks of 150 tokens of one block index), no expert is named more than 12 times, a bound that some block reaches.
All inputs are finite; a program needn't handle non-finite values.
Results may differ from the reference program's by a relative error of at most 0.034.
Values may be sent and summed in bfloat16 or wider, within the bound.
No kernel may reach another device: no remote copies, remote signals or barrier semaphores. Data moves between devices by JAX's collectives and lax.ppermute only.
A program may use at most 128 MiB of HBM per device.

```python
import math
import jax
import jax.numpy as jnp
import numpy as np
from jax import lax

D = 512
HEADS = 8
HEAD_DIM = 64
FF = 2048
EXPERTS = 32
SEQ = 50
TOP = 2
LAYERS = 2
IMG_DEV = 3
TOK_DEV = 150
IMAGES = 384
CAP = 12
N_DP = 8


def shard_levels(own_key, shape, shards, least, top_value):
    factor_of = 1.0
    for dim, parts in shards:
        steps = jax.random.uniform(jax.random.fold_in(jax.random.fold_in(own_key, 6), dim), (parts,), jnp.float32, least / len(shards), top_value / len(shards))
        factor_of = factor_of * jnp.repeat(jnp.exp(steps), shape[dim] // parts).reshape((-1,) + (1,) * (len(shape) - 1 - dim))
    return factor_of


def shared_out(own_key, own, number, rows, number_of, top, reach, skew):
    sequence = jax.random.permutation(own_key, number_of)
    crowded, usual = load_shares(number_of, rows * top, reach, skew, True), load_shares(number_of, rows * top, reach, skew, False)
    places = jnp.arange(number_of)

    def named(tallies, offset_by):
        used = int((tallies > 0).sum())
        fixed = max(1, used // 4)
        passed = fixed + (places - fixed + offset_by * (used - fixed)) % max(1, number_of - fixed)
        return jnp.zeros((number_of,), jnp.int32).at[sequence[jnp.where(places < fixed, places, passed)]].set(jnp.asarray(tallies, jnp.int32))

    tallies = jnp.where(number % 4 == 0, named(crowded, number // 4), named(usual, number - number // 4 - 1))
    mixed = jax.random.permutation(jax.random.fold_in(own, 3), number_of)
    donor, receiver = mixed[0:number_of // 2 * 2:2], mixed[1:number_of // 2 * 2:2]
    margin = jnp.minimum(tallies[donor] - 1, reach - tallies[receiver]) // 2
    margin = jnp.where((donor == sequence[0]) | (receiver == sequence[0]) | (tallies[receiver] == 0), 0, jnp.maximum(margin, 0))
    passed = jax.random.randint(jax.random.fold_in(own, 4), (number_of // 2,), 0, 1 << 20) % (margin + 1)
    tallies = tallies.at[donor].add(-passed).at[receiver].add(passed)
    labels = jnp.searchsorted(jnp.cumsum(tallies), jnp.arange(rows * top), side="right").astype(jnp.int32)
    listing = labels.reshape(top, rows).T
    listing = listing[jax.random.permutation(jax.random.fold_in(own, 1), rows)]
    offset_by = jax.random.randint(jax.random.fold_in(own, 2), (rows, 1), 0, top)
    return jnp.take_along_axis(listing, (jnp.arange(top)[None, :] + offset_by) % top, axis=1)


def load_shares(number_of, total, most, lean, full):
    weights = [(1 << 20) // math.isqrt(grade ** lean) + 1 for grade in range(1, number_of + 1)]
    largest = most if full else min(most, max(-(-total // number_of), total * weights[0] // sum(weights)))
    least = 1 if total - largest >= number_of - 1 else 0
    counts, spare = [largest] + [least] * (number_of - 1), total - largest - least * (number_of - 1)
    while spare > 0:
        candidates = [i for i in range(1, number_of) if counts[i] < largest] or [i for i in range(1, number_of) if counts[i] < most]
        mass, left = sum([weights[i] for i in candidates]), spare
        for i in candidates:
            more = min(most - counts[i], max(1, left * weights[i] // mass), spare)
            counts[i] = counts[i] + more
            spare = spare - more
    return np.array(counts)


def scatter_about(rng, shape, scale, reach, cuts=(), held_as=jnp.bfloat16):
    array = scale * jax.random.normal(rng, shape, jnp.float32)
    if cuts:
        array = array * shard_levels(rng, shape, cuts, -0.22, 0.18)
    return jnp.clip(array, -reach, reach).astype(held_as)


def setup_inputs(seed: int = 0) -> dict:
    arg_keys = jax.random.split(jax.random.key(seed), 10)
    tokens = scatter_about(arg_keys[0], (IMAGES, SEQ, D), 1.0, 6.0, ((0, 128),))
    cotangent = scatter_about(arg_keys[1], (IMAGES, SEQ, D), 1.0, 6.0, ((0, 128),))
    norm_gain = jnp.clip(1.0 + 0.15 * jax.random.normal(arg_keys[2], (LAYERS, 2, D), jnp.float32), 0.25, 1.75).astype(jnp.bfloat16)
    qkv_weight = scatter_about(arg_keys[3], (LAYERS, D, 3 * D), (D // 2) ** -0.5, 0.375, ((1, 128),))
    proj_weight = scatter_about(arg_keys[4], (LAYERS, D, D), (D // 4) ** -0.5, 0.5, ((1, 128),))
    router_weight = scatter_about(arg_keys[5], (LAYERS, D, EXPERTS), (2 * D) ** -0.5, 0.1875, ((1, 128),))
    expert_in = scatter_about(arg_keys[6], (LAYERS, EXPERTS, D, FF), D ** -0.5, 0.25, ((1, 16), (3, 8)))
    expert_out = scatter_about(arg_keys[7], (LAYERS, EXPERTS, FF, D), (FF // 2) ** -0.5, 0.1875, ((1, 16), (2, 8)))
    routes_keys = jax.random.split(jax.random.fold_in(arg_keys[8], 1), LAYERS * IMAGES * SEQ // TOK_DEV)
    routes_turns = jax.random.permutation(jax.random.fold_in(arg_keys[8], 3), LAYERS * IMAGES * SEQ // TOK_DEV)
    routes = jax.vmap(lambda own, number: shared_out(jax.random.fold_in(arg_keys[8], 2), own, number, TOK_DEV, EXPERTS, TOP, CAP, 1))(routes_keys, routes_turns).reshape((LAYERS, IMAGES, SEQ, TOP))
    return dict(tokens=tokens, cotangent=cotangent, norm_gain=norm_gain, qkv_weight=qkv_weight, proj_weight=proj_weight, router_weight=router_weight, expert_in=expert_in, expert_out=expert_out, routes=routes)


EPS = 1e-06
PRECISE = lax.Precision.HIGHEST

@jax.custom_vjp
def low(v):
    return lax.optimization_barrier(v.astype(jnp.bfloat16)).astype(jnp.float32)

@jax.custom_vjp
def low_back(v):
    return v

def low_keep(v):
    return (low(v), None)

def low_pass(kept, grad):
    return (grad,)

def back_keep(v):
    return (v, None)

def back_low(kept, grad):
    return (low(grad),)
low.defvjp(low_keep, low_pass)
low_back.defvjp(back_keep, back_low)

def normalize(values):
    centered = values - lax.optimization_barrier(jnp.mean(values, axis=-1, keepdims=True))
    return centered * lax.rsqrt(lax.optimization_barrier(jnp.mean(centered * centered, axis=-1, keepdims=True)) + EPS)

def attend_group(qkv_rows):
    heads_view = qkv_rows.reshape(qkv_rows.shape[0], qkv_rows.shape[1], 3, HEADS, HEAD_DIM)
    query, keys, values = (heads_view[:, :, 0], heads_view[:, :, 1], heads_view[:, :, 2])
    scores = low_back(jnp.einsum('gqhd,gkhd->ghqk', query, keys, precision=PRECISE) * HEAD_DIM ** (-0.5))
    maximum = lax.optimization_barrier(jnp.max(scores, axis=-1, keepdims=True))
    weights = jnp.exp(scores - maximum)
    probs_low = low(weights / lax.optimization_barrier(jnp.sum(weights, axis=-1, keepdims=True)))
    mixed = jnp.einsum('ghqk,gkhd->gqhd', probs_low, values, precision=PRECISE)
    return mixed.reshape(qkv_rows.shape[0], qkv_rows.shape[1], HEADS * HEAD_DIM)

def expert_block(inputs):
    received, weight_in, weight_out = inputs
    share_width = FF // N_DP
    total = jnp.zeros((received.shape[0], D), jnp.float32)
    for share_index in range(N_DP):
        lower = share_index * share_width
        rows_copy = low_back(received)
        before_gelu = low_back(jnp.dot(rows_copy, weight_in[:, lower:lower + share_width], preferred_element_type=jnp.float32, precision=PRECISE))
        hidden = low(jax.nn.gelu(before_gelu))
        total = total + low(jnp.dot(hidden, weight_out[lower:lower + share_width], preferred_element_type=jnp.float32, precision=PRECISE))
    return low(low_back(total))

def slot_index(route_ids, blocks):
    flat_picks = route_ids.reshape(blocks, -1).astype(jnp.int32)
    one_hot = (flat_picks[:, :, None] == jnp.arange(EXPERTS, dtype=jnp.int32)).astype(jnp.int32)
    before = jnp.cumsum(one_hot, axis=1, dtype=jnp.int32) - one_hot
    slots = lax.optimization_barrier(jnp.sum(before * one_hot, axis=2, dtype=jnp.int32))
    block_ids = jnp.arange(blocks, dtype=jnp.int32)[:, None]
    return (flat_picks * (blocks * CAP) + block_ids * CAP + slots).reshape(-1).astype(jnp.int32)

def apply_layer(stream, gain_rows, qkv_weight, proj_weight, router_weight, weight_in, weight_out, route_ids):
    blocks = IMAGES // IMG_DEV
    first_low = low(normalize(stream) * gain_rows[0])
    qkv_low = low_back(low(jnp.dot(first_low, qkv_weight, preferred_element_type=jnp.float32, precision=PRECISE)))
    grouped = qkv_low.reshape(blocks, IMG_DEV, SEQ, 3 * D)
    mixed = lax.map(jax.checkpoint(attend_group), grouped).reshape(-1, D)
    mixed_low = low_back(low(mixed))
    residual = stream + low_back(jnp.dot(mixed_low, proj_weight, preferred_element_type=jnp.float32, precision=PRECISE))
    second_low = low(normalize(residual) * gain_rows[1])
    logits = jnp.dot(second_low, router_weight, preferred_element_type=jnp.float32, precision=PRECISE)
    shifted = jnp.exp(logits - lax.optimization_barrier(jnp.max(logits, axis=-1, keepdims=True)))
    router_prob = shifted / lax.optimization_barrier(jnp.sum(shifted, axis=-1, keepdims=True))
    picked = route_ids.reshape(-1, TOP).astype(jnp.int32)
    chosen = jnp.take_along_axis(router_prob, picked, axis=1)
    gate_values = chosen / lax.optimization_barrier(jnp.sum(chosen, axis=1, keepdims=True))
    copies = low_back(jnp.broadcast_to(second_low[:, None, :], (second_low.shape[0], TOP, D))).reshape(-1, D)
    position = slot_index(route_ids, blocks)
    buffer = jnp.zeros((EXPERTS * blocks * CAP, D), jnp.float32).at[position].set(copies)
    returned = lax.map(jax.checkpoint(expert_block), (buffer.reshape(EXPERTS, blocks * CAP, D), weight_in, weight_out))
    combined = returned.reshape(-1, D)[position].reshape(-1, TOP, D)
    return residual + lax.optimization_barrier(jnp.sum(gate_values[:, :, None] * combined, axis=1))

def reference(tokens, cotangent, norm_gain, qkv_weight, proj_weight, router_weight, expert_in, expert_out, routes):

    def forward(stream, gains, qkv_all, proj_all, router_all, weights_in, weights_out):
        for layer_index in range(LAYERS):
            stream = apply_layer(stream, gains[layer_index], qkv_all[layer_index], proj_all[layer_index], router_all[layer_index], weights_in[layer_index], weights_out[layer_index], routes[layer_index])
        return stream
    primals = [operand.astype(jnp.float32) for operand in (tokens.reshape(-1, D), norm_gain, qkv_weight, proj_weight, router_weight, expert_in, expert_out)]
    result, pullback = jax.vjp(forward, *primals)
    gradients = pullback(cotangent.reshape(-1, D).astype(jnp.float32))
    token_shape = tokens.shape
    return (result.reshape(token_shape).astype(jnp.bfloat16), gradients[0].reshape(token_shape), gradients[1], gradients[2], gradients[3], gradients[4], gradients[5], gradients[6])
```

```python
import jax
import jax.numpy as jnp
from jax import lax
from jax.experimental import pallas as pl
from jax.experimental.pallas import tpu as pltpu
from jax.sharding import PartitionSpec as P

HEADS = 8
HEAD_DIM = 64
EXPERTS = 32
TOP = 2
LAYERS = 2
CAP = 12
D = 512
SEQ = 50
IMG = 3
TOK = 150
ROWS = 160
GROUPS = 16
LOCAL = 2
SLOTS = 384
HALF = 192
SHARDS = 8
FF_S = 256
WIDE = 2176
EPS = 1e-06
SCALE = HEAD_DIM ** (-0.5)
GELU_C = 0.7978845608028654
GELU_A = 0.044715

BF = jnp.bfloat16
F32 = jnp.float32


def dot(a, b):
    return jnp.dot(a, b, preferred_element_type=F32)


def dot_nt(a, b):
    return lax.dot_general(a, b, (((1,), (1,)), ((), ())), preferred_element_type=F32)


def dot_tn(a, b):
    return lax.dot_general(a, b, (((0,), (0,)), ((), ())), preferred_element_type=F32)


def iota(shape, dim):
    return lax.broadcasted_iota(jnp.int32, shape, dim)


def normalize(values):
    centered = values - jnp.mean(values, axis=-1, keepdims=True)
    inverse = lax.rsqrt(jnp.mean(centered * centered, axis=-1, keepdims=True) + EPS)
    return centered * inverse, inverse


def norm_back(upstream, normed, inverse, gain):
    scaled = upstream * gain
    mean_grad = jnp.mean(scaled, axis=-1, keepdims=True)
    mean_prod = jnp.mean(scaled * normed, axis=-1, keepdims=True)
    return inverse * (scaled - mean_grad - normed * mean_prod)


def split_low(values):
    high = values.astype(BF)
    return high, (values - high.astype(F32)).astype(BF)


def same_image():
    def image(dim):
        place = iota((ROWS, ROWS), dim)
        one = jnp.int32(1)
        zero = jnp.int32(0)
        return (
            jnp.where(place >= SEQ, one, zero)
            + jnp.where(place >= 2 * SEQ, one, zero)
            + jnp.where(place >= 3 * SEQ, one, zero)
        )

    return image(0) == image(1)


def head_probs(query, keys, half, same):
    lanes = iota(query.shape, 1)
    own = (lanes >= HEAD_DIM) if half else (lanes < HEAD_DIM)
    query = jnp.where(own, query, jnp.zeros_like(query))
    scores = jnp.where(same, dot_nt(query, keys) * SCALE, -1e30)
    weights = jnp.exp(scores - jnp.max(scores, axis=-1, keepdims=True))
    return weights / jnp.sum(weights, axis=-1, keepdims=True)


def gains_of(block):
    turned = block.astype(F32).T
    return turned[EXPERTS : EXPERTS + 1], turned[EXPERTS + 1 : EXPERTS + 2]


def routing(second, block, routes, chunk):
    logits = dot(second, block)
    lanes = iota((ROWS, 128), 1)
    logits = jnp.where(lanes < EXPERTS, logits, -1e30)
    shifted = jnp.exp(logits - jnp.max(logits, axis=-1, keepdims=True))
    prob = shifted / jnp.sum(shifted, axis=-1, keepdims=True)
    masks = [jnp.where(lanes == routes[:, k : k + 1], 1.0, 0.0) for k in range(TOP)]
    chosen = [jnp.sum(mask * prob, axis=-1, keepdims=True) for mask in masks]
    total = jnp.where(routes[:, 0:1] >= 0, chosen[0] + chosen[1], 1.0)
    gates = [value / total for value in chosen]
    earlier = jnp.where(iota((ROWS, ROWS), 1) < iota((ROWS, ROWS), 0), 1.0, 0.0).astype(BF)
    before = dot(earlier, (masks[0] + masks[1]).astype(BF))
    places = []
    for k in range(TOP):
        slot = jnp.sum(masks[k] * before, axis=-1, keepdims=True).astype(jnp.int32)
        expert = routes[:, k : k + 1]
        base = (expert >> 1) * chunk + (expert & 1) * CAP
        places.append(jnp.where(expert >= 0, base + slot, -1))
    return prob, masks, total, gates, places


def picks(place, count):
    return jnp.where(iota((ROWS, count), 1) == place, 1.0, 0.0).astype(BF)


def forward_kernel(last, *refs):
    if last:
        (w_ref, routes_ref, grad_ref, prev_ref, ret_ref, keep_in, x_ref, x1_ref, qkv_ref, mixed_ref, send_ref) = refs
        kept = keep_in[...]
        back = ret_ref[...]
        stream = prev_ref[...]
        for k in range(TOP):
            place = kept[:, 2 + k : 3 + k].astype(jnp.int32)
            stream = stream + kept[:, k : k + 1] * dot(picks(place, SLOTS), back)
        x_ref[...] = stream
    else:
        (w_ref, routes_ref, tokens_ref, x1_ref, qkv_ref, mixed_ref, send_ref, keep_ref) = refs
        stream = tokens_ref[...].astype(F32)
    chunk = 48 if last else 24
    block = w_ref[:, 2048:WIDE]
    gain_one, gain_two = gains_of(block)
    normed, _ = normalize(stream)
    first = (normed * gain_one).astype(BF)
    qkv_ref[...] = dot(first, w_ref[:, :1536]).astype(BF)
    same = same_image()
    low_half = iota((ROWS, 128), 1) < HEAD_DIM
    for pair in range(HEADS // 2):
        left = pair * 128
        query = qkv_ref[:, left : left + 128]
        keys = qkv_ref[:, 512 + left : 640 + left]
        values = qkv_ref[:, 1024 + left : 1152 + left]
        parts = [dot(head_probs(query, keys, half, same).astype(BF), values) for half in range(2)]
        mixed_ref[:, left : left + 128] = jnp.where(low_half, parts[0], parts[1]).astype(BF)
    residual = stream + dot(mixed_ref[...], w_ref[:, 1536:2048])
    x1_ref[...] = residual
    normed_two, _ = normalize(residual)
    second = (normed_two * gain_two).astype(BF)
    _, _, _, gates, places = routing(second, block, routes_ref[...], chunk)
    count = GROUPS * chunk
    outgoing = dot_tn(picks(places[0], count) + picks(places[1], count), second)
    if last:
        grad = grad_ref[...].astype(F32)
        for k in range(TOP):
            outgoing = outgoing + dot_tn(
                picks(jnp.where(places[k] >= 0, places[k] + 24, -1), count), (gates[k] * grad).astype(BF)
            )
    else:
        lanes = iota((ROWS, 128), 1)
        kept = jnp.where(lanes == 0, gates[0], jnp.where(lanes == 1, gates[1], 0.0))
        kept = jnp.where(lanes == 2, places[0].astype(F32), kept)
        keep_ref[...] = jnp.where(lanes == 3, places[1].astype(F32), kept)
    send_ref[...] = outgoing.astype(BF)


def backward_kernel(last, *refs):
    if last:
        (w_ref, routes_ref, grad_ref, back_ref, x1_ref, x_ref, qkv_ref, mixed_ref, keep_in,
         g_ref, prev_ref, out_ref, send_ref, dqkv_ref) = refs
        chunk = 48
    else:
        (w_ref, routes_ref, grad_ref, ret_ref, back_ref, x1_ref, x_ref, qkv_ref, mixed_ref,
         g_ref, prev_ref, dqkv_ref) = refs
        chunk = 24
    count = GROUPS * chunk
    block = w_ref[:, 2048:WIDE]
    gain_one, gain_two = gains_of(block)
    grad = grad_ref[...].astype(F32)
    residual = x1_ref[...]
    normed_two, inverse_two = normalize(residual)
    second = (normed_two * gain_two).astype(BF)
    prob, masks, total, gates, places = routing(second, block, routes_ref[...], chunk)
    chooser = [picks(place, count) for place in places]
    back = back_ref[...]
    if last:
        returned = back
        shift = [picks(jnp.where(place >= 0, place + 24, -1), count) for place in places]
        drow = dot(shift[0] + shift[1], back)
    else:
        returned = ret_ref[...]
        drow = dot(chooser[0] + chooser[1], back)
    combined = [dot(choice, returned) for choice in chooser]
    if last:
        output = residual + (gates[0] * combined[0] + gates[1] * combined[1])
        for image in range(IMG):
            out_ref[image] = output[image * SEQ : (image + 1) * SEQ].astype(BF)
    dgate = [jnp.sum(grad * value, axis=-1, keepdims=True) for value in combined]
    inner = dgate[0] * gates[0] + dgate[1] * gates[1]
    dprob = sum((dgate[k] - inner) / total * masks[k] for k in range(TOP))
    dlogit = prob * (dprob - jnp.sum(dprob * prob, axis=-1, keepdims=True))
    logit_high, logit_low = split_low(dlogit)
    dsecond = dot_nt(logit_high, block) + dot_nt(logit_low, block) + drow
    small = dot_tn(second, logit_high) + dot_tn(second, logit_low)
    lanes = iota((ROWS, 128), 1)
    mark_two = jnp.where(lanes == EXPERTS + 1, 1.0, 0.0).astype(BF)
    high, low = split_low(dsecond * normed_two)
    small = small + dot_tn(high, mark_two) + dot_tn(low, mark_two)
    grad = grad + norm_back(dsecond, normed_two, inverse_two, gain_two)
    branch = grad.astype(BF)
    g_ref[:, 1536:2048] = dot_tn(mixed_ref[...], branch).astype(BF)
    dmixed = dot_nt(branch, w_ref[:, 1536:2048]).astype(BF)
    same = same_image()
    low_half = lanes < HEAD_DIM
    for pair in range(HEADS // 2):
        left = pair * 128
        query = qkv_ref[:, left : left + 128]
        keys = qkv_ref[:, 512 + left : 640 + left]
        values = qkv_ref[:, 1024 + left : 1152 + left]
        upstream = dmixed[:, left : left + 128]
        dq, dk, dv = [], [], []
        for half in range(2):
            own = jnp.logical_not(low_half) if half else low_half
            probs = head_probs(query, keys, half, same)
            dv.append(dot_tn(probs.astype(BF), upstream))
            dprobs = dot_nt(jnp.where(own, upstream, jnp.zeros_like(upstream)), values)
            dscores = probs * (dprobs - jnp.sum(dprobs * probs, axis=-1, keepdims=True))
            dscores = dscores.astype(BF)
            dq.append(dot(dscores, keys) * SCALE)
            dk.append(dot_tn(dscores, query) * SCALE)
        dqkv_ref[:, left : left + 128] = jnp.where(low_half, dq[0], dq[1]).astype(BF)
        dqkv_ref[:, 512 + left : 640 + left] = jnp.where(low_half, dk[0], dk[1]).astype(BF)
        dqkv_ref[:, 1024 + left : 1152 + left] = jnp.where(low_half, dv[0], dv[1]).astype(BF)
    normed, inverse = normalize(x_ref[...].astype(F32))
    first = (normed * gain_one).astype(BF)
    dqkv = dqkv_ref[...]
    g_ref[:, :1536] = dot_tn(first, dqkv).astype(BF)
    dfirst = dot_nt(dqkv, w_ref[:, :1536])
    mark_one = jnp.where(lanes == EXPERTS, 1.0, 0.0).astype(BF)
    high, low = split_low(dfirst * normed)
    small = small + dot_tn(high, mark_one) + dot_tn(low, mark_one)
    g_ref[:, 2048:WIDE] = small.astype(BF)
    grad = grad + norm_back(dfirst, normed, inverse, gain_one)
    if last:
        prev_ref[...] = grad
        kept = keep_in[...]
        outgoing = jnp.zeros((SLOTS, D), F32)
        for k in range(TOP):
            place = kept[:, 2 + k : 3 + k].astype(jnp.int32)
            outgoing = outgoing + dot_tn(picks(place, SLOTS), (kept[:, k : k + 1] * grad).astype(BF))
        send_ref[...] = outgoing.astype(BF)
    else:
        for image in range(IMG):
            prev_ref[image] = grad[image * SEQ : (image + 1) * SEQ]


def arrange(chunk, shift):
    place = iota((SLOTS, GROUPS * chunk), 0)
    local = jnp.where(place >= HALF, jnp.int32(1), jnp.int32(0))
    rest = place - local * HALF
    source = (rest * 171) >> 11
    target = source * chunk + local * CAP + (rest - source * CAP) + shift
    return jnp.where(iota((SLOTS, GROUPS * chunk), 1) == target, 1.0, 0.0).astype(BF)


def load_weights(at_ref, in_hbm, out_hbm, in_buf, out_buf, sems):
    me = at_ref[0]
    copies = []
    for local in range(LOCAL):
        for step in range(SHARDS):
            ahead, other = step // 2, step % 2
            shard = ((me // 2 + ahead) % 4) * 2 + (me % 2 + other) % 2
            pair = (
                pltpu.make_async_copy(in_hbm.at[shard, local], in_buf.at[local, step], sems.at[0, local, step]),
                pltpu.make_async_copy(out_hbm.at[shard, local], out_buf.at[local, step], sems.at[1, local, step]),
            )
            for copy in pair:
                copy.start()
            copies.append(pair)
    return copies


def expert_forward(at_ref, recv_ref, in_hbm, out_hbm, ret_ref, rows_ref, in_buf, out_buf, sems):
    copies = load_weights(at_ref, in_hbm, out_hbm, in_buf, out_buf, sems)
    order = arrange(24, 0)
    rows_ref[...] = dot(order, recv_ref[...]).astype(BF)
    totals = []
    for local in range(LOCAL):
        rows = rows_ref[local * HALF : (local + 1) * HALF]
        total = jnp.zeros((HALF, D), F32)
        for step in range(SHARDS):
            for copy in copies[local * SHARDS + step]:
                copy.wait()
            pre = dot(rows, in_buf[local, step])
            bend = jnp.tanh(GELU_C * (pre + GELU_A * pre * pre * pre))
            hidden = (0.5 * pre * (1.0 + bend)).astype(BF)
            total = total + dot(hidden, out_buf[local, step])
        totals.append(total.astype(BF))
    ret_ref[...] = dot_tn(order, jnp.concatenate(totals, axis=0)).astype(BF)


def expert_backward(last, at_ref, *refs):
    if last:
        recv_ref, in_hbm, out_hbm, back_ref = refs[:4]
        refs = refs[4:]
    else:
        rows_ref, recv_ref, in_hbm, out_hbm, back_ref = refs[:5]
        refs = refs[5:]
    own_in, own_out = refs[0:4], refs[4:8]
    far_in, far_out, rest_in, rest_out, in_buf, out_buf, sems = refs[8:15]
    copies = load_weights(at_ref, in_hbm, out_hbm, in_buf, out_buf, sems)
    recv = recv_ref[...]
    if last:
        order = arrange(48, 0)
        order_back = arrange(48, 24)
        rows_all = dot(order, recv).astype(BF)
        grads_all = dot(order_back, recv).astype(BF)
    else:
        order_back = arrange(24, 0)
        rows_all = rows_ref[...]
        grads_all = dot(order_back, recv).astype(BF)
    totals, back_totals = [], []
    for local in range(LOCAL):
        rows = rows_all[local * HALF : (local + 1) * HALF]
        grads = grads_all[local * HALF : (local + 1) * HALF]
        rows_turned = rows.T
        total = jnp.zeros((HALF, D), F32)
        back_total = jnp.zeros((HALF, D), F32)
        for step in range(SHARDS):
            for copy in copies[local * SHARDS + step]:
                copy.wait()
            first_use = in_buf[local, step]
            second_use = out_buf[local, step]
            pre = dot(rows, first_use)
            square = pre * pre
            bend = jnp.tanh(GELU_C * (pre + GELU_A * pre * square))
            hidden = (0.5 * pre * (1.0 + bend)).astype(BF)
            if last:
                total = total + dot(hidden, second_use)
            slope = 0.5 * (1.0 + bend) + (0.5 * GELU_C) * pre * (1.0 - bend * bend) * (
                1.0 + (3.0 * GELU_A) * square
            )
            dpre = (dot_nt(grads, second_use) * slope).astype(BF)
            back_total = back_total + dot_nt(dpre, first_use)
            grad_in = dot(rows_turned, dpre).astype(BF)
            grad_out = dot_tn(hidden, grads).astype(BF)
            ahead, other = step // 2, step % 2
            if other == 0:
                own_in[ahead][local] = grad_in
                own_out[ahead][local] = grad_out
            elif ahead == 2:
                far_in[local] = grad_in
                far_out[local] = grad_out
            else:
                place = {0: 0, 1: 1, 3: 2}[ahead]
                rest_in[place, local] = grad_in
                rest_out[place, local] = grad_out
        totals.append(total.astype(BF))
        back_totals.append(back_total.astype(BF))
    result = dot_tn(order_back, jnp.concatenate(back_totals, axis=0))
    if last:
        result = result + dot_tn(order, jnp.concatenate(totals, axis=0))
    back_ref[...] = result.astype(BF)


VM = pl.BlockSpec(memory_space=pltpu.VMEM)
SM = pl.BlockSpec(memory_space=pltpu.SMEM)
HB = pl.BlockSpec(memory_space=pl.ANY)


def shape(*dims, dtype=BF):
    return jax.ShapeDtypeStruct(dims, dtype)


def call(body, outs, in_specs, args, scratch=(), flops=1e9, moved=4e6, name=None, limit=48):
    return pl.pallas_call(
        body,
        out_shape=outs,
        in_specs=in_specs,
        out_specs=[VM] * len(outs),
        scratch_shapes=list(scratch),
        compiler_params=pltpu.CompilerParams(vmem_limit_bytes=limit * 1024 * 1024),
        cost_estimate=pl.CostEstimate(flops=int(flops), bytes_accessed=int(moved), transcendentals=0),
        name=name,
    )(*args)


WEIGHT_SCRATCH = (
    pltpu.VMEM((LOCAL, SHARDS, D, FF_S), BF),
    pltpu.VMEM((LOCAL, SHARDS, FF_S, D), BF),
    pltpu.SemaphoreType.DMA((2, LOCAL, SHARDS)),
)


def forward_first(weights, routes, tokens):
    def body(*refs):
        forward_kernel(False, *refs)

    outs = [shape(ROWS, D, dtype=F32), shape(ROWS, 1536), shape(ROWS, D), shape(SLOTS, D), shape(ROWS, 128, dtype=F32)]
    return call(body, outs, [VM] * 3, (weights, routes, tokens), name="dense_forward_first", flops=4e9)


def forward_last(weights, routes, grad, prev, ret, keep):
    def body(*refs):
        forward_kernel(True, *refs)

    outs = [shape(ROWS, D, dtype=F32), shape(ROWS, D, dtype=F32), shape(ROWS, 1536), shape(ROWS, D), shape(2 * SLOTS, D)]
    return call(body, outs, [VM] * 6, (weights, routes, grad, prev, ret, keep), name="dense_forward_last", flops=4e9)


def backward_last(*args):
    def body(*refs):
        backward_kernel(True, *refs)

    outs = [shape(D, WIDE), shape(ROWS, D, dtype=F32), shape(IMG, SEQ, D), shape(SLOTS, D)]
    return call(
        body, outs, [VM] * len(args), args, [pltpu.VMEM((ROWS, 1536), BF)], name="dense_backward_last", flops=1e10
    )


def backward_first(*args):
    def body(*refs):
        backward_kernel(False, *refs)

    outs = [shape(D, WIDE), shape(IMG, SEQ, D, dtype=F32)]
    return call(
        body, outs, [VM] * len(args), args, [pltpu.VMEM((ROWS, 1536), BF)], name="dense_backward_first", flops=1e10
    )


def experts_forward(at, recv, w_in, w_out):
    outs = [shape(SLOTS, D), shape(SLOTS, D)]
    return call(
        expert_forward, outs, [SM, VM, HB, HB], (at, recv, w_in, w_out), WEIGHT_SCRATCH, name="expert_forward",
        flops=4e9, moved=9e6,
    )


def experts_backward(last, args):
    def body(*refs):
        expert_backward(last, *refs)

    in_shape, out_shape = (LOCAL, D, FF_S), (LOCAL, FF_S, D)
    outs = [shape((2 if last else 1) * SLOTS, D)]
    outs += [shape(*in_shape)] * 4 + [shape(*out_shape)] * 4
    outs += [shape(*in_shape), shape(*out_shape), shape(3, *in_shape), shape(3, *out_shape)]
    specs = [SM] + [VM] * (len(args) - 3) + [HB, HB]
    return call(body, outs, specs, args, WEIGHT_SCRATCH, name="expert_backward", flops=1e10, moved=2e7)


def across(value, dx, dc):
    moves = [(x * 2 + c, ((x + dx) % 4) * 2 + (c + dc) % 2) for x in range(4) for c in range(2)]
    return lax.ppermute(value, "dp", moves)


def swap_experts(value, chunk):
    arrived = lax.all_to_all(value.reshape(GROUPS, chunk, D), "experts", split_axis=0, concat_axis=0, tiled=True)
    return arrived.reshape(GROUPS * chunk, D)


def add(*values):
    total = values[0].astype(F32)
    for value in values[1:]:
        total = total + value.astype(F32)
    return total


def reduce_experts(parts):
    own_in, own_out = parts[0:4], parts[4:8]
    far_in, far_out, rest_in, rest_out = parts[8:12]
    got_far_in, got_far_out = across(far_in, 0, 1), across(far_out, 0, 1)
    got_in, got_out = across(rest_in, 0, 1), across(rest_out, 0, 1)
    move_in = across(add(own_in[2], got_far_in).astype(BF), 1, 0)
    move_out = across(add(own_out[2], got_far_out).astype(BF), -1, 0)
    right_out = across(add(own_out[1], got_out[1]).astype(BF), 1, 0)
    left_in = across(add(own_in[3], got_in[2]).astype(BF), -1, 0)
    right_in = across(add(own_in[1], got_in[1], move_in).astype(BF), 1, 0)
    left_out = across(add(own_out[3], got_out[2], move_out).astype(BF), -1, 0)
    return add(own_in[0], got_in[0], left_in, right_in), add(own_out[0], got_out[0], left_out, right_out)


def reduce_dense(grads):
    arrived = lax.all_to_all(grads.reshape(GROUPS, 32, WIDE), "experts", split_axis=0, concat_axis=0, tiled=True)
    part = jnp.sum(arrived.astype(F32), axis=0).astype(BF)
    arrived = lax.all_to_all(part.reshape(SHARDS, 4, WIDE), "dp", split_axis=0, concat_axis=0, tiled=True)
    return jnp.sum(arrived.astype(F32), axis=0)


def local(
    tokens,
    cotangent,
    norm_gain,
    qkv_weight,
    proj_weight,
    router_weight,
    expert_in,
    expert_out,
    routes,
):
    pad = ((0, ROWS - TOK), (0, 0))
    tokens_pad = jnp.pad(tokens.reshape(TOK, D), pad)
    grad_pad = jnp.pad(cotangent.reshape(TOK, D), pad)
    routes_pad = [jnp.pad(routes[layer].reshape(TOK, TOP), pad, constant_values=-1) for layer in range(LAYERS)]
    at = lax.axis_index("dp").astype(jnp.int32).reshape(1)
    packed = jnp.concatenate(
        [
            qkv_weight,
            proj_weight,
            router_weight,
            norm_gain.transpose(0, 2, 1),
            jnp.zeros((LAYERS, 4, WIDE - 2048 - EXPERTS - 2), BF),
        ],
        axis=2,
    )
    weights = []
    for layer in range(LAYERS):
        near = lax.all_gather(packed[layer], "dp", axis=0, tiled=True)
        weights.append(lax.all_gather(near, "experts", axis=0, tiled=True))
    w_in = [lax.all_gather(expert_in[layer], "dp", axis=0, tiled=False) for layer in range(LAYERS)]
    w_out = [lax.all_gather(expert_out[layer], "dp", axis=0, tiled=False) for layer in range(LAYERS)]

    x1_a, qkv_a, mixed_a, send, keep = forward_first(weights[0], routes_pad[0], tokens_pad)
    recv = swap_experts(send, 24)
    ret, rows_a = experts_forward(at, recv, w_in[0], w_out[0])
    ret_a = swap_experts(ret, 24)
    x_b, x1_b, qkv_b, mixed_b, send = forward_last(weights[1], routes_pad[1], grad_pad, x1_a, ret_a, keep)
    recv = swap_experts(send, 48)
    parts_b = experts_backward(True, (at, recv, w_in[1], w_out[1]))
    back_b = swap_experts(parts_b[0], 48)
    sums_b = reduce_experts(parts_b[1:])
    dense_b, grad, output, send = backward_last(
        weights[1], routes_pad[1], grad_pad, back_b, x1_b, x_b, qkv_b, mixed_b, keep
    )
    recv = swap_experts(send, 24)
    parts_a = experts_backward(False, (at, rows_a, recv, w_in[0], w_out[0]))
    back_a = swap_experts(parts_a[0], 24)
    sums_a = reduce_experts(parts_a[1:])
    dense_a, grad_tokens = backward_first(
        weights[0], routes_pad[0], grad, ret_a, back_a, x1_a, tokens_pad, qkv_a, mixed_a
    )
    dense = jnp.stack([reduce_dense(dense_a), reduce_dense(dense_b)])
    grad_gain = dense[:, :, 2048 + EXPERTS : 2048 + EXPERTS + 2].transpose(0, 2, 1)
    return (
        output,
        grad_tokens,
        grad_gain,
        dense[:, :, :1536],
        dense[:, :, 1536:2048],
        dense[:, :, 2048 : 2048 + EXPERTS],
        jnp.stack([sums_a[0], sums_b[0]]),
        jnp.stack([sums_a[1], sums_b[1]]),
    )


def solution(mesh):
    placed = (
        P(("experts", "dp"), None, None),
        P(("experts", "dp"), None, None),
        P(None, None, ("experts", "dp")),
        P(None, ("experts", "dp"), None),
        P(None, ("experts", "dp"), None),
        P(None, ("experts", "dp"), None),
        P(None, "experts", None, "dp"),
        P(None, "experts", "dp", None),
        P(None, ("experts", "dp"), None, None),
    )
    return jax.shard_map(
        local,
        mesh=mesh,
        in_specs=placed,
        out_specs=(
            P(("experts", "dp"), None, None),
            P(("experts", "dp"), None, None),
            P(None, None, ("experts", "dp")),
            P(None, ("experts", "dp"), None),
            P(None, ("experts", "dp"), None),
            P(None, ("experts", "dp"), None),
            P(None, "experts", None, "dp"),
            P(None, "experts", "dp", None),
        ),
        check_vma=False,
    )
```

```python
import jax
import jax.numpy as jnp
from jax import lax
from jax.experimental import pallas as pl
from jax.experimental.pallas import tpu as pltpu
from jax.sharding import PartitionSpec as P

HEADS = 8
HEAD_DIM = 64
EXPERTS = 32
TOP = 2
LAYERS = 2
CAP = 12
D = 512
SEQ = 50
IMG = 3
TOK = 150
ROWS = 160
GROUPS = 16
LOCAL = 2
SLOTS = 384
HALF = 192
SHARDS = 8
FF_S = 256
WIDE = 2176
PACK = 2304
EPS = 1e-06
SCALE = HEAD_DIM ** (-0.5)
GELU_C = 0.7978845608028654
GELU_A = 0.044715

BF = jnp.bfloat16
F32 = jnp.float32


def dot(a, b):
    return jnp.dot(a, b, preferred_element_type=F32)


def dot_nt(a, b):
    return lax.dot_general(a, b, (((1,), (1,)), ((), ())), preferred_element_type=F32)


def dot_tn(a, b):
    return lax.dot_general(a, b, (((0,), (0,)), ((), ())), preferred_element_type=F32)


def iota(shape, dim):
    return lax.broadcasted_iota(jnp.int32, shape, dim)


def normalize(values):
    centered = values - jnp.mean(values, axis=-1, keepdims=True)
    inverse = lax.rsqrt(jnp.mean(centered * centered, axis=-1, keepdims=True) + EPS)
    return centered * inverse, inverse


def norm_back(upstream, normed, inverse, gain):
    scaled = upstream * gain
    mean_grad = jnp.mean(scaled, axis=-1, keepdims=True)
    mean_prod = jnp.mean(scaled * normed, axis=-1, keepdims=True)
    return inverse * (scaled - mean_grad - normed * mean_prod)


def split_low(values):
    high = values.astype(BF)
    return high, (values - high.astype(F32)).astype(BF)


def same_image():
    def image(dim):
        place = iota((ROWS, ROWS), dim)
        one = jnp.int32(1)
        zero = jnp.int32(0)
        return (
            jnp.where(place >= SEQ, one, zero)
            + jnp.where(place >= 2 * SEQ, one, zero)
            + jnp.where(place >= 3 * SEQ, one, zero)
        )

    return image(0) == image(1)


def head_probs(query, keys, half, same):
    lanes = iota(query.shape, 1)
    own = (lanes >= HEAD_DIM) if half else (lanes < HEAD_DIM)
    query = jnp.where(own, query, jnp.zeros_like(query))
    scores = jnp.where(same, dot_nt(query, keys) * SCALE, -1e30)
    weights = jnp.exp(scores - jnp.max(scores, axis=-1, keepdims=True))
    return weights / jnp.sum(weights, axis=-1, keepdims=True)


def gains_of(block):
    turned = block.astype(F32).T
    return turned[EXPERTS : EXPERTS + 1], turned[EXPERTS + 1 : EXPERTS + 2]


def routing(second, block, routes, chunk):
    logits = dot(second, block)
    lanes = iota((ROWS, 128), 1)
    logits = jnp.where(lanes < EXPERTS, logits, -1e30)
    shifted = jnp.exp(logits - jnp.max(logits, axis=-1, keepdims=True))
    prob = shifted / jnp.sum(shifted, axis=-1, keepdims=True)
    masks = [jnp.where(lanes == routes[:, k : k + 1], 1.0, 0.0) for k in range(TOP)]
    chosen = [jnp.sum(mask * prob, axis=-1, keepdims=True) for mask in masks]
    total = jnp.where(routes[:, 0:1] >= 0, chosen[0] + chosen[1], 1.0)
    gates = [value / total for value in chosen]
    earlier = jnp.where(iota((ROWS, ROWS), 1) < iota((ROWS, ROWS), 0), 1.0, 0.0).astype(BF)
    before = dot(earlier, (masks[0] + masks[1]).astype(BF))
    places = []
    for k in range(TOP):
        slot = jnp.sum(masks[k] * before, axis=-1, keepdims=True).astype(jnp.int32)
        expert = routes[:, k : k + 1]
        base = (expert >> 1) * chunk + (expert & 1) * CAP
        places.append(jnp.where(expert >= 0, base + slot, -1))
    return prob, masks, total, gates, places


def picks(place, count):
    return jnp.where(iota((ROWS, count), 1) == place, 1.0, 0.0).astype(BF)


def forward_kernel(last, *refs):
    if last:
        (w_ref, routes_ref, grad_ref, prev_ref, ret_ref, keep_in, x_ref, x1_ref, qkv_ref, mixed_ref, send_ref) = refs
        kept = keep_in[...]
        back = ret_ref[...]
        stream = prev_ref[...]
        for k in range(TOP):
            place = kept[:, 2 + k : 3 + k].astype(jnp.int32)
            stream = stream + kept[:, k : k + 1] * dot(picks(place, SLOTS), back)
        x_ref[...] = stream
    else:
        (w_ref, routes_ref, tokens_ref, x1_ref, qkv_ref, mixed_ref, send_ref, keep_ref) = refs
        stream = tokens_ref[...].astype(F32)
    chunk = 48 if last else 24
    block = w_ref[:, 2048:WIDE]
    gain_one, gain_two = gains_of(block)
    normed, _ = normalize(stream)
    first = (normed * gain_one).astype(BF)
    qkv_ref[...] = dot(first, w_ref[:, :1536]).astype(BF)
    same = same_image()
    low_half = iota((ROWS, 128), 1) < HEAD_DIM
    for pair in range(HEADS // 2):
        left = pair * 128
        query = qkv_ref[:, left : left + 128]
        keys = qkv_ref[:, 512 + left : 640 + left]
        values = qkv_ref[:, 1024 + left : 1152 + left]
        parts = [dot(head_probs(query, keys, half, same).astype(BF), values) for half in range(2)]
        mixed_ref[:, left : left + 128] = jnp.where(low_half, parts[0], parts[1]).astype(BF)
    residual = stream + dot(mixed_ref[...], w_ref[:, 1536:2048])
    x1_ref[...] = residual
    normed_two, _ = normalize(residual)
    second = (normed_two * gain_two).astype(BF)
    _, _, _, gates, places = routing(second, block, routes_ref[...], chunk)
    count = GROUPS * chunk
    outgoing = dot_tn(picks(places[0], count) + picks(places[1], count), second)
    if last:
        grad = grad_ref[...].astype(F32)
        for k in range(TOP):
            outgoing = outgoing + dot_tn(
                picks(jnp.where(places[k] >= 0, places[k] + 24, -1), count), (gates[k] * grad).astype(BF)
            )
    else:
        lanes = iota((ROWS, 128), 1)
        kept = jnp.where(lanes == 0, gates[0], jnp.where(lanes == 1, gates[1], 0.0))
        kept = jnp.where(lanes == 2, places[0].astype(F32), kept)
        keep_ref[...] = jnp.where(lanes == 3, places[1].astype(F32), kept)
    send_ref[...] = outgoing.astype(BF)


def backward_kernel(last, *refs):
    if last:
        (at_ref, w_ref, routes_ref, grad_ref, back_ref, x1_ref, x_ref, qkv_ref, mixed_ref, keep_in,
         stay_ref, give_ref, prev_ref, out_ref, send_ref, dqkv_ref, g_ref) = refs
        chunk = 48
    else:
        (at_ref, w_ref, routes_ref, grad_ref, ret_ref, back_ref, x1_ref, x_ref, qkv_ref, mixed_ref,
         stay_ref, give_ref, prev_ref, dqkv_ref, g_ref) = refs
        chunk = 24
    count = GROUPS * chunk
    block = w_ref[:, 2048:WIDE]
    gain_one, gain_two = gains_of(block)
    grad = grad_ref[...].astype(F32)
    residual = x1_ref[...]
    normed_two, inverse_two = normalize(residual)
    second = (normed_two * gain_two).astype(BF)
    prob, masks, total, gates, places = routing(second, block, routes_ref[...], chunk)
    chooser = [picks(place, count) for place in places]
    back = back_ref[...]
    if last:
        returned = back
        shift = [picks(jnp.where(place >= 0, place + 24, -1), count) for place in places]
        drow = dot(shift[0] + shift[1], back)
    else:
        returned = ret_ref[...]
        drow = dot(chooser[0] + chooser[1], back)
    combined = [dot(choice, returned) for choice in chooser]
    if last:
        output = residual + (gates[0] * combined[0] + gates[1] * combined[1])
        for image in range(IMG):
            out_ref[image] = output[image * SEQ : (image + 1) * SEQ].astype(BF)
    dgate = [jnp.sum(grad * value, axis=-1, keepdims=True) for value in combined]
    inner = dgate[0] * gates[0] + dgate[1] * gates[1]
    dprob = sum((dgate[k] - inner) / total * masks[k] for k in range(TOP))
    dlogit = prob * (dprob - jnp.sum(dprob * prob, axis=-1, keepdims=True))
    logit_high, logit_low = split_low(dlogit)
    dsecond = dot_nt(logit_high, block) + dot_nt(logit_low, block) + drow
    small = dot_tn(second, logit_high) + dot_tn(second, logit_low)
    lanes = iota((ROWS, 128), 1)
    mark_two = jnp.where(lanes == EXPERTS + 1, 1.0, 0.0).astype(BF)
    high, low = split_low(dsecond * normed_two)
    small = small + dot_tn(high, mark_two) + dot_tn(low, mark_two)
    grad = grad + norm_back(dsecond, normed_two, inverse_two, gain_two)
    branch = grad.astype(BF)
    g_ref[1, :, 384:896] = dot_tn(mixed_ref[...], branch).astype(BF)
    dmixed = dot_nt(branch, w_ref[:, 1536:2048]).astype(BF)
    same = same_image()
    low_half = lanes < HEAD_DIM
    for pair in range(HEADS // 2):
        left = pair * 128
        query = qkv_ref[:, left : left + 128]
        keys = qkv_ref[:, 512 + left : 640 + left]
        values = qkv_ref[:, 1024 + left : 1152 + left]
        upstream = dmixed[:, left : left + 128]
        dq, dk, dv = [], [], []
        for half in range(2):
            own = jnp.logical_not(low_half) if half else low_half
            probs = head_probs(query, keys, half, same)
            dv.append(dot_tn(probs.astype(BF), upstream))
            dprobs = dot_nt(jnp.where(own, upstream, jnp.zeros_like(upstream)), values)
            dscores = probs * (dprobs - jnp.sum(dprobs * probs, axis=-1, keepdims=True))
            dscores = dscores.astype(BF)
            dq.append(dot(dscores, keys) * SCALE)
            dk.append(dot_tn(dscores, query) * SCALE)
        dqkv_ref[:, left : left + 128] = jnp.where(low_half, dq[0], dq[1]).astype(BF)
        dqkv_ref[:, 512 + left : 640 + left] = jnp.where(low_half, dk[0], dk[1]).astype(BF)
        dqkv_ref[:, 1024 + left : 1152 + left] = jnp.where(low_half, dv[0], dv[1]).astype(BF)
    normed, inverse = normalize(x_ref[...].astype(F32))
    first = (normed * gain_one).astype(BF)
    dqkv = dqkv_ref[...]
    g_ref[0] = dot_tn(first, dqkv[:, :1152]).astype(BF)
    g_ref[1, :, :384] = dot_tn(first, dqkv[:, 1152:]).astype(BF)
    dfirst = dot_nt(dqkv, w_ref[:, :1536])
    mark_one = jnp.where(lanes == EXPERTS, 1.0, 0.0).astype(BF)
    high, low = split_low(dfirst * normed)
    small = small + dot_tn(high, mark_one) + dot_tn(low, mark_one)
    g_ref[1, :, 896:1024] = small.astype(BF)
    g_ref[1, :, 1024:] = jnp.zeros((D, 128), BF)
    core = at_ref[0] % 2
    stay_ref[...] = g_ref[core]
    give_ref[...] = g_ref[1 - core]
    grad = grad + norm_back(dfirst, normed, inverse, gain_one)
    if last:
        prev_ref[...] = grad
        kept = keep_in[...]
        outgoing = jnp.zeros((SLOTS, D), F32)
        for k in range(TOP):
            place = kept[:, 2 + k : 3 + k].astype(jnp.int32)
            outgoing = outgoing + dot_tn(picks(place, SLOTS), (kept[:, k : k + 1] * grad).astype(BF))
        send_ref[...] = outgoing.astype(BF)
    else:
        for image in range(IMG):
            prev_ref[image] = grad[image * SEQ : (image + 1) * SEQ]


def arrange(chunk, shift):
    place = iota((SLOTS, GROUPS * chunk), 0)
    local = jnp.where(place >= HALF, jnp.int32(1), jnp.int32(0))
    rest = place - local * HALF
    source = (rest * 171) >> 11
    target = source * chunk + local * CAP + (rest - source * CAP) + shift
    return jnp.where(iota((SLOTS, GROUPS * chunk), 1) == target, 1.0, 0.0).astype(BF)


def load_weights(source, buffer, sems):
    copies = []
    for local in range(LOCAL):
        for step in range(SHARDS):
            copy = pltpu.make_async_copy(source.at[step, local], buffer.at[local, step], sems.at[local, step])
            copy.start()
            copies.append(copy)
    return copies


def unpack_out(tile):
    return jnp.concatenate([tile[D : D + FF_S], tile[D + FF_S :]], axis=1)


def expert_forward(recv_ref, source, ret_ref, rows_ref, buffer, sems):
    copies = load_weights(source, buffer, sems)
    order = arrange(24, 0)
    rows_ref[...] = dot(order, recv_ref[...]).astype(BF)
    totals = []
    for local in range(LOCAL):
        rows = rows_ref[local * HALF : (local + 1) * HALF]
        total = jnp.zeros((HALF, D), F32)
        for step in range(SHARDS):
            copies[local * SHARDS + step].wait()
            tile = buffer[local, step]
            pre = dot(rows, tile[:D])
            bend = jnp.tanh(GELU_C * (pre + GELU_A * pre * pre * pre))
            hidden = (0.5 * pre * (1.0 + bend)).astype(BF)
            total = total + dot(hidden, unpack_out(tile))
        totals.append(total.astype(BF))
    ret_ref[...] = dot_tn(order, jnp.concatenate(totals, axis=0)).astype(BF)


def expert_backward(last, *refs):
    if last:
        recv_ref, source, back_ref, grads_to, buffer, staged, sems, out_sems = refs
    else:
        rows_ref, recv_ref, source, back_ref, grads_to, buffer, staged, sems, out_sems = refs
    copies = load_weights(source, buffer, sems)
    recv = recv_ref[...]
    if last:
        order = arrange(48, 0)
        order_back = arrange(48, 24)
        rows_all = dot(order, recv).astype(BF)
        grads_all = dot(order_back, recv).astype(BF)
    else:
        order_back = arrange(24, 0)
        rows_all = rows_ref[...]
        grads_all = dot(order_back, recv).astype(BF)
    totals, back_totals, sent = [], [], []
    for local in range(LOCAL):
        rows = rows_all[local * HALF : (local + 1) * HALF]
        grads = grads_all[local * HALF : (local + 1) * HALF]
        rows_turned = rows.T
        total = jnp.zeros((HALF, D), F32)
        back_total = jnp.zeros((HALF, D), F32)
        for step in range(SHARDS):
            copies[local * SHARDS + step].wait()
            tile = buffer[local, step]
            first_use = tile[:D]
            second_use = unpack_out(tile)
            pre = dot(rows, first_use)
            square = pre * pre
            bend = jnp.tanh(GELU_C * (pre + GELU_A * pre * square))
            hidden = (0.5 * pre * (1.0 + bend)).astype(BF)
            if last:
                total = total + dot(hidden, second_use)
            slope = 0.5 * (1.0 + bend) + (0.5 * GELU_C) * pre * (1.0 - bend * bend) * (
                1.0 + (3.0 * GELU_A) * square
            )
            dpre = (dot_nt(grads, second_use) * slope).astype(BF)
            back_total = back_total + dot_nt(dpre, first_use)
            grad_out = dot_tn(hidden, grads).astype(BF)
            staged[local, step, :D] = dot(rows_turned, dpre).astype(BF)
            staged[local, step, D : D + FF_S] = grad_out[:, :FF_S]
            staged[local, step, D + FF_S :] = grad_out[:, FF_S:]
            copy = pltpu.make_async_copy(staged.at[local, step], grads_to.at[step, local], out_sems.at[local, step])
            copy.start()
            sent.append(copy)
        totals.append(total.astype(BF))
        back_totals.append(back_total.astype(BF))
    result = dot_tn(order_back, jnp.concatenate(back_totals, axis=0))
    if last:
        result = result + dot_tn(order, jnp.concatenate(totals, axis=0))
    back_ref[...] = result.astype(BF)
    for copy in sent:
        copy.wait()


VM = pl.BlockSpec(memory_space=pltpu.VMEM)
HM = pl.BlockSpec(memory_space=pltpu.HBM)
SM = pl.BlockSpec(memory_space=pltpu.SMEM)


def shape(*dims, dtype=BF):
    return jax.ShapeDtypeStruct(dims, dtype)


def call(body, outs, in_specs, args, scratch=(), flops=1e9, moved=4e6, name=None, limit=24, out_specs=None):
    return pl.pallas_call(
        body,
        out_shape=outs,
        in_specs=in_specs,
        out_specs=out_specs or [VM] * len(outs),
        scratch_shapes=list(scratch),
        compiler_params=pltpu.CompilerParams(vmem_limit_bytes=limit * 1024 * 1024),
        cost_estimate=pl.CostEstimate(flops=int(flops), bytes_accessed=int(moved), transcendentals=0),
        name=name,
    )(*args)


TILES = pltpu.VMEM((LOCAL, SHARDS, 2 * D, FF_S), BF)
TILE_SEMS = pltpu.SemaphoreType.DMA((LOCAL, SHARDS))


def forward_first(weights, routes, tokens):
    def body(*refs):
        forward_kernel(False, *refs)

    outs = [shape(ROWS, D, dtype=F32), shape(ROWS, 1536), shape(ROWS, D), shape(SLOTS, D), shape(ROWS, 128, dtype=F32)]
    return call(body, outs, [VM] * 3, (weights, routes, tokens), name="dense_forward_first", flops=4e9)


def forward_last(weights, routes, grad, prev, ret, keep):
    def body(*refs):
        forward_kernel(True, *refs)

    outs = [shape(ROWS, D, dtype=F32), shape(ROWS, D, dtype=F32), shape(ROWS, 1536), shape(ROWS, D), shape(2 * SLOTS, D)]
    return call(body, outs, [VM] * 6, (weights, routes, grad, prev, ret, keep), name="dense_forward_last", flops=4e9)


DENSE_SCRATCH = (pltpu.VMEM((ROWS, 1536), BF), pltpu.VMEM((2, D, PACK // 2), BF))


def backward_last(*args):
    def body(*refs):
        backward_kernel(True, *refs)

    outs = [shape(D, PACK // 2)] * 2 + [shape(ROWS, D, dtype=F32), shape(IMG, SEQ, D), shape(SLOTS, D)]
    specs = [SM] + [VM] * (len(args) - 1)
    return call(body, outs, specs, args, DENSE_SCRATCH, name="dense_backward_last", flops=1e10)


def backward_first(*args):
    def body(*refs):
        backward_kernel(False, *refs)

    outs = [shape(D, PACK // 2)] * 2 + [shape(IMG, SEQ, D, dtype=F32)]
    specs = [SM] + [VM] * (len(args) - 1)
    return call(body, outs, specs, args, DENSE_SCRATCH, name="dense_backward_first", flops=1e10)


def experts_forward(recv, source):
    outs = [shape(SLOTS, D), shape(SLOTS, D)]
    return call(
        expert_forward, outs, [VM, HM], (recv, source), (TILES, TILE_SEMS), name="expert_forward",
        flops=4e9, moved=9e6, limit=54,
    )


def experts_backward(last, args):
    def body(*refs):
        expert_backward(last, *refs)

    outs = [shape((2 if last else 1) * SLOTS, D), shape(SHARDS, LOCAL, 2 * D, FF_S)]
    return call(
        body, outs, [VM] * (len(args) - 1) + [HM], args, (TILES, TILES, TILE_SEMS, TILE_SEMS),
        name="expert_backward_last" if last else "expert_backward_first", flops=1e10, moved=2e7,
        out_specs=[VM, HM], limit=54,
    )


def across(value, dx, dc):
    moves = [(x * 2 + c, ((x + dx) % 4) * 2 + (c + dc) % 2) for x in range(4) for c in range(2)]
    return lax.ppermute(value, "dp", moves)


def swap_experts(value, chunk):
    arrived = lax.all_to_all(value.reshape(GROUPS, chunk, D), "experts", split_axis=0, concat_axis=0, tiled=True)
    return arrived.reshape(GROUPS * chunk, D)


def add(*values):
    total = values[0].astype(F32)
    for value in values[1:]:
        total = total + value.astype(F32)
    return total


def together(*values):
    return lax.optimization_barrier(values)


def sum_shards(grads):
    total = lax.psum_scatter(grads, "dp", scatter_dimension=0, tiled=False).astype(F32)
    return total[:, :D], jnp.concatenate([total[:, D : D + FF_S], total[:, D + FF_S :]], axis=2)


def pack_experts(first, second):
    return jnp.concatenate([first, second[:, :, :FF_S], second[:, :, FF_S:]], axis=1)


def swap_halves(core, mine, other, axis):
    low = core == 0
    return jnp.concatenate([jnp.where(low, mine, other), jnp.where(low, other, mine)], axis=axis)


def near_dense(packed):
    at = lax.axis_index("dp")
    core, chip = at % 2, at // 2
    half = PACK // 2
    low = core == 0
    mine = jnp.where(low, packed[..., :half], packed[..., half:])
    give = jnp.where(low, packed[..., half:], packed[..., :half])
    rows = swap_halves(core, mine, across(give, 0, 1), 1)
    ring = jnp.concatenate([rows, across(rows, -1, 0), across(rows, 2, 0), across(rows, 1, 0)], axis=1)
    return lax.dynamic_slice_in_dim(jnp.concatenate([ring, ring], axis=1), ((4 - chip) % 4) * 8, 32, axis=1)


def finish_dense(half):
    return swap_halves(lax.axis_index("dp") % 2, half, across(half, 0, 1), 1)


def reduce_dense(stays, gots):
    parts = jnp.stack([add(stay, got).astype(BF).reshape(GROUPS, 32, PACK // 2) for stay, got in zip(stays, gots)], axis=1)
    arrived = lax.all_to_all(parts, "experts", split_axis=0, concat_axis=0, tiled=True)
    part = jnp.sum(arrived.astype(F32), axis=0).astype(BF).reshape(LAYERS, 4, 8, PACK // 2).transpose(1, 0, 2, 3)
    columns = [[chip * 2 + core for chip in range(4)] for core in range(2)]
    arrived = lax.all_to_all(part, "dp", split_axis=0, concat_axis=0, tiled=True, axis_index_groups=columns)
    total = jnp.sum(arrived.astype(F32), axis=0)
    core = lax.axis_index("dp") % 2
    low = core == 0
    mine = jnp.where(low, total[:, :4], total[:, 4:])
    got = across(jnp.where(low, total[:, 4:], total[:, :4]).astype(BF), 0, 1).astype(F32)
    return jnp.concatenate([jnp.where(low, mine, got), jnp.where(low, got, mine)], axis=2)


def local(
    tokens,
    cotangent,
    norm_gain,
    qkv_weight,
    proj_weight,
    router_weight,
    expert_in,
    expert_out,
    routes,
):
    pad = ((0, ROWS - TOK), (0, 0))
    tokens_pad = jnp.pad(tokens.reshape(TOK, D), pad)
    grad_pad = jnp.pad(cotangent.reshape(TOK, D), pad)
    routes_pad = [jnp.pad(routes[layer].reshape(TOK, TOP), pad, constant_values=-1) for layer in range(LAYERS)]
    packed = jnp.concatenate(
        [
            qkv_weight,
            proj_weight,
            router_weight,
            norm_gain.transpose(0, 2, 1),
            jnp.zeros((LAYERS, 4, PACK - 2048 - EXPERTS - 2), BF),
        ],
        axis=2,
    )
    near = near_dense(packed)
    expert_packs = [pack_experts(expert_in[layer], expert_out[layer]) for layer in range(LAYERS)]
    at = lax.axis_index("dp").astype(jnp.int32).reshape(1)
    experts_a = lax.all_gather(expert_packs[0], "dp", axis=0, tiled=False)
    halves = lax.all_to_all(
        jnp.broadcast_to(near[None], (GROUPS, LAYERS, 32, PACK // 2)), "experts", split_axis=0, concat_axis=0, tiled=True
    )
    weights_a = finish_dense(halves[:, 0].reshape(D, PACK // 2))

    x1_a, qkv_a, mixed_a, send, keep = forward_first(weights_a, routes_pad[0], tokens_pad)
    recv = swap_experts(send, 24)
    experts_b = lax.all_gather(expert_packs[1], "dp", axis=0, tiled=False)
    ret, rows_a = experts_forward(recv, experts_a)
    ret_a = swap_experts(ret, 24)
    weights_b = finish_dense(halves[:, 1].reshape(D, PACK // 2))
    x_b, x1_b, qkv_b, mixed_b, send = forward_last(weights_b, routes_pad[1], grad_pad, x1_a, ret_a, keep)
    recv = swap_experts(send, 48)
    back_b, grads_b = experts_backward(True, (recv, experts_b))
    sums_b = sum_shards(grads_b)
    back_b = swap_experts(back_b, 48)
    stay_b, give_b, grad, output, send = backward_last(
        at, weights_b, routes_pad[1], grad_pad, back_b, x1_b, x_b, qkv_b, mixed_b, keep
    )
    recv = swap_experts(send, 24)
    back_a, grads_a = experts_backward(False, (rows_a, recv, experts_a))
    sums_a = sum_shards(grads_a)
    back_a, got_b = together(swap_experts(back_a, 24), across(give_b, 0, 1))
    stay_a, give_a, grad_tokens = backward_first(
        at, weights_a, routes_pad[0], grad, ret_a, back_a, x1_a, tokens_pad, qkv_a, mixed_a
    )
    dense = reduce_dense([stay_a, stay_b], [across(give_a, 0, 1), got_b])
    grad_gain = dense[:, :, 2048 + EXPERTS : 2048 + EXPERTS + 2].transpose(0, 2, 1)
    return (
        output,
        grad_tokens,
        grad_gain,
        dense[:, :, :1536],
        dense[:, :, 1536:2048],
        dense[:, :, 2048 : 2048 + EXPERTS],
        jnp.stack([sums_a[0], sums_b[0]]),
        jnp.stack([sums_a[1], sums_b[1]]),
    )


def solution(mesh):
    placed = (
        P(("experts", "dp"), None, None),
        P(("experts", "dp"), None, None),
        P(None, None, ("experts", "dp")),
        P(None, ("experts", "dp"), None),
        P(None, ("experts", "dp"), None),
        P(None, ("experts", "dp"), None),
        P(None, "experts", None, "dp"),
        P(None, "experts", "dp", None),
        P(None, ("experts", "dp"), None, None),
    )
    return jax.shard_map(
        local,
        mesh=mesh,
        in_specs=placed,
        out_specs=(
            P(("experts", "dp"), None, None),
            P(("experts", "dp"), None, None),
            P(None, None, ("experts", "dp")),
            P(None, ("experts", "dp"), None),
            P(None, ("experts", "dp"), None),
            P(None, ("experts", "dp"), None),
            P(None, "experts", None, "dp"),
            P(None, "experts", "dp", None),
        ),
        check_vma=False,
    )
```

```python
import jax
import jax.numpy as jnp
from jax import lax
from jax.experimental import pallas as pl
from jax.experimental.pallas import tpu as pltpu
from jax.sharding import PartitionSpec as P

HEADS = 8
HEAD_DIM = 64
EXPERTS = 32
TOP = 2
LAYERS = 2
CAP = 12
D = 512
SEQ = 50
IMG = 3
TOK = 150
ROWS = 160
GROUPS = 16
LOCAL = 2
SLOTS = 384
HALF = 192
SHARDS = 8
FF_S = 256
WIDE = 2176
EPS = 1e-06
SCALE = HEAD_DIM ** (-0.5)
GELU_C = 0.7978845608028654
GELU_A = 0.044715

BF = jnp.bfloat16
F32 = jnp.float32


def dot(a, b):
    return jnp.dot(a, b, preferred_element_type=F32)


def dot_nt(a, b):
    return lax.dot_general(a, b, (((1,), (1,)), ((), ())), preferred_element_type=F32)


def dot_tn(a, b):
    return lax.dot_general(a, b, (((0,), (0,)), ((), ())), preferred_element_type=F32)


def iota(shape, dim):
    return lax.broadcasted_iota(jnp.int32, shape, dim)


def normalize(values):
    centered = values - jnp.mean(values, axis=-1, keepdims=True)
    inverse = lax.rsqrt(jnp.mean(centered * centered, axis=-1, keepdims=True) + EPS)
    return centered * inverse, inverse


def norm_back(upstream, normed, inverse, gain):
    scaled = upstream * gain
    mean_grad = jnp.mean(scaled, axis=-1, keepdims=True)
    mean_prod = jnp.mean(scaled * normed, axis=-1, keepdims=True)
    return inverse * (scaled - mean_grad - normed * mean_prod)


def split_low(values):
    high = values.astype(BF)
    return high, (values - high.astype(F32)).astype(BF)


def same_image():
    def image(dim):
        place = iota((ROWS, ROWS), dim)
        one = jnp.int32(1)
        zero = jnp.int32(0)
        return (
            jnp.where(place >= SEQ, one, zero)
            + jnp.where(place >= 2 * SEQ, one, zero)
            + jnp.where(place >= 3 * SEQ, one, zero)
        )

    return image(0) == image(1)


def head_probs(query, keys, half, same):
    lanes = iota(query.shape, 1)
    own = (lanes >= HEAD_DIM) if half else (lanes < HEAD_DIM)
    query = jnp.where(own, query, jnp.zeros_like(query))
    scores = jnp.where(same, dot_nt(query, keys) * SCALE, -1e30)
    weights = jnp.exp(scores - jnp.max(scores, axis=-1, keepdims=True))
    return weights / jnp.sum(weights, axis=-1, keepdims=True)


def gains_of(block):
    turned = block.astype(F32).T
    return turned[EXPERTS : EXPERTS + 1], turned[EXPERTS + 1 : EXPERTS + 2]


def routing(second, block, routes, chunk):
    logits = dot(second, block)
    lanes = iota((ROWS, 128), 1)
    logits = jnp.where(lanes < EXPERTS, logits, -1e30)
    shifted = jnp.exp(logits - jnp.max(logits, axis=-1, keepdims=True))
    prob = shifted / jnp.sum(shifted, axis=-1, keepdims=True)
    masks = [jnp.where(lanes == routes[:, k : k + 1], 1.0, 0.0) for k in range(TOP)]
    chosen = [jnp.sum(mask * prob, axis=-1, keepdims=True) for mask in masks]
    total = jnp.where(routes[:, 0:1] >= 0, chosen[0] + chosen[1], 1.0)
    gates = [value / total for value in chosen]
    earlier = jnp.where(iota((ROWS, ROWS), 1) < iota((ROWS, ROWS), 0), 1.0, 0.0).astype(BF)
    before = dot(earlier, (masks[0] + masks[1]).astype(BF))
    places = []
    for k in range(TOP):
        slot = jnp.sum(masks[k] * before, axis=-1, keepdims=True).astype(jnp.int32)
        expert = routes[:, k : k + 1]
        base = (expert >> 1) * chunk + (expert & 1) * CAP
        places.append(jnp.where(expert >= 0, base + slot, -1))
    return prob, masks, total, gates, places


def picks(place, count):
    return jnp.where(iota((ROWS, count), 1) == place, 1.0, 0.0).astype(BF)


def forward_kernel(last, *refs):
    if last:
        (near_ref, far_ref, from_ref, routes_ref, grad_ref, prev_ref, ret_ref, keep_in,
         x_ref, x1_ref, qkv_ref, mixed_ref, send_ref, w_ref) = refs
        kept = keep_in[...]
        back = ret_ref[...]
        stream = prev_ref[...]
        for k in range(TOP):
            place = kept[:, 2 + k : 3 + k].astype(jnp.int32)
            stream = stream + kept[:, k : k + 1] * dot(picks(place, SLOTS), back)
        x_ref[...] = stream
    else:
        (near_ref, far_ref, from_ref, routes_ref, tokens_ref, x1_ref, qkv_ref, mixed_ref, send_ref, keep_ref, w_ref) = refs
        stream = tokens_ref[...].astype(F32)
    chunk = 48 if last else 24
    order = jnp.where(iota((D, D), 0) == from_ref[...], 1.0, 0.0).astype(BF)
    for left, right in ((0, 512), (512, 1024), (1024, 1536), (1536, 2048), (2048, WIDE)):
        w_ref[:, left:right] = (
            dot(order[:, : D // 2], near_ref[:, left:right]) + dot(order[:, D // 2 :], far_ref[:, left:right])
        ).astype(BF)
    block = w_ref[:, 2048:WIDE]
    gain_one, gain_two = gains_of(block)
    normed, _ = normalize(stream)
    first = (normed * gain_one).astype(BF)
    qkv_ref[...] = dot(first, w_ref[:, :1536]).astype(BF)
    same = same_image()
    low_half = iota((ROWS, 128), 1) < HEAD_DIM
    for pair in range(HEADS // 2):
        left = pair * 128
        query = qkv_ref[:, left : left + 128]
        keys = qkv_ref[:, 512 + left : 640 + left]
        values = qkv_ref[:, 1024 + left : 1152 + left]
        parts = [dot(head_probs(query, keys, half, same).astype(BF), values) for half in range(2)]
        mixed_ref[:, left : left + 128] = jnp.where(low_half, parts[0], parts[1]).astype(BF)
    residual = stream + dot(mixed_ref[...], w_ref[:, 1536:2048])
    x1_ref[...] = residual
    normed_two, _ = normalize(residual)
    second = (normed_two * gain_two).astype(BF)
    _, _, _, gates, places = routing(second, block, routes_ref[...], chunk)
    count = GROUPS * chunk
    outgoing = dot_tn(picks(places[0], count) + picks(places[1], count), second)
    if last:
        grad = grad_ref[...].astype(F32)
        for k in range(TOP):
            outgoing = outgoing + dot_tn(
                picks(jnp.where(places[k] >= 0, places[k] + 24, -1), count), (gates[k] * grad).astype(BF)
            )
    else:
        lanes = iota((ROWS, 128), 1)
        kept = jnp.where(lanes == 0, gates[0], jnp.where(lanes == 1, gates[1], 0.0))
        kept = jnp.where(lanes == 2, places[0].astype(F32), kept)
        keep_ref[...] = jnp.where(lanes == 3, places[1].astype(F32), kept)
    send_ref[...] = outgoing.astype(BF)


def backward_kernel(last, *refs):
    if last:
        (into_ref, w_ref, routes_ref, grad_ref, back_ref, x1_ref, x_ref, qkv_ref, mixed_ref, keep_in,
         stay_ref, give_ref, prev_ref, out_ref, send_ref, dqkv_ref) = refs
        chunk = 48
    else:
        (into_ref, w_ref, routes_ref, grad_ref, ret_ref, back_ref, x1_ref, x_ref, qkv_ref, mixed_ref,
         stay_ref, give_ref, prev_ref, dqkv_ref) = refs
        chunk = 24
    count = GROUPS * chunk
    order = jnp.where(iota((D, D), 0) == into_ref[...], 1.0, 0.0).astype(BF)

    def ordered(values):
        return dot(values, order).astype(BF)

    def store(left, right, values):
        stay_ref[:, left:right] = values[: D // 2].astype(BF)
        give_ref[:, left:right] = values[D // 2 :].astype(BF)

    block = w_ref[:, 2048:WIDE]
    gain_one, gain_two = gains_of(block)
    grad = grad_ref[...].astype(F32)
    residual = x1_ref[...]
    normed_two, inverse_two = normalize(residual)
    second = (normed_two * gain_two).astype(BF)
    prob, masks, total, gates, places = routing(second, block, routes_ref[...], chunk)
    chooser = [picks(place, count) for place in places]
    back = back_ref[...]
    if last:
        returned = back
        shift = [picks(jnp.where(place >= 0, place + 24, -1), count) for place in places]
        drow = dot(shift[0] + shift[1], back)
    else:
        returned = ret_ref[...]
        drow = dot(chooser[0] + chooser[1], back)
    combined = [dot(choice, returned) for choice in chooser]
    if last:
        output = residual + (gates[0] * combined[0] + gates[1] * combined[1])
        for image in range(IMG):
            out_ref[image] = output[image * SEQ : (image + 1) * SEQ].astype(BF)
    dgate = [jnp.sum(grad * value, axis=-1, keepdims=True) for value in combined]
    inner = dgate[0] * gates[0] + dgate[1] * gates[1]
    dprob = sum((dgate[k] - inner) / total * masks[k] for k in range(TOP))
    dlogit = prob * (dprob - jnp.sum(dprob * prob, axis=-1, keepdims=True))
    logit_high, logit_low = split_low(dlogit)
    dsecond = dot_nt(logit_high, block) + dot_nt(logit_low, block) + drow
    second = ordered(second)
    small = dot_tn(second, logit_high) + dot_tn(second, logit_low)
    lanes = iota((ROWS, 128), 1)
    mark_two = jnp.where(lanes == EXPERTS + 1, 1.0, 0.0).astype(BF)
    high, low = split_low(dsecond * normed_two)
    small = small + dot_tn(ordered(high), mark_two) + dot_tn(ordered(low), mark_two)
    grad = grad + norm_back(dsecond, normed_two, inverse_two, gain_two)
    branch = grad.astype(BF)
    store(1536, 2048, dot_tn(ordered(mixed_ref[...]), branch))
    dmixed = dot_nt(branch, w_ref[:, 1536:2048]).astype(BF)
    same = same_image()
    low_half = lanes < HEAD_DIM
    for pair in range(HEADS // 2):
        left = pair * 128
        query = qkv_ref[:, left : left + 128]
        keys = qkv_ref[:, 512 + left : 640 + left]
        values = qkv_ref[:, 1024 + left : 1152 + left]
        upstream = dmixed[:, left : left + 128]
        dq, dk, dv = [], [], []
        for half in range(2):
            own = jnp.logical_not(low_half) if half else low_half
            probs = head_probs(query, keys, half, same)
            dv.append(dot_tn(probs.astype(BF), upstream))
            dprobs = dot_nt(jnp.where(own, upstream, jnp.zeros_like(upstream)), values)
            dscores = probs * (dprobs - jnp.sum(dprobs * probs, axis=-1, keepdims=True))
            dscores = dscores.astype(BF)
            dq.append(dot(dscores, keys) * SCALE)
            dk.append(dot_tn(dscores, query) * SCALE)
        dqkv_ref[:, left : left + 128] = jnp.where(low_half, dq[0], dq[1]).astype(BF)
        dqkv_ref[:, 512 + left : 640 + left] = jnp.where(low_half, dk[0], dk[1]).astype(BF)
        dqkv_ref[:, 1024 + left : 1152 + left] = jnp.where(low_half, dv[0], dv[1]).astype(BF)
    normed, inverse = normalize(x_ref[...].astype(F32))
    first = (normed * gain_one).astype(BF)
    dqkv = dqkv_ref[...]
    first = ordered(first)
    for left in range(0, 1536, 512):
        store(left, left + 512, dot_tn(first, dqkv[:, left : left + 512]))
    dfirst = dot_nt(dqkv, w_ref[:, :1536])
    mark_one = jnp.where(lanes == EXPERTS, 1.0, 0.0).astype(BF)
    high, low = split_low(dfirst * normed)
    small = small + dot_tn(ordered(high), mark_one) + dot_tn(ordered(low), mark_one)
    store(2048, WIDE, small)
    grad = grad + norm_back(dfirst, normed, inverse, gain_one)
    if last:
        prev_ref[...] = grad
        kept = keep_in[...]
        outgoing = jnp.zeros((SLOTS, D), F32)
        for k in range(TOP):
            place = kept[:, 2 + k : 3 + k].astype(jnp.int32)
            outgoing = outgoing + dot_tn(picks(place, SLOTS), (kept[:, k : k + 1] * grad).astype(BF))
        send_ref[...] = outgoing.astype(BF)
    else:
        for image in range(IMG):
            prev_ref[image] = grad[image * SEQ : (image + 1) * SEQ]


def arrange(chunk, shift):
    place = iota((SLOTS, GROUPS * chunk), 0)
    local = jnp.where(place >= HALF, jnp.int32(1), jnp.int32(0))
    rest = place - local * HALF
    source = (rest * 171) >> 11
    target = source * chunk + local * CAP + (rest - source * CAP) + shift
    return jnp.where(iota((SLOTS, GROUPS * chunk), 1) == target, 1.0, 0.0).astype(BF)


def load_weights(source, buffer, sems):
    copies = []
    for local in range(LOCAL):
        for step in range(SHARDS):
            copy = pltpu.make_async_copy(source.at[step, local], buffer.at[local, step], sems.at[local, step])
            copy.start()
            copies.append(copy)
    return copies


def unpack_out(tile):
    return jnp.concatenate([tile[D : D + FF_S], tile[D + FF_S :]], axis=1)


def expert_forward(recv_ref, source, ret_ref, rows_ref, buffer, sems):
    copies = load_weights(source, buffer, sems)
    order = arrange(24, 0)
    rows_ref[...] = dot(order, recv_ref[...]).astype(BF)
    totals = []
    for local in range(LOCAL):
        rows = rows_ref[local * HALF : (local + 1) * HALF]
        total = jnp.zeros((HALF, D), F32)
        for step in range(SHARDS):
            copies[local * SHARDS + step].wait()
            tile = buffer[local, step]
            pre = dot(rows, tile[:D])
            bend = jnp.tanh(GELU_C * (pre + GELU_A * pre * pre * pre))
            hidden = (0.5 * pre * (1.0 + bend)).astype(BF)
            total = total + dot(hidden, unpack_out(tile))
        totals.append(total.astype(BF))
    ret_ref[...] = dot_tn(order, jnp.concatenate(totals, axis=0)).astype(BF)


def expert_backward(last, *refs):
    if last:
        recv_ref, source, back_ref, grads_to, buffer, staged, sems, out_sems = refs
    else:
        rows_ref, recv_ref, source, back_ref, grads_to, buffer, staged, sems, out_sems = refs
    copies = load_weights(source, buffer, sems)
    recv = recv_ref[...]
    if last:
        order = arrange(48, 0)
        order_back = arrange(48, 24)
        rows_all = dot(order, recv).astype(BF)
        grads_all = dot(order_back, recv).astype(BF)
    else:
        order_back = arrange(24, 0)
        rows_all = rows_ref[...]
        grads_all = dot(order_back, recv).astype(BF)
    totals, back_totals, sent = [], [], []
    for local in range(LOCAL):
        rows = rows_all[local * HALF : (local + 1) * HALF]
        grads = grads_all[local * HALF : (local + 1) * HALF]
        rows_turned = rows.T
        total = jnp.zeros((HALF, D), F32)
        back_total = jnp.zeros((HALF, D), F32)
        for step in range(SHARDS):
            copies[local * SHARDS + step].wait()
            tile = buffer[local, step]
            first_use = tile[:D]
            second_use = unpack_out(tile)
            pre = dot(rows, first_use)
            square = pre * pre
            bend = jnp.tanh(GELU_C * (pre + GELU_A * pre * square))
            hidden = (0.5 * pre * (1.0 + bend)).astype(BF)
            if last:
                total = total + dot(hidden, second_use)
            slope = 0.5 * (1.0 + bend) + (0.5 * GELU_C) * pre * (1.0 - bend * bend) * (
                1.0 + (3.0 * GELU_A) * square
            )
            dpre = (dot_nt(grads, second_use) * slope).astype(BF)
            back_total = back_total + dot_nt(dpre, first_use)
            grad_out = dot_tn(hidden, grads).astype(BF)
            staged[local, step, :D] = dot(rows_turned, dpre).astype(BF)
            staged[local, step, D : D + FF_S] = grad_out[:, :FF_S]
            staged[local, step, D + FF_S :] = grad_out[:, FF_S:]
            copy = pltpu.make_async_copy(staged.at[local, step], grads_to.at[step, local], out_sems.at[local, step])
            copy.start()
            sent.append(copy)
        totals.append(total.astype(BF))
        back_totals.append(back_total.astype(BF))
    result = dot_tn(order_back, jnp.concatenate(back_totals, axis=0))
    if last:
        result = result + dot_tn(order, jnp.concatenate(totals, axis=0))
    back_ref[...] = result.astype(BF)
    for copy in sent:
        copy.wait()


VM = pl.BlockSpec(memory_space=pltpu.VMEM)
HM = pl.BlockSpec(memory_space=pltpu.HBM)


def shape(*dims, dtype=BF):
    return jax.ShapeDtypeStruct(dims, dtype)


def call(body, outs, in_specs, args, scratch=(), flops=1e9, moved=4e6, name=None, limit=24, out_specs=None):
    return pl.pallas_call(
        body,
        out_shape=outs,
        in_specs=in_specs,
        out_specs=out_specs or [VM] * len(outs),
        scratch_shapes=list(scratch),
        compiler_params=pltpu.CompilerParams(vmem_limit_bytes=limit * 1024 * 1024),
        cost_estimate=pl.CostEstimate(flops=int(flops), bytes_accessed=int(moved), transcendentals=0),
        name=name,
    )(*args)


TILES = pltpu.VMEM((LOCAL, SHARDS, 2 * D, FF_S), BF)
TILE_SEMS = pltpu.SemaphoreType.DMA((LOCAL, SHARDS))


def forward_first(*args):
    def body(*refs):
        forward_kernel(False, *refs)

    outs = [shape(ROWS, D, dtype=F32), shape(ROWS, 1536), shape(ROWS, D), shape(SLOTS, D), shape(ROWS, 128, dtype=F32), shape(D, WIDE)]
    return call(body, outs, [VM] * len(args), args, name="dense_forward_first", flops=4e9)


def forward_last(*args):
    def body(*refs):
        forward_kernel(True, *refs)

    outs = [shape(ROWS, D, dtype=F32), shape(ROWS, D, dtype=F32), shape(ROWS, 1536), shape(ROWS, D), shape(2 * SLOTS, D), shape(D, WIDE)]
    return call(body, outs, [VM] * len(args), args, name="dense_forward_last", flops=4e9)


DENSE_SCRATCH = (pltpu.VMEM((ROWS, 1536), BF),)


def backward_last(*args):
    def body(*refs):
        backward_kernel(True, *refs)

    outs = [shape(D // 2, WIDE)] * 2 + [shape(ROWS, D, dtype=F32), shape(IMG, SEQ, D), shape(SLOTS, D)]
    return call(body, outs, [VM] * len(args), args, DENSE_SCRATCH, name="dense_backward_last", flops=1e10)


def backward_first(*args):
    def body(*refs):
        backward_kernel(False, *refs)

    outs = [shape(D // 2, WIDE)] * 2 + [shape(IMG, SEQ, D, dtype=F32)]
    return call(body, outs, [VM] * len(args), args, DENSE_SCRATCH, name="dense_backward_first", flops=1e10)


def experts_forward(recv, source):
    outs = [shape(SLOTS, D), shape(SLOTS, D)]
    return call(
        expert_forward, outs, [VM, HM], (recv, source), (TILES, TILE_SEMS), name="expert_forward",
        flops=4e9, moved=9e6, limit=54,
    )


def experts_backward(last, args):
    def body(*refs):
        expert_backward(last, *refs)

    outs = [shape((2 if last else 1) * SLOTS, D), shape(SHARDS, LOCAL, 2 * D, FF_S)]
    return call(
        body, outs, [VM] * (len(args) - 1) + [HM], args, (TILES, TILES, TILE_SEMS, TILE_SEMS),
        name="expert_backward_last" if last else "expert_backward_first", flops=1e10, moved=2e7,
        out_specs=[VM, HM], limit=54,
    )


def across(value, dx, dc):
    moves = [(x * 2 + c, ((x + dx) % 4) * 2 + (c + dc) % 2) for x in range(4) for c in range(2)]
    return lax.ppermute(value, "dp", moves)


def swap_experts(value, chunk):
    arrived = lax.all_to_all(value.reshape(GROUPS, chunk, D), "experts", split_axis=0, concat_axis=0, tiled=True)
    return arrived.reshape(GROUPS * chunk, D)


def add(*values):
    total = values[0].astype(F32)
    for value in values[1:]:
        total = total + value.astype(F32)
    return total


def together(*values):
    return lax.optimization_barrier(values)


def sum_shards(grads):
    total = lax.psum_scatter(grads, "dp", scatter_dimension=0, tiled=False).astype(F32)
    return total[:, :D], jnp.concatenate([total[:, D : D + FF_S], total[:, D + FF_S :]], axis=2)


def pack_experts(first, second):
    return jnp.concatenate([first, second[:, :, :FF_S], second[:, :, FF_S:]], axis=1)


def along(value, dy, dz):
    moves = [(y * 4 + z, ((y + dy) % 4) * 4 + (z + dz) % 4) for y in range(4) for z in range(4)]
    return lax.ppermute(value, "experts", moves)


def source_rows(relative):
    group, rank = lax.axis_index("experts"), lax.axis_index("dp")
    place = jnp.arange(D, dtype=jnp.int32)[None]
    half, rest = place // 256, place % 256
    if relative:
        block = ((group // 4 + rest // 64) % 4) * 4 + (group % 4 + rest // 16) % 4
    else:
        block = rest // 16
    chip = (rank // 2 + (rest % 16) // 4) % 4
    return block * 32 + chip * 8 + ((rank % 2 + half) % 2) * 4 + rest % 4


def target_rows():
    core = lax.axis_index("dp") % 2
    place = jnp.arange(D, dtype=jnp.int32)[None]
    half, rest = place // 256, place % 256
    return rest // 4 * 8 + ((core + half) % 2) * 4 + rest % 4


def near_dense(packed):
    return jnp.concatenate([packed, across(packed, -1, 0), across(packed, 2, 0), across(packed, 1, 0)], axis=1)


def swap_dense(stay, got):
    parts = add(stay, got).astype(BF).reshape(GROUPS, 16, WIDE)
    return lax.all_to_all(parts, "experts", split_axis=0, concat_axis=0, tiled=True)


def group_sums(arrived):
    return jnp.sum(arrived.astype(F32), axis=0).astype(BF).reshape(4, 4, WIDE)


def finish_dense(parts):
    columns = [[chip * 2 + core for chip in range(4)] for core in range(2)]
    arrived = lax.all_to_all(
        jnp.stack(parts, axis=1), "dp", split_axis=0, concat_axis=0, tiled=True, axis_index_groups=columns
    )
    return jnp.sum(arrived.astype(F32), axis=0)


def local(
    tokens,
    cotangent,
    norm_gain,
    qkv_weight,
    proj_weight,
    router_weight,
    expert_in,
    expert_out,
    routes,
):
    pad = ((0, ROWS - TOK), (0, 0))
    tokens_pad = jnp.pad(tokens.reshape(TOK, D), pad)
    grad_pad = jnp.pad(cotangent.reshape(TOK, D), pad)
    routes_pad = [jnp.pad(routes[layer].reshape(TOK, TOP), pad, constant_values=-1) for layer in range(LAYERS)]
    packed = jnp.concatenate(
        [
            qkv_weight,
            proj_weight,
            router_weight,
            norm_gain.transpose(0, 2, 1),
            jnp.zeros((LAYERS, 4, WIDE - 2048 - EXPERTS - 2), BF),
        ],
        axis=2,
    )
    near = near_dense(packed)
    expert_packs = [pack_experts(expert_in[layer], expert_out[layer]) for layer in range(LAYERS)]
    rows_from = [source_rows(False), source_rows(True)]
    rows_into = target_rows()
    experts_a = lax.all_gather(expert_packs[0], "dp", axis=0, tiled=False)
    near_b = near[1]
    half_a = lax.all_to_all(
        jnp.broadcast_to(near[0][None], (GROUPS, 16, WIDE)), "experts", split_axis=0, concat_axis=0, tiled=True
    ).reshape(D // 2, WIDE)
    half_a, *ring = together(half_a, near_b, along(near_b, 0, -1), along(near_b, 0, 2), along(near_b, 0, 1))
    near_b = jnp.concatenate(ring, axis=0)
    ring = [near_b, along(near_b, -1, 0), along(near_b, 2, 0), along(near_b, 1, 0)]

    x1_a, qkv_a, mixed_a, send, keep, weights_a = forward_first(
        half_a, across(half_a, 0, 1), rows_from[0], routes_pad[0], tokens_pad
    )
    recv = swap_experts(send, 24)
    experts_b = lax.all_gather(expert_packs[1], "dp", axis=0, tiled=False)
    ret, rows_a = experts_forward(recv, experts_a)
    ret, *ring = together(ret, *ring)
    half_b = jnp.concatenate(ring, axis=0)
    other_b = across(half_b, 0, 1)
    ret_a, half_b, other_b = together(swap_experts(ret, 24), half_b, other_b)
    x_b, x1_b, qkv_b, mixed_b, send, weights_b = forward_last(
        half_b, other_b, rows_from[1], routes_pad[1], grad_pad, x1_a, ret_a, keep
    )
    recv = swap_experts(send, 48)
    back_b, grads_b = experts_backward(True, (recv, experts_b))
    sums_b = sum_shards(grads_b)
    back_b = swap_experts(back_b, 48)
    stay_b, give_b, grad, output, send = backward_last(
        rows_into, weights_b, routes_pad[1], grad_pad, back_b, x1_b, x_b, qkv_b, mixed_b, keep
    )
    recv, got_b = together(swap_experts(send, 24), across(give_b, 0, 1))
    arrived_b = swap_dense(stay_b, got_b)
    back_a, grads_a = experts_backward(False, (rows_a, recv, experts_a))
    back_a, grads_a, arrived_b = together(back_a, grads_a, arrived_b)
    sums_a = sum_shards(grads_a)
    back_a = swap_experts(back_a, 24)
    stay_a, give_a, grad_tokens = backward_first(
        rows_into, weights_a, routes_pad[0], grad, ret_a, back_a, x1_a, tokens_pad, qkv_a, mixed_a
    )
    part_b = group_sums(arrived_b)
    arrived_a = swap_dense(stay_a, across(give_a, 0, 1))
    grad_in, grad_out = jnp.stack([sums_a[0], sums_b[0]]), jnp.stack([sums_a[1], sums_b[1]])
    arrived_a, part_b, grad_in, grad_out = together(arrived_a, part_b, grad_in, grad_out)
    dense = finish_dense([group_sums(arrived_a), part_b])
    grad_gain = dense[:, :, 2048 + EXPERTS : 2048 + EXPERTS + 2].transpose(0, 2, 1)
    return (
        output,
        grad_tokens,
        grad_gain,
        dense[:, :, :1536],
        dense[:, :, 1536:2048],
        dense[:, :, 2048 : 2048 + EXPERTS],
        grad_in,
        grad_out,
    )


def solution(mesh):
    placed = (
        P(("experts", "dp"), None, None),
        P(("experts", "dp"), None, None),
        P(None, None, ("experts", "dp")),
        P(None, ("experts", "dp"), None),
        P(None, ("experts", "dp"), None),
        P(None, ("experts", "dp"), None),
        P(None, "experts", None, "dp"),
        P(None, "experts", "dp", None),
        P(None, ("experts", "dp"), None, None),
    )
    return jax.shard_map(
        local,
        mesh=mesh,
        in_specs=placed,
        out_specs=(
            P(("experts", "dp"), None, None),
            P(("experts", "dp"), None, None),
            P(None, None, ("experts", "dp")),
            P(None, ("experts", "dp"), None),
            P(None, ("experts", "dp"), None),
            P(None, ("experts", "dp"), None),
            P(None, "experts", None, "dp"),
            P(None, "experts", "dp", None),
        ),
        check_vma=False,
    )
```

```python
import jax
import jax.numpy as jnp
from jax import lax
from jax.experimental import pallas as pl
from jax.experimental.pallas import tpu as pltpu
from jax.sharding import PartitionSpec as P

HEADS = 8
HEAD_DIM = 64
EXPERTS = 32
TOP = 2
LAYERS = 2
CAP = 12
D = 512
SEQ = 50
IMG = 3
TOK = 150
ROWS = 160
GROUPS = 16
LOCAL = 2
SLOTS = 384
HALF = 192
SHARDS = 8
FF_S = 256
SPAN = 4
WIDE = 2176
EPS = 1e-06
SCALE = HEAD_DIM ** (-0.5)
GELU_C = 0.7978845608028654
GELU_A = 0.044715

BF = jnp.bfloat16
F32 = jnp.float32


def dot(a, b):
    return jnp.dot(a, b, preferred_element_type=F32)


def dot_nt(a, b):
    return lax.dot_general(a, b, (((1,), (1,)), ((), ())), preferred_element_type=F32)


def dot_tn(a, b):
    return lax.dot_general(a, b, (((0,), (0,)), ((), ())), preferred_element_type=F32)


def iota(shape, dim):
    return lax.broadcasted_iota(jnp.int32, shape, dim)


def normalize(values):
    centered = values - jnp.mean(values, axis=-1, keepdims=True)
    inverse = lax.rsqrt(jnp.mean(centered * centered, axis=-1, keepdims=True) + EPS)
    return centered * inverse, inverse


def norm_back(upstream, normed, inverse, gain):
    scaled = upstream * gain
    mean_grad = jnp.mean(scaled, axis=-1, keepdims=True)
    mean_prod = jnp.mean(scaled * normed, axis=-1, keepdims=True)
    return inverse * (scaled - mean_grad - normed * mean_prod)


def split_low(values):
    high = values.astype(BF)
    return high, (values - high.astype(F32)).astype(BF)


def same_image():
    def image(dim):
        place = iota((2 * ROWS, ROWS), dim)
        if dim == 0:
            place = jnp.where(place >= ROWS, place - ROWS, place)
        one = jnp.int32(1)
        zero = jnp.int32(0)
        return (
            jnp.where(place >= SEQ, one, zero)
            + jnp.where(place >= 2 * SEQ, one, zero)
            + jnp.where(place >= 3 * SEQ, one, zero)
        )

    return image(0) == image(1)


def halves(pair):
    low = iota(pair.shape, 1) < HEAD_DIM
    zero = jnp.zeros_like(pair)
    return jnp.concatenate([jnp.where(low, pair, zero), jnp.where(low, zero, pair)], axis=0)


def pair_probs(queries, keys, same):
    scores = jnp.where(same, dot_nt(queries, keys) * SCALE, -1e30)
    weights = jnp.exp(scores - jnp.max(scores, axis=-1, keepdims=True))
    return weights / jnp.sum(weights, axis=-1, keepdims=True)


def gains_of(block):
    turned = block.astype(F32).T
    return turned[EXPERTS : EXPERTS + 1], turned[EXPERTS + 1 : EXPERTS + 2]


def routing(second, block, routes, chunk):
    logits = dot(second, block)
    lanes = iota((ROWS, 128), 1)
    logits = jnp.where(lanes < EXPERTS, logits, -1e30)
    shifted = jnp.exp(logits - jnp.max(logits, axis=-1, keepdims=True))
    prob = shifted / jnp.sum(shifted, axis=-1, keepdims=True)
    masks = [jnp.where(lanes == routes[:, k : k + 1], 1.0, 0.0) for k in range(TOP)]
    chosen = [jnp.sum(mask * prob, axis=-1, keepdims=True) for mask in masks]
    total = jnp.where(routes[:, 0:1] >= 0, chosen[0] + chosen[1], 1.0)
    gates = [value / total for value in chosen]
    earlier = jnp.where(iota((ROWS, ROWS), 1) < iota((ROWS, ROWS), 0), 1.0, 0.0).astype(BF)
    before = dot(earlier, (masks[0] + masks[1]).astype(BF))
    places = []
    for k in range(TOP):
        slot = jnp.sum(masks[k] * before, axis=-1, keepdims=True).astype(jnp.int32)
        expert = routes[:, k : k + 1]
        base = (expert >> 1) * chunk + (expert & 1) * CAP
        places.append(jnp.where(expert >= 0, base + slot, -1))
    return prob, masks, total, gates, places


def picks(place, count):
    return jnp.where(iota((ROWS, count), 1) == place, 1.0, 0.0).astype(BF)


def columns_as_rows(columns):
    lanes = iota((ROWS, 128), 1)
    table = jnp.zeros((ROWS, 128), F32)
    for lane, column in enumerate(columns):
        table = jnp.where(lanes == lane, column.astype(F32), table)
    turned = table.T
    return [turned[lane : lane + 1].astype(jnp.int32) for lane in range(len(columns))]


def placed(place_row, count):
    return jnp.where(iota((count, ROWS), 0) == place_row, 1.0, 0.0).astype(BF)


def forward_kernel(last, *refs):
    if last:
        (near_ref, far_ref, from_ref, routes_ref, grad_ref, prev_ref, ret_ref, keep_in,
         x_ref, x1_ref, qkv_ref, mixed_ref, send_ref, w_ref) = refs
        kept = keep_in[...]
        back = ret_ref[...]
        stream = prev_ref[...]
        for k in range(TOP):
            place = kept[:, 2 + k : 3 + k].astype(jnp.int32)
            stream = stream + kept[:, k : k + 1] * dot(picks(place, SLOTS), back)
        x_ref[...] = stream
    else:
        (near_ref, far_ref, from_ref, routes_ref, tokens_ref, x1_ref, qkv_ref, mixed_ref, send_ref, keep_ref, w_ref) = refs
        stream = tokens_ref[...].astype(F32)
    chunk = 48 if last else 24
    order = jnp.where(iota((D, D), 0) == from_ref[...], 1.0, 0.0).astype(BF)
    for left, right in ((0, 512), (512, 1024), (1024, 1536), (1536, 2048), (2048, WIDE)):
        w_ref[:, left:right] = (
            dot(order[:, : D // 2], near_ref[:, left:right]) + dot(order[:, D // 2 :], far_ref[:, left:right])
        ).astype(BF)
    block = w_ref[:, 2048:WIDE]
    gain_one, gain_two = gains_of(block)
    normed, _ = normalize(stream)
    first = (normed * gain_one).astype(BF)
    qkv_ref[...] = dot(first, w_ref[:, :1536]).astype(BF)
    same = same_image()
    low_half = iota((ROWS, 128), 1) < HEAD_DIM
    for pair in range(HEADS // 2):
        left = pair * 128
        query = qkv_ref[:, left : left + 128]
        keys = qkv_ref[:, 512 + left : 640 + left]
        values = qkv_ref[:, 1024 + left : 1152 + left]
        both = dot(pair_probs(halves(query), keys, same).astype(BF), values)
        mixed_ref[:, left : left + 128] = jnp.where(low_half, both[:ROWS], both[ROWS:]).astype(BF)
    residual = stream + dot(mixed_ref[...], w_ref[:, 1536:2048])
    x1_ref[...] = residual
    normed_two, _ = normalize(residual)
    second = (normed_two * gain_two).astype(BF)
    _, _, _, gates, places = routing(second, block, routes_ref[...], chunk)
    count = GROUPS * chunk
    place_rows = columns_as_rows(places)
    outgoing = dot(placed(place_rows[0], count) + placed(place_rows[1], count), second)
    if last:
        grad = grad_ref[...].astype(F32)
        for k in range(TOP):
            target = jnp.where(place_rows[k] >= 0, place_rows[k] + 24, -1)
            outgoing = outgoing + dot(placed(target, count), (gates[k] * grad).astype(BF))
    else:
        lanes = iota((ROWS, 128), 1)
        kept = jnp.where(lanes == 0, gates[0], jnp.where(lanes == 1, gates[1], 0.0))
        kept = jnp.where(lanes == 2, places[0].astype(F32), kept)
        keep_ref[...] = jnp.where(lanes == 3, places[1].astype(F32), kept)
    send_ref[...] = outgoing.astype(BF)


def backward_kernel(last, *refs):
    if last:
        (into_ref, w_ref, routes_ref, grad_ref, back_ref, x1_ref, x_ref, qkv_ref, mixed_ref, keep_in,
         stay_ref, give_ref, prev_ref, out_ref, send_ref, dqkv_ref) = refs
        chunk = 48
    else:
        (into_ref, w_ref, routes_ref, grad_ref, ret_ref, back_ref, x1_ref, x_ref, qkv_ref, mixed_ref,
         stay_ref, give_ref, prev_ref, dqkv_ref) = refs
        chunk = 24
    count = GROUPS * chunk
    order = jnp.where(iota((D, D), 1) == into_ref[...], 1.0, 0.0).astype(BF)

    def ordered(values):
        return dot_nt(order, values).astype(BF)

    def store(left, right, values):
        stay_ref[:, left:right] = values[: D // 2].astype(BF)
        give_ref[:, left:right] = values[D // 2 :].astype(BF)

    block = w_ref[:, 2048:WIDE]
    gain_one, gain_two = gains_of(block)
    grad = grad_ref[...].astype(F32)
    residual = x1_ref[...]
    normed_two, inverse_two = normalize(residual)
    second = (normed_two * gain_two).astype(BF)
    prob, masks, total, gates, places = routing(second, block, routes_ref[...], chunk)
    chooser = [picks(place, count) for place in places]
    back = back_ref[...]
    if last:
        returned = back
        shift = [picks(jnp.where(place >= 0, place + 24, -1), count) for place in places]
        drow = dot(shift[0] + shift[1], back)
    else:
        returned = ret_ref[...]
        drow = dot(chooser[0] + chooser[1], back)
    combined = [dot(choice, returned) for choice in chooser]
    if last:
        output = residual + (gates[0] * combined[0] + gates[1] * combined[1])
        for image in range(IMG):
            out_ref[image] = output[image * SEQ : (image + 1) * SEQ].astype(BF)
    dgate = [jnp.sum(grad * value, axis=-1, keepdims=True) for value in combined]
    inner = dgate[0] * gates[0] + dgate[1] * gates[1]
    dprob = sum((dgate[k] - inner) / total * masks[k] for k in range(TOP))
    dlogit = prob * (dprob - jnp.sum(dprob * prob, axis=-1, keepdims=True))
    logit_high, logit_low = split_low(dlogit)
    dsecond = dot_nt(logit_high, block) + dot_nt(logit_low, block) + drow
    second = ordered(second)
    small = dot(second, logit_high) + dot(second, logit_low)
    lanes = iota((ROWS, 128), 1)
    gain_grad_two = jnp.sum(dsecond * normed_two, axis=0, keepdims=True)
    grad = grad + norm_back(dsecond, normed_two, inverse_two, gain_two)
    branch = grad.astype(BF)
    store(1536, 2048, dot(ordered(mixed_ref[...]), branch))
    dmixed = dot_nt(branch, w_ref[:, 1536:2048]).astype(BF)
    same = same_image()
    low_half = lanes < HEAD_DIM
    for pair in range(HEADS // 2):
        left = pair * 128
        query = qkv_ref[:, left : left + 128]
        keys = qkv_ref[:, 512 + left : 640 + left]
        values = qkv_ref[:, 1024 + left : 1152 + left]
        queries = halves(query)
        upstream = halves(dmixed[:, left : left + 128])
        probs = pair_probs(queries, keys, same)
        dv = dot_tn(probs.astype(BF), upstream)
        dprobs = dot_nt(upstream, values)
        dscores = (probs * (dprobs - jnp.sum(dprobs * probs, axis=-1, keepdims=True))).astype(BF)
        dq = dot(dscores, keys) * SCALE
        dk = dot_tn(dscores, queries) * SCALE
        dqkv_ref[:, left : left + 128] = jnp.where(low_half, dq[:ROWS], dq[ROWS:]).astype(BF)
        dqkv_ref[:, 512 + left : 640 + left] = dk.astype(BF)
        dqkv_ref[:, 1024 + left : 1152 + left] = dv.astype(BF)
    normed, inverse = normalize(x_ref[...].astype(F32))
    first = (normed * gain_one).astype(BF)
    dqkv = dqkv_ref[...]
    first = ordered(first)
    for left in range(0, 1536, 512):
        store(left, left + 512, dot(first, dqkv[:, left : left + 512]))
    dfirst = dot_nt(dqkv, w_ref[:, :1536])
    gain_grad_one = jnp.sum(dfirst * normed, axis=0, keepdims=True)
    places = iota((128, D), 0)
    gain_grads = jnp.where(places == EXPERTS, gain_grad_one, jnp.where(places == EXPERTS + 1, gain_grad_two, 0.0))
    high, low = split_low(gain_grads)
    store(2048, WIDE, small + dot_nt(order, high) + dot_nt(order, low))
    grad = grad + norm_back(dfirst, normed, inverse, gain_one)
    if last:
        prev_ref[...] = grad
        kept = keep_in[...]
        outgoing = jnp.zeros((SLOTS, D), F32)
        place_rows = columns_as_rows([kept[:, 2 + k : 3 + k] for k in range(TOP)])
        for k in range(TOP):
            outgoing = outgoing + dot(placed(place_rows[k], SLOTS), (kept[:, k : k + 1] * grad).astype(BF))
        send_ref[...] = outgoing.astype(BF)
    else:
        for image in range(IMG):
            prev_ref[image] = grad[image * SEQ : (image + 1) * SEQ]


def arrange(chunk, shift, turned=False):
    count = GROUPS * chunk
    place = iota((1, SLOTS) if turned else (SLOTS, 1), 1 if turned else 0)
    local = jnp.where(place >= HALF, jnp.int32(1), jnp.int32(0))
    rest = place - local * HALF
    source = (rest * 171) >> 11
    target = source * chunk + local * CAP + (rest - source * CAP) + shift
    other = iota((count, SLOTS), 0) if turned else iota((SLOTS, count), 1)
    return jnp.where(other == target, 1.0, 0.0).astype(BF)


def tile_copies(packed, local, step, wide, tall, sems):
    span, part = step // SPAN, step % SPAN
    columns = pl.ds(part * FF_S, FF_S)
    shard = packed.at[step, local]
    pairs = (
        (shard.at[pl.ds(0, D)], wide.at[local, span, :, columns]),
        (shard.at[pl.ds(D, FF_S)], tall.at[local, span, columns, pl.ds(0, FF_S)]),
        (shard.at[pl.ds(D + FF_S, FF_S)], tall.at[local, span, columns, pl.ds(FF_S, FF_S)]),
    )
    return [(far, here, sems.at[local, step, place]) for place, (far, here) in enumerate(pairs)]


def load_weights(packed, wide, tall, sems):
    copies = []
    for local in range(LOCAL):
        for step in range(SHARDS):
            for far, here, sem in tile_copies(packed, local, step, wide, tall, sems):
                copy = pltpu.make_async_copy(far, here, sem)
                copy.start()
                copies.append(copy)
    return copies


def wait_span(copies, local, span):
    first = 3 * (local * SHARDS + span * SPAN)
    for copy in copies[first : first + 3 * SPAN]:
        copy.wait()


def expert_forward(recv_ref, packed, ret_ref, rows_ref, wide, tall, sems):
    copies = load_weights(packed, wide, tall, sems)
    rows_ref[...] = dot(arrange(24, 0), recv_ref[...]).astype(BF)
    totals = []
    for local in range(LOCAL):
        rows = rows_ref[local * HALF : (local + 1) * HALF]
        total = jnp.zeros((HALF, D), F32)
        for span in range(SHARDS // SPAN):
            wait_span(copies, local, span)
            pre = dot(rows, wide[local, span])
            bend = jnp.tanh(GELU_C * (pre + GELU_A * pre * pre * pre))
            hidden = (0.5 * pre * (1.0 + bend)).astype(BF)
            total = total + dot(hidden, tall[local, span])
        totals.append(total.astype(BF))
    ret_ref[...] = dot(arrange(24, 0, True), jnp.concatenate(totals, axis=0)).astype(BF)


def expert_backward(last, *refs):
    if last:
        recv_ref, packed, back_ref, grads_to, wide, tall, wide_out, tall_out, sems, out_sems = refs
    else:
        rows_ref, recv_ref, packed, back_ref, grads_to, wide, tall, wide_out, tall_out, sems, out_sems = refs
    copies = load_weights(packed, wide, tall, sems)
    recv = recv_ref[...]
    if last:
        rows_all = dot(arrange(48, 0), recv).astype(BF)
        grads_all = dot(arrange(48, 24), recv).astype(BF)
    else:
        rows_all = rows_ref[...]
        grads_all = dot(arrange(24, 0), recv).astype(BF)
    totals, back_totals, sent = [], [], []
    for local in range(LOCAL):
        rows = rows_all[local * HALF : (local + 1) * HALF]
        grads = grads_all[local * HALF : (local + 1) * HALF]
        rows_turned = rows.T
        total = jnp.zeros((HALF, D), F32)
        back_total = jnp.zeros((HALF, D), F32)
        for span in range(SHARDS // SPAN):
            wait_span(copies, local, span)
            first_use = wide[local, span]
            second_use = tall[local, span]
            pre = dot(rows, first_use)
            slope_in = dot_nt(grads, second_use)
            square = pre * pre
            bend = jnp.tanh(GELU_C * (pre + GELU_A * pre * square))
            hidden = (0.5 * pre * (1.0 + bend)).astype(BF)
            slope = 0.5 * (1.0 + bend) + (0.5 * GELU_C) * pre * (1.0 - bend * bend) * (
                1.0 + (3.0 * GELU_A) * square
            )
            dpre = (slope_in * slope).astype(BF)
            if last:
                total = total + dot(hidden, second_use)
            back_total = back_total + dot_nt(dpre, first_use)
            wide_out[local, span] = dot(rows_turned, dpre).astype(BF)
            tall_out[local, span] = dot_tn(hidden, grads).astype(BF)
            for step in range(span * SPAN, (span + 1) * SPAN):
                for far, here, sem in tile_copies(grads_to, local, step, wide_out, tall_out, out_sems):
                    copy = pltpu.make_async_copy(here, far, sem)
                    copy.start()
                    sent.append(copy)
        totals.append(total.astype(BF))
        back_totals.append(back_total.astype(BF))
    result = dot(arrange(48 if last else 24, 24 if last else 0, True), jnp.concatenate(back_totals, axis=0))
    if last:
        result = result + dot(arrange(48, 0, True), jnp.concatenate(totals, axis=0))
    back_ref[...] = result.astype(BF)
    for copy in sent:
        copy.wait()


VM = pl.BlockSpec(memory_space=pltpu.VMEM)
HM = pl.BlockSpec(memory_space=pltpu.HBM)


def shape(*dims, dtype=BF):
    return jax.ShapeDtypeStruct(dims, dtype)


def call(body, outs, in_specs, args, scratch=(), flops=1e9, moved=4e6, name=None, limit=24, out_specs=None):
    return pl.pallas_call(
        body,
        out_shape=outs,
        in_specs=in_specs,
        out_specs=out_specs or [VM] * len(outs),
        scratch_shapes=list(scratch),
        compiler_params=pltpu.CompilerParams(vmem_limit_bytes=limit * 1024 * 1024),
        cost_estimate=pl.CostEstimate(flops=int(flops), bytes_accessed=int(moved), transcendentals=0),
        name=name,
    )(*args)


WIDE_TILES = pltpu.VMEM((LOCAL, SHARDS // SPAN, D, SPAN * FF_S), BF)
TALL_TILES = pltpu.VMEM((LOCAL, SHARDS // SPAN, SPAN * FF_S, D), BF)
TILE_SEMS = pltpu.SemaphoreType.DMA((LOCAL, SHARDS, 3))


def forward_first(*args):
    def body(*refs):
        forward_kernel(False, *refs)

    outs = [shape(ROWS, D, dtype=F32), shape(ROWS, 1536), shape(ROWS, D), shape(SLOTS, D), shape(ROWS, 128, dtype=F32), shape(D, WIDE)]
    return call(body, outs, [VM] * len(args), args, name="dense_forward_first", flops=4e9)


def forward_last(*args):
    def body(*refs):
        forward_kernel(True, *refs)

    outs = [shape(ROWS, D, dtype=F32), shape(ROWS, D, dtype=F32), shape(ROWS, 1536), shape(ROWS, D), shape(2 * SLOTS, D), shape(D, WIDE)]
    return call(body, outs, [VM] * len(args), args, name="dense_forward_last", flops=4e9)


DENSE_SCRATCH = (pltpu.VMEM((ROWS, 1536), BF),)


def backward_last(*args):
    def body(*refs):
        backward_kernel(True, *refs)

    outs = [shape(D // 2, WIDE)] * 2 + [shape(ROWS, D, dtype=F32), shape(IMG, SEQ, D), shape(SLOTS, D)]
    return call(body, outs, [VM] * len(args), args, DENSE_SCRATCH, name="dense_backward_last", flops=1e10)


def backward_first(*args):
    def body(*refs):
        backward_kernel(False, *refs)

    outs = [shape(D // 2, WIDE)] * 2 + [shape(IMG, SEQ, D, dtype=F32)]
    return call(body, outs, [VM] * len(args), args, DENSE_SCRATCH, name="dense_backward_first", flops=1e10)


def experts_forward(recv, source):
    outs = [shape(SLOTS, D), shape(SLOTS, D)]
    return call(
        expert_forward, outs, [VM, HM], (recv, source), (WIDE_TILES, TALL_TILES, TILE_SEMS), name="expert_forward",
        flops=4e9, moved=9e6, limit=54,
    )


def experts_backward(last, args):
    def body(*refs):
        expert_backward(last, *refs)

    outs = [shape((2 if last else 1) * SLOTS, D), shape(SHARDS, LOCAL, 2 * D, FF_S)]
    return call(
        body, outs, [VM] * (len(args) - 1) + [HM], args, (WIDE_TILES, TALL_TILES, WIDE_TILES, TALL_TILES, TILE_SEMS, TILE_SEMS),
        name="expert_backward_last" if last else "expert_backward_first", flops=1e10, moved=2e7,
        out_specs=[VM, HM], limit=54,
    )


def across(value, dx, dc):
    moves = [(x * 2 + c, ((x + dx) % 4) * 2 + (c + dc) % 2) for x in range(4) for c in range(2)]
    return lax.ppermute(value, "dp", moves)


def swap_experts(value, chunk):
    arrived = lax.all_to_all(value.reshape(GROUPS, chunk, D), "experts", split_axis=0, concat_axis=0, tiled=True)
    return arrived.reshape(GROUPS * chunk, D)


def add(*values):
    total = values[0].astype(F32)
    for value in values[1:]:
        total = total + value.astype(F32)
    return total


def together(*values):
    return lax.optimization_barrier(values)


def sum_shards(grads):
    return lax.psum_scatter(grads, "dp", scatter_dimension=0, tiled=False)


def unpack_experts(totals):
    total = jnp.stack(totals).astype(F32)
    return total[:, :, :D], jnp.concatenate([total[:, :, D : D + FF_S], total[:, :, D + FF_S :]], axis=3)


def pack_experts(first, second):
    return jnp.concatenate([first, second[:, :, :FF_S], second[:, :, FF_S:]], axis=1)


def along(value, dy, dz):
    moves = [(y * 4 + z, ((y + dy) % 4) * 4 + (z + dz) % 4) for y in range(4) for z in range(4)]
    return lax.ppermute(value, "experts", moves)


def source_rows(relative):
    group, rank = lax.axis_index("experts"), lax.axis_index("dp")
    place = jnp.arange(D, dtype=jnp.int32)[None]
    half, rest = place // 256, place % 256
    if relative:
        block = ((group // 4 + rest // 64) % 4) * 4 + (group % 4 + rest // 16) % 4
    else:
        block = rest // 16
    chip = (rank // 2 + (rest % 16) // 4) % 4
    return block * 32 + chip * 8 + ((rank % 2 + half) % 2) * 4 + rest % 4


def target_rows():
    core = lax.axis_index("dp") % 2
    place = jnp.arange(D, dtype=jnp.int32)[:, None]
    half, rest = place // 256, place % 256
    return rest // 4 * 8 + ((core + half) % 2) * 4 + rest % 4


def near_dense(packed):
    return jnp.concatenate([packed, across(packed, -1, 0), across(packed, 2, 0), across(packed, 1, 0)], axis=1)


def swap_dense(stay, got):
    parts = add(stay, got).astype(BF).reshape(GROUPS, 16, WIDE)
    return lax.all_to_all(parts, "experts", split_axis=0, concat_axis=0, tiled=True)


def group_sums(arrived):
    return jnp.sum(arrived.astype(F32), axis=0).astype(BF).reshape(4, 4, WIDE)


def swap_chips(parts):
    columns = [[chip * 2 + core for chip in range(4)] for core in range(2)]
    return lax.all_to_all(
        jnp.stack(parts, axis=1), "dp", split_axis=0, concat_axis=0, tiled=True, axis_index_groups=columns
    )


def local(
    tokens,
    cotangent,
    norm_gain,
    qkv_weight,
    proj_weight,
    router_weight,
    expert_in,
    expert_out,
    routes,
):
    pad = ((0, ROWS - TOK), (0, 0))
    tokens_pad = jnp.pad(tokens.reshape(TOK, D), pad)
    grad_pad = jnp.pad(cotangent.reshape(TOK, D), pad)
    routes_pad = [jnp.pad(routes[layer].reshape(TOK, TOP), pad, constant_values=-1) for layer in range(LAYERS)]
    packed = jnp.concatenate(
        [
            qkv_weight,
            proj_weight,
            router_weight,
            norm_gain.transpose(0, 2, 1),
            jnp.zeros((LAYERS, 4, WIDE - 2048 - EXPERTS - 2), BF),
        ],
        axis=2,
    )
    near = near_dense(packed)
    expert_packs = [pack_experts(expert_in[layer], expert_out[layer]) for layer in range(LAYERS)]
    rows_from = [source_rows(False), source_rows(True)]
    rows_into = target_rows()
    experts_a = lax.all_gather(expert_packs[0], "dp", axis=0, tiled=False)
    near_b = near[1]
    half_a = lax.all_to_all(
        jnp.broadcast_to(near[0][None], (GROUPS, 16, WIDE)), "experts", split_axis=0, concat_axis=0, tiled=True
    ).reshape(D // 2, WIDE)
    half_a, near_b, pack_b = together(half_a, near_b, expert_packs[1])
    ring = [near_b, along(near_b, 0, -1), along(near_b, 0, 2), along(near_b, 0, 1)]
    x1_a, qkv_a, mixed_a, send, keep, weights_a = forward_first(
        half_a, across(half_a, 0, 1), rows_from[0], routes_pad[0], tokens_pad
    )
    send, *ring = together(send, *ring)
    near_b = jnp.concatenate(ring, axis=0)
    ring = [near_b, along(near_b, -1, 0), along(near_b, 2, 0), along(near_b, 1, 0)]
    recv = swap_experts(send, 24)
    experts_b = lax.all_gather(pack_b, "dp", axis=0, tiled=False)
    ret, rows_a = experts_forward(recv, experts_a)
    ret, *ring = together(ret, *ring)
    half_b = jnp.concatenate(ring, axis=0)
    other_b = across(half_b, 0, 1)
    ret_a, half_b, other_b = together(swap_experts(ret, 24), half_b, other_b)
    x_b, x1_b, qkv_b, mixed_b, send, weights_b = forward_last(
        half_b, other_b, rows_from[1], routes_pad[1], grad_pad, x1_a, ret_a, keep
    )
    recv = swap_experts(send, 48)
    back_b, grads_b = experts_backward(True, (recv, experts_b))
    sums_b = sum_shards(grads_b)
    back_b = swap_experts(back_b, 48)
    stay_b, give_b, grad, output, send = backward_last(
        rows_into, weights_b, routes_pad[1], grad_pad, back_b, x1_b, x_b, qkv_b, mixed_b, keep
    )
    recv, got_b = together(swap_experts(send, 24), across(give_b, 0, 1))
    arrived_b = swap_dense(stay_b, got_b)
    back_a, grads_a = experts_backward(False, (rows_a, recv, experts_a))
    back_a, grads_a, arrived_b = together(back_a, grads_a, arrived_b)
    sums_a = sum_shards(grads_a)
    back_a = swap_experts(back_a, 24)
    stay_a, give_a, grad_tokens = backward_first(
        rows_into, weights_a, routes_pad[0], grad, ret_a, back_a, x1_a, tokens_pad, qkv_a, mixed_a
    )
    part_b = group_sums(arrived_b)
    arrived_a = swap_dense(stay_a, across(give_a, 0, 1))
    arrived_a, part_b = together(arrived_a, part_b)
    grad_in, grad_out = unpack_experts([sums_a, sums_b])
    arrived, grad_in, grad_out = together(swap_chips([group_sums(arrived_a), part_b]), grad_in, grad_out)
    dense = jnp.sum(arrived.astype(F32), axis=0)
    grad_gain = dense[:, :, 2048 + EXPERTS : 2048 + EXPERTS + 2].transpose(0, 2, 1)
    return (
        output,
        grad_tokens,
        grad_gain,
        dense[:, :, :1536],
        dense[:, :, 1536:2048],
        dense[:, :, 2048 : 2048 + EXPERTS],
        grad_in,
        grad_out,
    )


def solution(mesh):
    placed = (
        P(("experts", "dp"), None, None),
        P(("experts", "dp"), None, None),
        P(None, None, ("experts", "dp")),
        P(None, ("experts", "dp"), None),
        P(None, ("experts", "dp"), None),
        P(None, ("experts", "dp"), None),
        P(None, "experts", None, "dp"),
        P(None, "experts", "dp", None),
        P(None, ("experts", "dp"), None, None),
    )
    return jax.shard_map(
        local,
        mesh=mesh,
        in_specs=placed,
        out_specs=(
            P(("experts", "dp"), None, None),
            P(("experts", "dp"), None, None),
            P(None, None, ("experts", "dp")),
            P(None, ("experts", "dp"), None),
            P(None, ("experts", "dp"), None),
            P(None, ("experts", "dp"), None),
            P(None, "experts", None, "dp"),
            P(None, "experts", "dp", None),
        ),
        check_vma=False,
    )
```

```python
import jax
import jax.numpy as jnp
from jax import lax
from jax.experimental import pallas as pl
from jax.experimental.pallas import tpu as pltpu
from jax.sharding import PartitionSpec as P

HEADS = 8
HEAD_DIM = 64
EXPERTS = 32
TOP = 2
LAYERS = 2
CAP = 12
D = 512
SEQ = 50
IMG = 3
TOK = 150
ROWS = 160
GROUPS = 16
LOCAL = 2
SLOTS = 384
HALF = 192
SHARDS = 8
FF_S = 256
SPAN = 4
WIDE = 2176
EPS = 1e-06
SCALE = HEAD_DIM ** (-0.5)
GELU_C = 0.7978845608028654
GELU_A = 0.044715

BF = jnp.bfloat16
F32 = jnp.float32


def dot(a, b):
    return jnp.dot(a, b, preferred_element_type=F32)


def dot_nt(a, b):
    return lax.dot_general(a, b, (((1,), (1,)), ((), ())), preferred_element_type=F32)


def dot_tn(a, b):
    return lax.dot_general(a, b, (((0,), (0,)), ((), ())), preferred_element_type=F32)


def iota(shape, dim):
    return lax.broadcasted_iota(jnp.int32, shape, dim)


def normalize(values):
    centered = values - jnp.mean(values, axis=-1, keepdims=True)
    inverse = lax.rsqrt(jnp.mean(centered * centered, axis=-1, keepdims=True) + EPS)
    return centered * inverse, inverse


def norm_back(upstream, normed, inverse, gain):
    scaled = upstream * gain
    mean_grad = jnp.mean(scaled, axis=-1, keepdims=True)
    mean_prod = jnp.mean(scaled * normed, axis=-1, keepdims=True)
    return inverse * (scaled - mean_grad - normed * mean_prod)


def split_low(values):
    high = values.astype(BF)
    return high, (values - high.astype(F32)).astype(BF)


def same_image():
    def image(dim):
        place = iota((2 * ROWS, ROWS), dim)
        if dim == 0:
            place = jnp.where(place >= ROWS, place - ROWS, place)
        one = jnp.int32(1)
        zero = jnp.int32(0)
        return (
            jnp.where(place >= SEQ, one, zero)
            + jnp.where(place >= 2 * SEQ, one, zero)
            + jnp.where(place >= 3 * SEQ, one, zero)
        )

    return image(0) == image(1)


def halves(pair):
    low = iota(pair.shape, 1) < HEAD_DIM
    zero = jnp.zeros_like(pair)
    return jnp.concatenate([jnp.where(low, pair, zero), jnp.where(low, zero, pair)], axis=0)


def pair_probs(queries, keys, same):
    scores = jnp.where(same, dot_nt(queries, keys) * SCALE, -1e30)
    weights = jnp.exp(scores - jnp.max(scores, axis=-1, keepdims=True))
    return weights / jnp.sum(weights, axis=-1, keepdims=True)


def gains_of(block):
    turned = block.astype(F32).T
    return turned[EXPERTS : EXPERTS + 1], turned[EXPERTS + 1 : EXPERTS + 2]


def routing(second, block, routes, chunk):
    logits = dot(second, block)
    lanes = iota((ROWS, 128), 1)
    logits = jnp.where(lanes < EXPERTS, logits, -1e30)
    shifted = jnp.exp(logits - jnp.max(logits, axis=-1, keepdims=True))
    prob = shifted / jnp.sum(shifted, axis=-1, keepdims=True)
    masks = [jnp.where(lanes == routes[:, k : k + 1], 1.0, 0.0) for k in range(TOP)]
    chosen = [jnp.sum(mask * prob, axis=-1, keepdims=True) for mask in masks]
    total = jnp.where(routes[:, 0:1] >= 0, chosen[0] + chosen[1], 1.0)
    gates = [value / total for value in chosen]
    earlier = jnp.where(iota((ROWS, ROWS), 1) < iota((ROWS, ROWS), 0), 1.0, 0.0).astype(BF)
    before = dot(earlier, (masks[0] + masks[1]).astype(BF))
    places = []
    for k in range(TOP):
        slot = jnp.sum(masks[k] * before, axis=-1, keepdims=True).astype(jnp.int32)
        expert = routes[:, k : k + 1]
        base = (expert >> 1) * chunk + (expert & 1) * CAP
        places.append(jnp.where(expert >= 0, base + slot, -1))
    return prob, masks, total, gates, places


def picks(place, count):
    return jnp.where(iota((ROWS, count), 1) == place, 1.0, 0.0).astype(BF)


def columns_as_rows(columns):
    lanes = iota((ROWS, 128), 1)
    table = jnp.zeros((ROWS, 128), F32)
    for lane, column in enumerate(columns):
        table = jnp.where(lanes == lane, column.astype(F32), table)
    turned = table.T
    return [turned[lane : lane + 1].astype(jnp.int32) for lane in range(len(columns))]


def placed(place_row, count):
    return jnp.where(iota((count, ROWS), 0) == place_row, 1.0, 0.0).astype(BF)


def forward_kernel(last, *refs):
    if last:
        pieces, refs = refs[:8], refs[8:]
        (from_ref, routes_ref, grad_ref, prev_ref, ret_ref, keep_in,
         x_ref, x1_ref, qkv_ref, mixed_ref, send_ref, w_ref, rows_ref) = refs
        for place, piece in enumerate(pieces):
            rows_ref[place * 64 : (place + 1) * 64] = piece[...]
        near_ref, far_ref = rows_ref.at[: D // 2], rows_ref.at[D // 2 :]
        kept = keep_in[...]
        back = ret_ref[...]
        stream = prev_ref[...]
        for k in range(TOP):
            place = kept[:, 2 + k : 3 + k].astype(jnp.int32)
            stream = stream + kept[:, k : k + 1] * dot(picks(place, SLOTS), back)
        x_ref[...] = stream
    else:
        (near_ref, far_ref, from_ref, routes_ref, tokens_ref, x1_ref, qkv_ref, mixed_ref, send_ref, keep_ref, w_ref) = refs
        stream = tokens_ref[...].astype(F32)
    chunk = 48 if last else 24
    order = jnp.where(iota((D, D), 0) == from_ref[...], 1.0, 0.0).astype(BF)
    for left, right in ((0, 512), (512, 1024), (1024, 1536), (1536, 2048), (2048, WIDE)):
        w_ref[:, left:right] = (
            dot(order[:, : D // 2], near_ref[:, left:right]) + dot(order[:, D // 2 :], far_ref[:, left:right])
        ).astype(BF)
    block = w_ref[:, 2048:WIDE]
    gain_one, gain_two = gains_of(block)
    normed, _ = normalize(stream)
    first = (normed * gain_one).astype(BF)
    qkv_ref[...] = dot(first, w_ref[:, :1536]).astype(BF)
    same = same_image()
    low_half = iota((ROWS, 128), 1) < HEAD_DIM
    for pair in range(HEADS // 2):
        left = pair * 128
        query = qkv_ref[:, left : left + 128]
        keys = qkv_ref[:, 512 + left : 640 + left]
        values = qkv_ref[:, 1024 + left : 1152 + left]
        both = dot(pair_probs(halves(query), keys, same).astype(BF), values)
        mixed_ref[:, left : left + 128] = jnp.where(low_half, both[:ROWS], both[ROWS:]).astype(BF)
    residual = stream + dot(mixed_ref[...], w_ref[:, 1536:2048])
    x1_ref[...] = residual
    normed_two, _ = normalize(residual)
    second = (normed_two * gain_two).astype(BF)
    _, _, _, gates, places = routing(second, block, routes_ref[...], chunk)
    count = GROUPS * chunk
    place_rows = columns_as_rows(places)
    outgoing = dot(placed(place_rows[0], count) + placed(place_rows[1], count), second)
    if last:
        grad = grad_ref[...].astype(F32)
        for k in range(TOP):
            target = jnp.where(place_rows[k] >= 0, place_rows[k] + 24, -1)
            outgoing = outgoing + dot(placed(target, count), (gates[k] * grad).astype(BF))
    else:
        lanes = iota((ROWS, 128), 1)
        kept = jnp.where(lanes == 0, gates[0], jnp.where(lanes == 1, gates[1], 0.0))
        kept = jnp.where(lanes == 2, places[0].astype(F32), kept)
        keep_ref[...] = jnp.where(lanes == 3, places[1].astype(F32), kept)
    send_ref[...] = outgoing.astype(BF)


def backward_kernel(last, *refs):
    if last:
        (into_ref, w_ref, routes_ref, grad_ref, back_ref, x1_ref, x_ref, qkv_ref, mixed_ref, keep_in,
         stay_ref, give_ref, prev_ref, out_ref, send_ref, dqkv_ref) = refs
        chunk = 48
    else:
        (into_ref, w_ref, routes_ref, grad_ref, ret_ref, back_ref, x1_ref, x_ref, qkv_ref, mixed_ref,
         stay_ref, give_ref, prev_ref, dqkv_ref) = refs
        chunk = 24
    count = GROUPS * chunk
    order = jnp.where(iota((D, D), 1) == into_ref[...], 1.0, 0.0).astype(BF)

    def ordered(values):
        return dot_nt(order, values).astype(BF)

    def store(left, right, values):
        stay_ref[:, left:right] = values[: D // 2].astype(BF)
        give_ref[:, left:right] = values[D // 2 :].astype(BF)

    block = w_ref[:, 2048:WIDE]
    gain_one, gain_two = gains_of(block)
    grad = grad_ref[...].astype(F32)
    residual = x1_ref[...]
    normed_two, inverse_two = normalize(residual)
    second = (normed_two * gain_two).astype(BF)
    prob, masks, total, gates, places = routing(second, block, routes_ref[...], chunk)
    chooser = [picks(place, count) for place in places]
    back = back_ref[...]
    if last:
        returned = back
        shift = [picks(jnp.where(place >= 0, place + 24, -1), count) for place in places]
        drow = dot(shift[0] + shift[1], back)
    else:
        returned = ret_ref[...]
        drow = dot(chooser[0] + chooser[1], back)
    combined = [dot(choice, returned) for choice in chooser]
    if last:
        output = residual + (gates[0] * combined[0] + gates[1] * combined[1])
        for image in range(IMG):
            out_ref[image] = output[image * SEQ : (image + 1) * SEQ].astype(BF)
    dgate = [jnp.sum(grad * value, axis=-1, keepdims=True) for value in combined]
    inner = dgate[0] * gates[0] + dgate[1] * gates[1]
    dprob = sum((dgate[k] - inner) / total * masks[k] for k in range(TOP))
    dlogit = prob * (dprob - jnp.sum(dprob * prob, axis=-1, keepdims=True))
    logit_high, logit_low = split_low(dlogit)
    dsecond = dot_nt(logit_high, block) + dot_nt(logit_low, block) + drow
    second = ordered(second)
    small = dot(second, logit_high) + dot(second, logit_low)
    lanes = iota((ROWS, 128), 1)
    gain_grad_two = jnp.sum(dsecond * normed_two, axis=0, keepdims=True)
    grad = grad + norm_back(dsecond, normed_two, inverse_two, gain_two)
    branch = grad.astype(BF)
    store(1536, 2048, dot(ordered(mixed_ref[...]), branch))
    dmixed = dot_nt(branch, w_ref[:, 1536:2048]).astype(BF)
    same = same_image()
    low_half = lanes < HEAD_DIM
    for pair in range(HEADS // 2):
        left = pair * 128
        query = qkv_ref[:, left : left + 128]
        keys = qkv_ref[:, 512 + left : 640 + left]
        values = qkv_ref[:, 1024 + left : 1152 + left]
        queries = halves(query)
        upstream = halves(dmixed[:, left : left + 128])
        probs = pair_probs(queries, keys, same)
        dv = dot_tn(probs.astype(BF), upstream)
        dprobs = dot_nt(upstream, values)
        dscores = (probs * (dprobs - jnp.sum(dprobs * probs, axis=-1, keepdims=True))).astype(BF)
        dq = dot(dscores, keys) * SCALE
        dk = dot_tn(dscores, queries) * SCALE
        dqkv_ref[:, left : left + 128] = jnp.where(low_half, dq[:ROWS], dq[ROWS:]).astype(BF)
        dqkv_ref[:, 512 + left : 640 + left] = dk.astype(BF)
        dqkv_ref[:, 1024 + left : 1152 + left] = dv.astype(BF)
    normed, inverse = normalize(x_ref[...].astype(F32))
    first = (normed * gain_one).astype(BF)
    dqkv = dqkv_ref[...]
    first = ordered(first)
    for left in range(0, 1536, 512):
        store(left, left + 512, dot(first, dqkv[:, left : left + 512]))
    dfirst = dot_nt(dqkv, w_ref[:, :1536])
    gain_grad_one = jnp.sum(dfirst * normed, axis=0, keepdims=True)
    places = iota((128, D), 0)
    gain_grads = jnp.where(places == EXPERTS, gain_grad_one, jnp.where(places == EXPERTS + 1, gain_grad_two, 0.0))
    high, low = split_low(gain_grads)
    store(2048, WIDE, small + dot_nt(order, high) + dot_nt(order, low))
    grad = grad + norm_back(dfirst, normed, inverse, gain_one)
    if last:
        prev_ref[...] = grad
        kept = keep_in[...]
        outgoing = jnp.zeros((SLOTS, D), F32)
        place_rows = columns_as_rows([kept[:, 2 + k : 3 + k] for k in range(TOP)])
        for k in range(TOP):
            outgoing = outgoing + dot(placed(place_rows[k], SLOTS), (kept[:, k : k + 1] * grad).astype(BF))
        send_ref[...] = outgoing.astype(BF)
    else:
        for image in range(IMG):
            prev_ref[image] = grad[image * SEQ : (image + 1) * SEQ]


def arrange(chunk, shift, turned=False):
    count = GROUPS * chunk
    place = iota((1, SLOTS) if turned else (SLOTS, 1), 1 if turned else 0)
    local = jnp.where(place >= HALF, jnp.int32(1), jnp.int32(0))
    rest = place - local * HALF
    source = (rest * 171) >> 11
    target = source * chunk + local * CAP + (rest - source * CAP) + shift
    other = iota((count, SLOTS), 0) if turned else iota((SLOTS, count), 1)
    return jnp.where(other == target, 1.0, 0.0).astype(BF)


def tile_copies(packed, local, step, wide, tall, sems):
    span, part = step // SPAN, step % SPAN
    columns = pl.ds(part * FF_S, FF_S)
    shard = packed.at[step, local]
    pairs = (
        (shard.at[pl.ds(0, D)], wide.at[local, span, :, columns]),
        (shard.at[pl.ds(D, FF_S)], tall.at[local, span, columns, pl.ds(0, FF_S)]),
        (shard.at[pl.ds(D + FF_S, FF_S)], tall.at[local, span, columns, pl.ds(FF_S, FF_S)]),
    )
    return [(far, here, sems.at[local, step, place]) for place, (far, here) in enumerate(pairs)]


def load_weights(packed, wide, tall, sems):
    copies = []
    for local in range(LOCAL):
        for step in range(SHARDS):
            for far, here, sem in tile_copies(packed, local, step, wide, tall, sems):
                copy = pltpu.make_async_copy(far, here, sem)
                copy.start()
                copies.append(copy)
    return copies


def wait_span(copies, local, span):
    first = 3 * (local * SHARDS + span * SPAN)
    for copy in copies[first : first + 3 * SPAN]:
        copy.wait()


def expert_forward(recv_ref, packed, ret_ref, rows_ref, wide, tall, sems):
    copies = load_weights(packed, wide, tall, sems)
    rows_ref[...] = dot(arrange(24, 0), recv_ref[...]).astype(BF)
    totals = []
    for local in range(LOCAL):
        rows = rows_ref[local * HALF : (local + 1) * HALF]
        total = jnp.zeros((HALF, D), F32)
        for span in range(SHARDS // SPAN):
            wait_span(copies, local, span)
            pre = dot(rows, wide[local, span])
            bend = jnp.tanh(GELU_C * (pre + GELU_A * pre * pre * pre))
            hidden = (0.5 * pre * (1.0 + bend)).astype(BF)
            total = total + dot(hidden, tall[local, span])
        totals.append(total.astype(BF))
    ret_ref[...] = dot(arrange(24, 0, True), jnp.concatenate(totals, axis=0)).astype(BF)


def expert_backward(last, *refs):
    if last:
        recv_ref, packed, back_ref, grads_to, wide, tall, wide_out, tall_out, sems, out_sems = refs
    else:
        rows_ref, recv_ref, packed, back_ref, grads_to, wide, tall, wide_out, tall_out, sems, out_sems = refs
    copies = load_weights(packed, wide, tall, sems)
    recv = recv_ref[...]
    if last:
        rows_all = dot(arrange(48, 0), recv).astype(BF)
        grads_all = dot(arrange(48, 24), recv).astype(BF)
    else:
        rows_all = rows_ref[...]
        grads_all = dot(arrange(24, 0), recv).astype(BF)
    totals, back_totals, sent = [], [], []
    for local in range(LOCAL):
        rows = rows_all[local * HALF : (local + 1) * HALF]
        grads = grads_all[local * HALF : (local + 1) * HALF]
        rows_turned = rows.T
        total = jnp.zeros((HALF, D), F32)
        back_total = jnp.zeros((HALF, D), F32)
        for span in range(SHARDS // SPAN):
            wait_span(copies, local, span)
            first_use = wide[local, span]
            second_use = tall[local, span]
            pre = dot(rows, first_use)
            slope_in = dot_nt(grads, second_use)
            square = pre * pre
            bend = jnp.tanh(GELU_C * (pre + GELU_A * pre * square))
            hidden = (0.5 * pre * (1.0 + bend)).astype(BF)
            slope = 0.5 * (1.0 + bend) + (0.5 * GELU_C) * pre * (1.0 - bend * bend) * (
                1.0 + (3.0 * GELU_A) * square
            )
            dpre = (slope_in * slope).astype(BF)
            if last:
                total = total + dot(hidden, second_use)
            back_total = back_total + dot_nt(dpre, first_use)
            wide_out[local, span] = dot(rows_turned, dpre).astype(BF)
            tall_out[local, span] = dot_tn(hidden, grads).astype(BF)
            for step in range(span * SPAN, (span + 1) * SPAN):
                for far, here, sem in tile_copies(grads_to, local, step, wide_out, tall_out, out_sems):
                    copy = pltpu.make_async_copy(here, far, sem)
                    copy.start()
                    sent.append(copy)
        totals.append(total.astype(BF))
        back_totals.append(back_total.astype(BF))
    result = dot(arrange(48 if last else 24, 24 if last else 0, True), jnp.concatenate(back_totals, axis=0))
    if last:
        result = result + dot(arrange(48, 0, True), jnp.concatenate(totals, axis=0))
    back_ref[...] = result.astype(BF)
    for copy in sent:
        copy.wait()


VM = pl.BlockSpec(memory_space=pltpu.VMEM)
HM = pl.BlockSpec(memory_space=pltpu.HBM)


def shape(*dims, dtype=BF):
    return jax.ShapeDtypeStruct(dims, dtype)


def call(body, outs, in_specs, args, scratch=(), flops=1e9, moved=4e6, name=None, limit=24, out_specs=None, aliases={}):
    return pl.pallas_call(
        body,
        out_shape=outs,
        in_specs=in_specs,
        out_specs=out_specs or [VM] * len(outs),
        scratch_shapes=list(scratch),
        input_output_aliases=aliases,
        compiler_params=pltpu.CompilerParams(vmem_limit_bytes=limit * 1024 * 1024),
        cost_estimate=pl.CostEstimate(flops=int(flops), bytes_accessed=int(moved), transcendentals=0),
        name=name,
    )(*args)


WIDE_TILES = pltpu.VMEM((LOCAL, SHARDS // SPAN, D, SPAN * FF_S), BF)
TALL_TILES = pltpu.VMEM((LOCAL, SHARDS // SPAN, SPAN * FF_S, D), BF)
TILE_SEMS = pltpu.SemaphoreType.DMA((LOCAL, SHARDS, 3))


def forward_first(*args):
    def body(*refs):
        forward_kernel(False, *refs)

    outs = [shape(ROWS, D, dtype=F32), shape(ROWS, 1536), shape(ROWS, D), shape(SLOTS, D), shape(ROWS, 128, dtype=F32), shape(D, WIDE)]
    return call(body, outs, [VM] * len(args), args, name="dense_forward_first", flops=4e9)


def forward_last(*args):
    def body(*refs):
        forward_kernel(True, *refs)

    outs = [shape(ROWS, D, dtype=F32), shape(ROWS, D, dtype=F32), shape(ROWS, 1536), shape(ROWS, D), shape(2 * SLOTS, D), shape(D, WIDE)]
    return call(
        body, outs, [VM] * len(args), args, [pltpu.VMEM((D, WIDE), BF)], name="dense_forward_last", flops=4e9
    )


DENSE_SCRATCH = (pltpu.VMEM((ROWS, 1536), BF),)


def backward_last(*args):
    def body(*refs):
        backward_kernel(True, *refs)

    outs = [shape(D // 2, WIDE)] * 2 + [shape(ROWS, D, dtype=F32), shape(IMG, SEQ, D), shape(SLOTS, D)]
    return call(body, outs, [VM] * len(args), args, DENSE_SCRATCH, name="dense_backward_last", flops=1e10)


def backward_first(*args):
    def body(*refs):
        backward_kernel(False, *refs)

    outs = [shape(D // 2, WIDE)] * 2 + [shape(IMG, SEQ, D, dtype=F32)]
    return call(body, outs, [VM] * len(args), args, DENSE_SCRATCH, name="dense_backward_first", flops=1e10)


def experts_forward(recv, source):
    outs = [shape(SLOTS, D), shape(SLOTS, D)]
    return call(
        expert_forward, outs, [VM, HM], (recv, source), (WIDE_TILES, TALL_TILES, TILE_SEMS), name="expert_forward",
        flops=4e9, moved=9e6, limit=54,
    )


def experts_backward(last, args):
    def body(*refs):
        expert_backward(last, *refs)

    outs = [shape((2 if last else 1) * SLOTS, D), shape(SHARDS, LOCAL, 2 * D, FF_S)]
    return call(
        body, outs, [VM] * (len(args) - 1) + [HM], args, (WIDE_TILES, TALL_TILES, WIDE_TILES, TALL_TILES, TILE_SEMS, TILE_SEMS),
        name="expert_backward_last" if last else "expert_backward_first", flops=1e10, moved=2e7,
        out_specs=[VM, HM], limit=54,
    )


def across(value, dx, dc):
    moves = [(x * 2 + c, ((x + dx) % 4) * 2 + (c + dc) % 2) for x in range(4) for c in range(2)]
    return lax.ppermute(value, "dp", moves)


def swap_experts(value, chunk):
    arrived = lax.all_to_all(value.reshape(GROUPS, chunk, D), "experts", split_axis=0, concat_axis=0, tiled=True)
    return arrived.reshape(GROUPS * chunk, D)


def add(*values):
    total = values[0].astype(F32)
    for value in values[1:]:
        total = total + value.astype(F32)
    return total


def together(*values):
    return lax.optimization_barrier(values)


def sum_shards(grads):
    return lax.psum_scatter(grads, "dp", scatter_dimension=0, tiled=False)


def unpack_experts(layer, total, earlier=()):
    def body(total_ref, *refs):
        in_ref, out_ref, packed, wide, tall, sems, out_sems = refs[len(earlier) :]
        copies, sent = [], []
        for local in range(LOCAL):
            copies.append(pltpu.make_async_copy(total_ref.at[local], packed.at[local], sems.at[local]))
            copies[-1].start()
        for local in range(LOCAL):
            copies[local].wait()
            wide[local] = packed[local, :D].astype(F32)
            tall[local, :, :FF_S] = packed[local, D : D + FF_S].astype(F32)
            tall[local, :, FF_S:] = packed[local, D + FF_S :].astype(F32)
            for place, (here, far) in enumerate(((wide, in_ref), (tall, out_ref))):
                sent.append(pltpu.make_async_copy(here.at[local], far.at[layer, local], out_sems.at[local, place]))
                sent[-1].start()
        for copy in sent:
            copy.wait()

    in_shape, out_shape = (LOCAL, D, FF_S), (LOCAL, FF_S, D)
    scratch = (
        pltpu.VMEM((LOCAL, 2 * D, FF_S), BF),
        pltpu.VMEM(in_shape, F32),
        pltpu.VMEM(out_shape, F32),
        pltpu.SemaphoreType.DMA((LOCAL,)),
        pltpu.SemaphoreType.DMA((LOCAL, 2)),
    )
    outs = [shape(LAYERS, *in_shape, dtype=F32), shape(LAYERS, *out_shape, dtype=F32)]
    return call(
        body, outs, [HM] * (1 + len(earlier)), (total, *earlier), scratch, name="unpack_experts", flops=1e6,
        moved=6e6, out_specs=[HM] * 2, aliases={1: 0, 2: 1} if earlier else {}, limit=58,
    )


def unpack_dense(arrived):
    def body(arrived_ref, gain_ref, qkv_ref, proj_ref, router_ref):
        for layer in range(LAYERS):
            total = arrived_ref[0, layer].astype(F32)
            for chip in range(1, 4):
                total = total + arrived_ref[chip, layer].astype(F32)
            qkv_ref[layer] = total[:, :1536]
            proj_ref[layer] = total[:, 1536:2048]
            small = total[:, 2048:]
            router_ref[layer] = small[:, :EXPERTS]
            turned = jnp.concatenate([small, small], axis=0).T
            gain_ref[layer] = turned[EXPERTS : EXPERTS + 2, :4]

    outs = [shape(LAYERS, 2, 4, dtype=F32)] + [shape(LAYERS, 4, width, dtype=F32) for width in (1536, 512, EXPERTS)]
    return call(body, outs, [VM], (arrived,), name="unpack_dense", flops=1e6, moved=3e5)


def pack_experts(first, second):
    return jnp.concatenate([first, second[:, :, :FF_S], second[:, :, FF_S:]], axis=1)


def along(value, dy, dz):
    moves = [(y * 4 + z, ((y + dy) % 4) * 4 + (z + dz) % 4) for y in range(4) for z in range(4)]
    return lax.ppermute(value, "experts", moves)


def source_rows(relative):
    group, rank = lax.axis_index("experts"), lax.axis_index("dp")
    place = jnp.arange(D, dtype=jnp.int32)[None]
    half, rest = place // 256, place % 256
    if relative:
        block = ((group // 4 + rest // 64) % 4) * 4 + (group % 4 + rest // 16) % 4
    else:
        block = rest // 16
    chip = (rank // 2 + (rest % 16) // 4) % 4
    return block * 32 + chip * 8 + ((rank % 2 + half) % 2) * 4 + rest % 4


def target_rows():
    core = lax.axis_index("dp") % 2
    place = jnp.arange(D, dtype=jnp.int32)[:, None]
    half, rest = place // 256, place % 256
    return rest // 4 * 8 + ((core + half) % 2) * 4 + rest % 4


def near_dense(packed):
    return jnp.concatenate([packed, across(packed, -1, 0), across(packed, 2, 0), across(packed, 1, 0)], axis=1)


def swap_dense(stay, got):
    parts = add(stay, got).astype(BF).reshape(GROUPS, 16, WIDE)
    return lax.all_to_all(parts, "experts", split_axis=0, concat_axis=0, tiled=True)


def group_sums(arrived):
    return jnp.sum(arrived.astype(F32), axis=0).astype(BF).reshape(4, 4, WIDE)


def swap_chips(parts):
    columns = [[chip * 2 + core for chip in range(4)] for core in range(2)]
    return lax.all_to_all(
        jnp.stack(parts, axis=1), "dp", split_axis=0, concat_axis=0, tiled=True, axis_index_groups=columns
    )


def local(
    tokens,
    cotangent,
    norm_gain,
    qkv_weight,
    proj_weight,
    router_weight,
    expert_in,
    expert_out,
    routes,
):
    pad = ((0, ROWS - TOK), (0, 0))
    tokens_pad = jnp.pad(tokens.reshape(TOK, D), pad)
    grad_pad = jnp.pad(cotangent.reshape(TOK, D), pad)
    routes_pad = [jnp.pad(routes[layer].reshape(TOK, TOP), pad, constant_values=-1) for layer in range(LAYERS)]
    packed = jnp.concatenate(
        [
            qkv_weight,
            proj_weight,
            router_weight,
            norm_gain.transpose(0, 2, 1),
            jnp.zeros((LAYERS, 4, WIDE - 2048 - EXPERTS - 2), BF),
        ],
        axis=2,
    )
    near = near_dense(packed)
    expert_packs = [pack_experts(expert_in[layer], expert_out[layer]) for layer in range(LAYERS)]
    rows_from = [source_rows(False), source_rows(True)]
    rows_into = target_rows()
    experts_a = lax.all_gather(expert_packs[0], "dp", axis=0, tiled=False)
    near_b = near[1]
    half_a = lax.all_to_all(
        jnp.broadcast_to(near[0][None], (GROUPS, 16, WIDE)), "experts", split_axis=0, concat_axis=0, tiled=True
    ).reshape(D // 2, WIDE)
    half_a, near_b, pack_b = together(half_a, near_b, expert_packs[1])
    ring = [near_b, along(near_b, 0, -1), along(near_b, 0, 2), along(near_b, 0, 1)]
    x1_a, qkv_a, mixed_a, send, keep, weights_a = forward_first(
        half_a, across(half_a, 0, 1), rows_from[0], routes_pad[0], tokens_pad
    )
    send, *ring = together(send, *ring)
    near_b = jnp.concatenate(ring, axis=0)
    ring = [near_b, along(near_b, -1, 0), along(near_b, 2, 0), along(near_b, 1, 0)]
    recv = swap_experts(send, 24)
    experts_b = lax.all_gather(pack_b, "dp", axis=0, tiled=False)
    ret, rows_a = experts_forward(recv, experts_a)
    rows_a, *ring = together(rows_a, *ring)
    others = [across(piece, 0, 1) for piece in ring]
    ret_a = swap_experts(ret, 24)
    x_b, x1_b, qkv_b, mixed_b, send, weights_b = forward_last(
        *ring, *others, rows_from[1], routes_pad[1], grad_pad, x1_a, ret_a, keep
    )
    recv = swap_experts(send, 48)
    back_b, grads_b = experts_backward(True, (recv, experts_b))
    sums_b = sum_shards(grads_b)
    back_b = swap_experts(back_b, 48)
    stay_b, give_b, grad, output, send = backward_last(
        rows_into, weights_b, routes_pad[1], grad_pad, back_b, x1_b, x_b, qkv_b, mixed_b, keep
    )
    recv, got_b = together(swap_experts(send, 24), across(give_b, 0, 1))
    arrived_b = swap_dense(stay_b, got_b)
    back_a, grads_a = experts_backward(False, (rows_a, recv, experts_a))
    back_a, grads_a, arrived_b = together(back_a, grads_a, arrived_b)
    sums_a = sum_shards(grads_a)
    back_a = swap_experts(back_a, 24)
    stay_a, give_a, grad_tokens = backward_first(
        rows_into, weights_a, routes_pad[0], grad, ret_a, back_a, x1_a, tokens_pad, qkv_a, mixed_a
    )
    part_b = group_sums(arrived_b)
    arrived_a = swap_dense(stay_a, across(give_a, 0, 1))
    arrived_a, part_b, *early = together(arrived_a, part_b, *unpack_experts(1, sums_b))
    grad_in, grad_out = unpack_experts(0, sums_a, early)
    arrived, grad_in, grad_out = together(swap_chips([group_sums(arrived_a), part_b]), grad_in, grad_out)
    grad_gain, grad_qkv, grad_proj, grad_router = unpack_dense(arrived)
    return (
        output,
        grad_tokens,
        grad_gain,
        grad_qkv,
        grad_proj,
        grad_router,
        grad_in,
        grad_out,
    )


def solution(mesh):
    placed = (
        P(("experts", "dp"), None, None),
        P(("experts", "dp"), None, None),
        P(None, None, ("experts", "dp")),
        P(None, ("experts", "dp"), None),
        P(None, ("experts", "dp"), None),
        P(None, ("experts", "dp"), None),
        P(None, "experts", None, "dp"),
        P(None, "experts", "dp", None),
        P(None, ("experts", "dp"), None, None),
    )
    return jax.shard_map(
        local,
        mesh=mesh,
        in_specs=placed,
        out_specs=(
            P(("experts", "dp"), None, None),
            P(("experts", "dp"), None, None),
            P(None, None, ("experts", "dp")),
            P(None, ("experts", "dp"), None),
            P(None, ("experts", "dp"), None),
            P(None, ("experts", "dp"), None),
            P(None, "experts", None, "dp"),
            P(None, "experts", "dp", None),
        ),
        check_vma=False,
    )
```

```python
import jax
import jax.numpy as jnp
from jax import lax
from jax.experimental import pallas as pl
from jax.experimental.pallas import tpu as pltpu
from jax.sharding import PartitionSpec as P

HEADS = 8
HEAD_DIM = 64
EXPERTS = 32
TOP = 2
LAYERS = 2
CAP = 12
D = 512
SEQ = 50
IMG = 3
TOK = 150
ROWS = 160
GROUPS = 16
LOCAL = 2
SLOTS = 384
HALF = 192
SHARDS = 8
FF_S = 256
SPAN = 4
WIDE = 2176
EPS = 1e-06
SCALE = HEAD_DIM ** (-0.5)
GELU_C = 0.7978845608028654
GELU_A = 0.044715

BF = jnp.bfloat16
F32 = jnp.float32


def dot(a, b):
    return jnp.dot(a, b, preferred_element_type=F32)


def dot_nt(a, b):
    return lax.dot_general(a, b, (((1,), (1,)), ((), ())), preferred_element_type=F32)


def dot_tn(a, b):
    return lax.dot_general(a, b, (((0,), (0,)), ((), ())), preferred_element_type=F32)


def iota(shape, dim):
    return lax.broadcasted_iota(jnp.int32, shape, dim)


def normalize(values):
    centered = values - jnp.mean(values, axis=-1, keepdims=True)
    inverse = lax.rsqrt(jnp.mean(centered * centered, axis=-1, keepdims=True) + EPS)
    return centered * inverse, inverse


def norm_back(upstream, normed, inverse, gain):
    scaled = upstream * gain
    mean_grad = jnp.mean(scaled, axis=-1, keepdims=True)
    mean_prod = jnp.mean(scaled * normed, axis=-1, keepdims=True)
    return inverse * (scaled - mean_grad - normed * mean_prod)


def split_low(values):
    high = values.astype(BF)
    return high, (values - high.astype(F32)).astype(BF)


def same_image():
    def image(dim):
        place = iota((2 * ROWS, ROWS), dim)
        if dim == 0:
            place = jnp.where(place >= ROWS, place - ROWS, place)
        one = jnp.int32(1)
        zero = jnp.int32(0)
        return (
            jnp.where(place >= SEQ, one, zero)
            + jnp.where(place >= 2 * SEQ, one, zero)
            + jnp.where(place >= 3 * SEQ, one, zero)
        )

    return image(0) == image(1)


def halves(pair):
    low = iota(pair.shape, 1) < HEAD_DIM
    zero = jnp.zeros_like(pair)
    return jnp.concatenate([jnp.where(low, pair, zero), jnp.where(low, zero, pair)], axis=0)


def pair_probs(queries, keys, same):
    scores = jnp.where(same, dot_nt(queries, keys) * SCALE, -1e30)
    weights = jnp.exp(scores - jnp.max(scores, axis=-1, keepdims=True))
    return weights / jnp.sum(weights, axis=-1, keepdims=True)


def gains_of(block):
    turned = block.astype(F32).T
    return turned[EXPERTS : EXPERTS + 1], turned[EXPERTS + 1 : EXPERTS + 2]


def routing(second, block, routes, chunk):
    logits = dot(second, block)
    lanes = iota((ROWS, 128), 1)
    logits = jnp.where(lanes < EXPERTS, logits, -1e30)
    shifted = jnp.exp(logits - jnp.max(logits, axis=-1, keepdims=True))
    prob = shifted / jnp.sum(shifted, axis=-1, keepdims=True)
    masks = [jnp.where(lanes == routes[:, k : k + 1], 1.0, 0.0) for k in range(TOP)]
    chosen = [jnp.sum(mask * prob, axis=-1, keepdims=True) for mask in masks]
    total = jnp.where(routes[:, 0:1] >= 0, chosen[0] + chosen[1], 1.0)
    gates = [value / total for value in chosen]
    earlier = jnp.where(iota((ROWS, ROWS), 1) < iota((ROWS, ROWS), 0), 1.0, 0.0).astype(BF)
    before = dot(earlier, (masks[0] + masks[1]).astype(BF))
    places = []
    for k in range(TOP):
        slot = jnp.sum(masks[k] * before, axis=-1, keepdims=True).astype(jnp.int32)
        expert = routes[:, k : k + 1]
        base = (expert >> 1) * chunk + (expert & 1) * CAP
        places.append(jnp.where(expert >= 0, base + slot, -1))
    return prob, masks, total, gates, places


def picks(place, count):
    return jnp.where(iota((ROWS, count), 1) == place, 1.0, 0.0).astype(BF)


def columns_as_rows(columns):
    lanes = iota((ROWS, 128), 1)
    table = jnp.zeros((ROWS, 128), F32)
    for lane, column in enumerate(columns):
        table = jnp.where(lanes == lane, column.astype(F32), table)
    turned = table.T
    return [turned[lane : lane + 1].astype(jnp.int32) for lane in range(len(columns))]


def placed(place_row, count):
    return jnp.where(iota((count, ROWS), 0) == place_row, 1.0, 0.0).astype(BF)


def forward_kernel(last, *refs):
    if last:
        pieces, refs = refs[:8], refs[8:]
        (from_ref, routes_ref, grad_ref, prev_ref, ret_ref, keep_in,
         x_ref, x1_ref, qkv_ref, mixed_ref, send_ref, w_ref, rows_ref) = refs
        for place, piece in enumerate(pieces):
            rows_ref[place * 64 : (place + 1) * 64] = piece[...]
        near_ref, far_ref = rows_ref.at[: D // 2], rows_ref.at[D // 2 :]
        kept = keep_in[...]
        back = ret_ref[...]
        stream = prev_ref[...]
        for k in range(TOP):
            place = kept[:, 2 + k : 3 + k].astype(jnp.int32)
            stream = stream + kept[:, k : k + 1] * dot(picks(place, SLOTS), back)
        x_ref[...] = stream
    else:
        (near_ref, far_ref, from_ref, routes_ref, tokens_ref, x1_ref, qkv_ref, mixed_ref, send_ref, keep_ref, w_ref) = refs
        stream = tokens_ref[...].astype(F32)
    chunk = 48 if last else 24
    order = jnp.where(iota((D, D), 0) == from_ref[...], 1.0, 0.0).astype(BF)
    for left, right in ((0, 512), (512, 1024), (1024, 1536), (1536, 2048), (2048, WIDE)):
        w_ref[:, left:right] = (
            dot(order[:, : D // 2], near_ref[:, left:right]) + dot(order[:, D // 2 :], far_ref[:, left:right])
        ).astype(BF)
    block = w_ref[:, 2048:WIDE]
    gain_one, gain_two = gains_of(block)
    normed, _ = normalize(stream)
    first = (normed * gain_one).astype(BF)
    qkv_ref[...] = dot(first, w_ref[:, :1536]).astype(BF)
    same = same_image()
    low_half = iota((ROWS, 128), 1) < HEAD_DIM
    for pair in range(HEADS // 2):
        left = pair * 128
        query = qkv_ref[:, left : left + 128]
        keys = qkv_ref[:, 512 + left : 640 + left]
        values = qkv_ref[:, 1024 + left : 1152 + left]
        both = dot(pair_probs(halves(query), keys, same).astype(BF), values)
        mixed_ref[:, left : left + 128] = jnp.where(low_half, both[:ROWS], both[ROWS:]).astype(BF)
    residual = stream + dot(mixed_ref[...], w_ref[:, 1536:2048])
    x1_ref[...] = residual
    normed_two, _ = normalize(residual)
    second = (normed_two * gain_two).astype(BF)
    _, _, _, gates, places = routing(second, block, routes_ref[...], chunk)
    count = GROUPS * chunk
    place_rows = columns_as_rows(places)
    outgoing = dot(placed(place_rows[0], count) + placed(place_rows[1], count), second)
    if last:
        grad = grad_ref[...].astype(F32)
        for k in range(TOP):
            target = jnp.where(place_rows[k] >= 0, place_rows[k] + 24, -1)
            outgoing = outgoing + dot(placed(target, count), (gates[k] * grad).astype(BF))
    else:
        lanes = iota((ROWS, 128), 1)
        kept = jnp.where(lanes == 0, gates[0], jnp.where(lanes == 1, gates[1], 0.0))
        kept = jnp.where(lanes == 2, places[0].astype(F32), kept)
        keep_ref[...] = jnp.where(lanes == 3, places[1].astype(F32), kept)
    send_ref[...] = outgoing.astype(BF)


def backward_kernel(last, *refs):
    if last:
        (into_ref, w_ref, routes_ref, grad_ref, back_ref, x1_ref, x_ref, qkv_ref, mixed_ref, keep_in,
         stay_ref, give_ref, prev_ref, out_ref, send_ref, dqkv_ref) = refs
        chunk = 48
    else:
        (into_ref, w_ref, routes_ref, grad_ref, ret_ref, back_ref, x1_ref, x_ref, qkv_ref, mixed_ref,
         stay_ref, give_ref, prev_ref, dqkv_ref) = refs
        chunk = 24
    count = GROUPS * chunk
    order = jnp.where(iota((D, D), 1) == into_ref[...], 1.0, 0.0).astype(BF)

    def ordered(values):
        return dot_nt(order, values).astype(BF)

    def store(left, right, values):
        stay_ref[:, left:right] = values[: D // 2].astype(BF)
        give_ref[:, left:right] = values[D // 2 :].astype(BF)

    block = w_ref[:, 2048:WIDE]
    gain_one, gain_two = gains_of(block)
    grad = grad_ref[...].astype(F32)
    residual = x1_ref[...]
    normed_two, inverse_two = normalize(residual)
    second = (normed_two * gain_two).astype(BF)
    prob, masks, total, gates, places = routing(second, block, routes_ref[...], chunk)
    chooser = [picks(place, count) for place in places]
    back = back_ref[...]
    if last:
        returned = back
        shift = [picks(jnp.where(place >= 0, place + 24, -1), count) for place in places]
        drow = dot(shift[0] + shift[1], back)
    else:
        returned = ret_ref[...]
        drow = dot(chooser[0] + chooser[1], back)
    combined = [dot(choice, returned) for choice in chooser]
    if last:
        output = residual + (gates[0] * combined[0] + gates[1] * combined[1])
        for image in range(IMG):
            out_ref[image] = output[image * SEQ : (image + 1) * SEQ].astype(BF)
    dgate = [jnp.sum(grad * value, axis=-1, keepdims=True) for value in combined]
    inner = dgate[0] * gates[0] + dgate[1] * gates[1]
    dprob = sum((dgate[k] - inner) / total * masks[k] for k in range(TOP))
    dlogit = prob * (dprob - jnp.sum(dprob * prob, axis=-1, keepdims=True))
    logit_high, logit_low = split_low(dlogit)
    dsecond = dot_nt(logit_high, block) + dot_nt(logit_low, block) + drow
    second = ordered(second)
    small = dot(second, logit_high) + dot(second, logit_low)
    lanes = iota((ROWS, 128), 1)
    gain_grad_two = jnp.sum(dsecond * normed_two, axis=0, keepdims=True)
    grad = grad + norm_back(dsecond, normed_two, inverse_two, gain_two)
    branch = grad.astype(BF)
    store(1536, 2048, dot(ordered(mixed_ref[...]), branch))
    dmixed = dot_nt(branch, w_ref[:, 1536:2048]).astype(BF)
    same = same_image()
    low_half = lanes < HEAD_DIM
    for pair in range(HEADS // 2):
        left = pair * 128
        query = qkv_ref[:, left : left + 128]
        keys = qkv_ref[:, 512 + left : 640 + left]
        values = qkv_ref[:, 1024 + left : 1152 + left]
        queries = halves(query)
        upstream = halves(dmixed[:, left : left + 128])
        probs = pair_probs(queries, keys, same)
        dv = dot_tn(probs.astype(BF), upstream)
        dprobs = dot_nt(upstream, values)
        dscores = (probs * (dprobs - jnp.sum(dprobs * probs, axis=-1, keepdims=True))).astype(BF)
        dq = dot(dscores, keys) * SCALE
        dk = dot_tn(dscores, queries) * SCALE
        dqkv_ref[:, left : left + 128] = jnp.where(low_half, dq[:ROWS], dq[ROWS:]).astype(BF)
        dqkv_ref[:, 512 + left : 640 + left] = dk.astype(BF)
        dqkv_ref[:, 1024 + left : 1152 + left] = dv.astype(BF)
    normed, inverse = normalize(x_ref[...].astype(F32))
    first = (normed * gain_one).astype(BF)
    dqkv = dqkv_ref[...]
    first = ordered(first)
    for left in range(0, 1536, 512):
        store(left, left + 512, dot(first, dqkv[:, left : left + 512]))
    dfirst = dot_nt(dqkv, w_ref[:, :1536])
    gain_grad_one = jnp.sum(dfirst * normed, axis=0, keepdims=True)
    places = iota((128, D), 0)
    gain_grads = jnp.where(places == EXPERTS, gain_grad_one, jnp.where(places == EXPERTS + 1, gain_grad_two, 0.0))
    high, low = split_low(gain_grads)
    store(2048, WIDE, small + dot_nt(order, high) + dot_nt(order, low))
    grad = grad + norm_back(dfirst, normed, inverse, gain_one)
    if last:
        prev_ref[...] = grad
        kept = keep_in[...]
        outgoing = jnp.zeros((SLOTS, D), F32)
        place_rows = columns_as_rows([kept[:, 2 + k : 3 + k] for k in range(TOP)])
        for k in range(TOP):
            outgoing = outgoing + dot(placed(place_rows[k], SLOTS), (kept[:, k : k + 1] * grad).astype(BF))
        send_ref[...] = outgoing.astype(BF)
    else:
        for image in range(IMG):
            prev_ref[image] = grad[image * SEQ : (image + 1) * SEQ]


def arrange(chunk, shift, turned=False):
    count = GROUPS * chunk
    place = iota((1, SLOTS) if turned else (SLOTS, 1), 1 if turned else 0)
    local = jnp.where(place >= HALF, jnp.int32(1), jnp.int32(0))
    rest = place - local * HALF
    source = (rest * 171) >> 11
    target = source * chunk + local * CAP + (rest - source * CAP) + shift
    other = iota((count, SLOTS), 0) if turned else iota((SLOTS, count), 1)
    return jnp.where(other == target, 1.0, 0.0).astype(BF)


def tile_copies(packed, local, step, wide, tall, sems):
    span, part = step // SPAN, step % SPAN
    columns = pl.ds(part * FF_S, FF_S)
    shard = packed.at[step, local]
    pairs = (
        (shard.at[pl.ds(0, D)], wide.at[local, span, :, columns]),
        (shard.at[pl.ds(D, FF_S)], tall.at[local, span, columns, pl.ds(0, FF_S)]),
        (shard.at[pl.ds(D + FF_S, FF_S)], tall.at[local, span, columns, pl.ds(FF_S, FF_S)]),
    )
    return [(far, here, sems.at[local, step, place]) for place, (far, here) in enumerate(pairs)]


def load_weights(packed, wide, tall, sems):
    copies = []
    for local in range(LOCAL):
        for step in range(SHARDS):
            for far, here, sem in tile_copies(packed, local, step, wide, tall, sems):
                copy = pltpu.make_async_copy(far, here, sem)
                copy.start()
                copies.append(copy)
    return copies


def wait_span(copies, local, span):
    first = 3 * (local * SHARDS + span * SPAN)
    for copy in copies[first : first + 3 * SPAN]:
        copy.wait()


def expert_forward(recv_ref, packed, ret_ref, rows_ref, wide, tall, sems):
    copies = load_weights(packed, wide, tall, sems)
    rows_ref[...] = dot(arrange(24, 0), recv_ref[...]).astype(BF)
    totals = []
    for local in range(LOCAL):
        rows = rows_ref[local * HALF : (local + 1) * HALF]
        total = jnp.zeros((HALF, D), F32)
        for span in range(SHARDS // SPAN):
            wait_span(copies, local, span)
            pre = dot(rows, wide[local, span])
            bend = jnp.tanh(GELU_C * (pre + GELU_A * pre * pre * pre))
            hidden = (0.5 * pre * (1.0 + bend)).astype(BF)
            total = total + dot(hidden, tall[local, span])
        totals.append(total.astype(BF))
    ret_ref[...] = dot(arrange(24, 0, True), jnp.concatenate(totals, axis=0)).astype(BF)


def expert_backward(last, *refs):
    if last:
        recv_ref, packed, back_ref, grads_to, wide, tall, wide_out, tall_out, sems, out_sems = refs
    else:
        rows_ref, recv_ref, packed, back_ref, grads_to, wide, tall, wide_out, tall_out, sems, out_sems = refs
    copies = load_weights(packed, wide, tall, sems)
    recv = recv_ref[...]
    if last:
        rows_all = dot(arrange(48, 0), recv).astype(BF)
        grads_all = dot(arrange(48, 24), recv).astype(BF)
    else:
        rows_all = rows_ref[...]
        grads_all = dot(arrange(24, 0), recv).astype(BF)
    totals, back_totals, sent = [], [], []
    for local in range(LOCAL):
        rows = rows_all[local * HALF : (local + 1) * HALF]
        grads = grads_all[local * HALF : (local + 1) * HALF]
        rows_turned = rows.T
        total = jnp.zeros((HALF, D), F32)
        back_total = jnp.zeros((HALF, D), F32)
        for span in range(SHARDS // SPAN):
            wait_span(copies, local, span)
            first_use = wide[local, span]
            second_use = tall[local, span]
            pre = dot(rows, first_use)
            slope_in = dot_nt(grads, second_use)
            square = pre * pre
            bend = jnp.tanh(GELU_C * (pre + GELU_A * pre * square))
            hidden = (0.5 * pre * (1.0 + bend)).astype(BF)
            slope = 0.5 * (1.0 + bend) + (0.5 * GELU_C) * pre * (1.0 - bend * bend) * (
                1.0 + (3.0 * GELU_A) * square
            )
            dpre = (slope_in * slope).astype(BF)
            if last:
                total = total + dot(hidden, second_use)
            back_total = back_total + dot_nt(dpre, first_use)
            wide_out[local, span] = dot(rows_turned, dpre).astype(BF)
            tall_out[local, span] = dot_tn(hidden, grads).astype(BF)
            for step in range(span * SPAN, (span + 1) * SPAN):
                for far, here, sem in tile_copies(grads_to, local, step, wide_out, tall_out, out_sems):
                    copy = pltpu.make_async_copy(here, far, sem)
                    copy.start()
                    sent.append(copy)
        totals.append(total.astype(BF))
        back_totals.append(back_total.astype(BF))
    result = dot(arrange(48 if last else 24, 24 if last else 0, True), jnp.concatenate(back_totals, axis=0))
    if last:
        result = result + dot(arrange(48, 0, True), jnp.concatenate(totals, axis=0))
    back_ref[...] = result.astype(BF)
    for copy in sent:
        copy.wait()


VM = pl.BlockSpec(memory_space=pltpu.VMEM)
HM = pl.BlockSpec(memory_space=pltpu.HBM)


def shape(*dims, dtype=BF):
    return jax.ShapeDtypeStruct(dims, dtype)


def call(body, outs, in_specs, args, scratch=(), flops=1e9, moved=4e6, name=None, limit=24, out_specs=None, aliases={}):
    return pl.pallas_call(
        body,
        out_shape=outs,
        in_specs=in_specs,
        out_specs=out_specs or [VM] * len(outs),
        scratch_shapes=list(scratch),
        input_output_aliases=aliases,
        compiler_params=pltpu.CompilerParams(vmem_limit_bytes=limit * 1024 * 1024),
        cost_estimate=pl.CostEstimate(flops=int(flops), bytes_accessed=int(moved), transcendentals=0),
        name=name,
    )(*args)


WIDE_TILES = pltpu.VMEM((LOCAL, SHARDS // SPAN, D, SPAN * FF_S), BF)
TALL_TILES = pltpu.VMEM((LOCAL, SHARDS // SPAN, SPAN * FF_S, D), BF)
TILE_SEMS = pltpu.SemaphoreType.DMA((LOCAL, SHARDS, 3))


def forward_first(*args):
    def body(*refs):
        forward_kernel(False, *refs)

    outs = [shape(ROWS, D, dtype=F32), shape(ROWS, 1536), shape(ROWS, D), shape(SLOTS, D), shape(ROWS, 128, dtype=F32), shape(D, WIDE)]
    return call(body, outs, [VM] * len(args), args, name="dense_forward_first", flops=4e9)


def forward_last(*args):
    def body(*refs):
        forward_kernel(True, *refs)

    outs = [shape(ROWS, D, dtype=F32), shape(ROWS, D, dtype=F32), shape(ROWS, 1536), shape(ROWS, D), shape(2 * SLOTS, D), shape(D, WIDE)]
    return call(
        body, outs, [VM] * len(args), args, [pltpu.VMEM((D, WIDE), BF)], name="dense_forward_last", flops=4e9, limit=58
    )


DENSE_SCRATCH = (pltpu.VMEM((ROWS, 1536), BF),)


def backward_last(*args):
    def body(*refs):
        backward_kernel(True, *refs)

    outs = [shape(D // 2, WIDE)] * 2 + [shape(ROWS, D, dtype=F32), shape(IMG, SEQ, D), shape(SLOTS, D)]
    return call(body, outs, [VM] * len(args), args, DENSE_SCRATCH, name="dense_backward_last", flops=1e10)


def backward_first(*args):
    def body(*refs):
        backward_kernel(False, *refs)

    outs = [shape(D // 2, WIDE)] * 2 + [shape(IMG, SEQ, D, dtype=F32)]
    return call(body, outs, [VM] * len(args), args, DENSE_SCRATCH, name="dense_backward_first", flops=1e10)


def experts_forward(recv, source):
    outs = [shape(SLOTS, D), shape(SLOTS, D)]
    return call(
        expert_forward, outs, [VM, HM], (recv, source), (WIDE_TILES, TALL_TILES, TILE_SEMS), name="expert_forward",
        flops=4e9, moved=9e6, limit=54,
    )


def experts_backward(last, args):
    def body(*refs):
        expert_backward(last, *refs)

    outs = [shape((2 if last else 1) * SLOTS, D), shape(SHARDS, LOCAL, 2 * D, FF_S)]
    return call(
        body, outs, [VM] * (len(args) - 1) + [HM], args, (WIDE_TILES, TALL_TILES, WIDE_TILES, TALL_TILES, TILE_SEMS, TILE_SEMS),
        name="expert_backward_last" if last else "expert_backward_first", flops=1e10, moved=2e7,
        out_specs=[VM, HM], limit=54,
    )


def across(value, dx, dc):
    moves = [(x * 2 + c, ((x + dx) % 4) * 2 + (c + dc) % 2) for x in range(4) for c in range(2)]
    return lax.ppermute(value, "dp", moves)


def swap_experts(value, chunk):
    arrived = lax.all_to_all(value.reshape(GROUPS, chunk, D), "experts", split_axis=0, concat_axis=0, tiled=True)
    return arrived.reshape(GROUPS * chunk, D)


def add(*values):
    total = values[0].astype(F32)
    for value in values[1:]:
        total = total + value.astype(F32)
    return total


def together(*values):
    return lax.optimization_barrier(values)


def sum_shards(grads):
    return lax.psum_scatter(grads, "dp", scatter_dimension=0, tiled=False)


def unpack_experts(layer, total, earlier=()):
    def body(total_ref, *refs):
        in_ref, out_ref, packed, wide, tall, sems, out_sems = refs[len(earlier) :]
        copies, sent = [], []
        for local in range(LOCAL):
            copies.append(pltpu.make_async_copy(total_ref.at[local], packed.at[local], sems.at[local]))
            copies[-1].start()
        for local in range(LOCAL):
            copies[local].wait()
            wide[local] = packed[local, :D].astype(F32)
            tall[local, :, :FF_S] = packed[local, D : D + FF_S].astype(F32)
            tall[local, :, FF_S:] = packed[local, D + FF_S :].astype(F32)
            for place, (here, far) in enumerate(((wide, in_ref), (tall, out_ref))):
                sent.append(pltpu.make_async_copy(here.at[local], far.at[layer, local], out_sems.at[local, place]))
                sent[-1].start()
        for copy in sent:
            copy.wait()

    in_shape, out_shape = (LOCAL, D, FF_S), (LOCAL, FF_S, D)
    scratch = (
        pltpu.VMEM((LOCAL, 2 * D, FF_S), BF),
        pltpu.VMEM(in_shape, F32),
        pltpu.VMEM(out_shape, F32),
        pltpu.SemaphoreType.DMA((LOCAL,)),
        pltpu.SemaphoreType.DMA((LOCAL, 2)),
    )
    outs = [shape(LAYERS, *in_shape, dtype=F32), shape(LAYERS, *out_shape, dtype=F32)]
    return call(
        body, outs, [HM] * (1 + len(earlier)), (total, *earlier), scratch, name="unpack_experts", flops=1e6,
        moved=6e6, out_specs=[HM] * 2, aliases={1: 0, 2: 1} if earlier else {}, limit=58,
    )


def unpack_dense(arrived):
    def body(arrived_ref, gain_ref, qkv_ref, proj_ref, router_ref):
        for layer in range(LAYERS):
            total = arrived_ref[0, layer].astype(F32)
            for chip in range(1, 4):
                total = total + arrived_ref[chip, layer].astype(F32)
            qkv_ref[layer] = total[:, :1536]
            proj_ref[layer] = total[:, 1536:2048]
            small = total[:, 2048:]
            router_ref[layer] = small[:, :EXPERTS]
            turned = jnp.concatenate([small, small], axis=0).T
            gain_ref[layer] = turned[EXPERTS : EXPERTS + 2, :4]

    outs = [shape(LAYERS, 2, 4, dtype=F32)] + [shape(LAYERS, 4, width, dtype=F32) for width in (1536, 512, EXPERTS)]
    return call(body, outs, [VM], (arrived,), name="unpack_dense", flops=1e6, moved=3e5)


def pack_experts(first, second):
    return jnp.concatenate([first, second[:, :, :FF_S], second[:, :, FF_S:]], axis=1)


def along(value, dy, dz):
    moves = [(y * 4 + z, ((y + dy) % 4) * 4 + (z + dz) % 4) for y in range(4) for z in range(4)]
    return lax.ppermute(value, "experts", moves)


def source_rows(relative):
    group, rank = lax.axis_index("experts"), lax.axis_index("dp")
    place = jnp.arange(D, dtype=jnp.int32)[None]
    half, rest = place // 256, place % 256
    if relative:
        block = ((group // 4 + rest // 64) % 4) * 4 + (group % 4 + rest // 16) % 4
    else:
        block = rest // 16
    chip = (rank // 2 + (rest % 16) // 4) % 4
    return block * 32 + chip * 8 + ((rank % 2 + half) % 2) * 4 + rest % 4


def target_rows():
    core = lax.axis_index("dp") % 2
    place = jnp.arange(D, dtype=jnp.int32)[:, None]
    half, rest = place // 256, place % 256
    return rest // 4 * 8 + ((core + half) % 2) * 4 + rest % 4


def near_dense(packed):
    return jnp.concatenate([packed, across(packed, -1, 0), across(packed, 2, 0), across(packed, 1, 0)], axis=1)


def swap_dense(stay, got):
    parts = add(stay, got).astype(BF).reshape(GROUPS, 16, WIDE)
    return lax.all_to_all(parts, "experts", split_axis=0, concat_axis=0, tiled=True)


def group_sums(arrived):
    return jnp.sum(arrived.astype(F32), axis=0).astype(BF).reshape(4, 4, WIDE)


def swap_chips(parts):
    columns = [[chip * 2 + core for chip in range(4)] for core in range(2)]
    return lax.all_to_all(
        jnp.stack(parts, axis=1), "dp", split_axis=0, concat_axis=0, tiled=True, axis_index_groups=columns
    )


def local(
    tokens,
    cotangent,
    norm_gain,
    qkv_weight,
    proj_weight,
    router_weight,
    expert_in,
    expert_out,
    routes,
):
    pad = ((0, ROWS - TOK), (0, 0))
    tokens_pad = jnp.pad(tokens.reshape(TOK, D), pad)
    grad_pad = jnp.pad(cotangent.reshape(TOK, D), pad)
    routes_pad = [jnp.pad(routes[layer].reshape(TOK, TOP), pad, constant_values=-1) for layer in range(LAYERS)]
    packed = jnp.concatenate(
        [
            qkv_weight,
            proj_weight,
            router_weight,
            norm_gain.transpose(0, 2, 1),
            jnp.zeros((LAYERS, 4, WIDE - 2048 - EXPERTS - 2), BF),
        ],
        axis=2,
    )
    near = near_dense(packed)
    expert_packs = [pack_experts(expert_in[layer], expert_out[layer]) for layer in range(LAYERS)]
    rows_from = [source_rows(False), source_rows(True)]
    rows_into = target_rows()
    experts_a = lax.all_gather(expert_packs[0], "dp", axis=0, tiled=False)
    near_b = near[1]
    half_a = lax.all_to_all(
        jnp.broadcast_to(near[0][None], (GROUPS, 16, WIDE)), "experts", split_axis=0, concat_axis=0, tiled=True
    ).reshape(D // 2, WIDE)
    half_a, near_b, pack_b, tokens_pad, grad_pad, rows_into, *rest = together(
        half_a, near_b, expert_packs[1], tokens_pad, grad_pad, rows_into, *routes_pad, *rows_from
    )
    routes_pad, rows_from = rest[:LAYERS], rest[LAYERS:]
    ring = [near_b, along(near_b, 0, -1), along(near_b, 0, 2), along(near_b, 0, 1)]
    x1_a, qkv_a, mixed_a, send, keep, weights_a = forward_first(
        half_a, across(half_a, 0, 1), rows_from[0], routes_pad[0], tokens_pad
    )
    send, *ring = together(send, *ring)
    near_b = jnp.concatenate(ring, axis=0)
    ring = [near_b, along(near_b, -1, 0), along(near_b, 2, 0), along(near_b, 1, 0)]
    recv = swap_experts(send, 24)
    experts_b = lax.all_gather(pack_b, "dp", axis=0, tiled=False)
    ret, rows_a = experts_forward(recv, experts_a)
    rows_a, *ring = together(rows_a, *ring)
    others = [across(piece, 0, 1) for piece in ring]
    ret_a = swap_experts(ret, 24)
    x_b, x1_b, qkv_b, mixed_b, send, weights_b = forward_last(
        *ring, *others, rows_from[1], routes_pad[1], grad_pad, x1_a, ret_a, keep
    )
    recv = swap_experts(send, 48)
    back_b, grads_b = experts_backward(True, (recv, experts_b))
    sums_b = sum_shards(grads_b)
    back_b = swap_experts(back_b, 48)
    stay_b, give_b, grad, output, send = backward_last(
        rows_into, weights_b, routes_pad[1], grad_pad, back_b, x1_b, x_b, qkv_b, mixed_b, keep
    )
    recv, got_b = together(swap_experts(send, 24), across(give_b, 0, 1))
    arrived_b = swap_dense(stay_b, got_b)
    back_a, grads_a = experts_backward(False, (rows_a, recv, experts_a))
    back_a, grads_a, arrived_b = together(back_a, grads_a, arrived_b)
    sums_a = sum_shards(grads_a)
    back_a = swap_experts(back_a, 24)
    stay_a, give_a, grad_tokens = backward_first(
        rows_into, weights_a, routes_pad[0], grad, ret_a, back_a, x1_a, tokens_pad, qkv_a, mixed_a
    )
    part_b = group_sums(arrived_b)
    arrived_a = swap_dense(stay_a, across(give_a, 0, 1))
    arrived_a, part_b, *early = together(arrived_a, part_b, *unpack_experts(1, sums_b))
    grad_in, grad_out = unpack_experts(0, sums_a, early)
    arrived, grad_in, grad_out = together(swap_chips([group_sums(arrived_a), part_b]), grad_in, grad_out)
    grad_gain, grad_qkv, grad_proj, grad_router = unpack_dense(arrived)
    return (
        output,
        grad_tokens,
        grad_gain,
        grad_qkv,
        grad_proj,
        grad_router,
        grad_in,
        grad_out,
    )


def solution(mesh):
    placed = (
        P(("experts", "dp"), None, None),
        P(("experts", "dp"), None, None),
        P(None, None, ("experts", "dp")),
        P(None, ("experts", "dp"), None),
        P(None, ("experts", "dp"), None),
        P(None, ("experts", "dp"), None),
        P(None, "experts", None, "dp"),
        P(None, "experts", "dp", None),
        P(None, ("experts", "dp"), None, None),
    )
    return jax.shard_map(
        local,
        mesh=mesh,
        in_specs=placed,
        out_specs=(
            P(("experts", "dp"), None, None),
            P(("experts", "dp"), None, None),
            P(None, None, ("experts", "dp")),
            P(None, ("experts", "dp"), None),
            P(None, ("experts", "dp"), None),
            P(None, ("experts", "dp"), None),
            P(None, "experts", None, "dp"),
            P(None, "experts", "dp", None),
        ),
        check_vma=False,
    )
```

```python
import jax
import jax.numpy as jnp
from jax import lax
from jax.experimental import pallas as pl
from jax.experimental.pallas import tpu as pltpu
from jax.sharding import PartitionSpec as P

HEADS = 8
HEAD_DIM = 64
EXPERTS = 32
TOP = 2
LAYERS = 2
CAP = 12
D = 512
SEQ = 50
IMG = 3
TOK = 150
ROWS = 160
GROUPS = 16
LOCAL = 2
SLOTS = 384
HALF = 192
SHARDS = 8
FF_S = 256
SPAN = 4
WIDE = 2176
EPS = 1e-06
SCALE = HEAD_DIM ** (-0.5)
GELU_C = 0.7978845608028654
GELU_A = 0.044715

BF = jnp.bfloat16
F32 = jnp.float32


def dot(a, b):
    return jnp.dot(a, b, preferred_element_type=F32)


def dot_nt(a, b):
    return lax.dot_general(a, b, (((1,), (1,)), ((), ())), preferred_element_type=F32)


def dot_tn(a, b):
    return lax.dot_general(a, b, (((0,), (0,)), ((), ())), preferred_element_type=F32)


def iota(shape, dim):
    return lax.broadcasted_iota(jnp.int32, shape, dim)


def normalize(values):
    centered = values - jnp.mean(values, axis=-1, keepdims=True)
    inverse = lax.rsqrt(jnp.mean(centered * centered, axis=-1, keepdims=True) + EPS)
    return centered * inverse, inverse


def norm_back(upstream, normed, inverse, gain):
    scaled = upstream * gain
    mean_grad = jnp.mean(scaled, axis=-1, keepdims=True)
    mean_prod = jnp.mean(scaled * normed, axis=-1, keepdims=True)
    return inverse * (scaled - mean_grad - normed * mean_prod)


def split_low(values):
    high = values.astype(BF)
    return high, (values - high.astype(F32)).astype(BF)


def same_image():
    def image(dim):
        place = iota((2 * ROWS, ROWS), dim)
        if dim == 0:
            place = jnp.where(place >= ROWS, place - ROWS, place)
        one = jnp.int32(1)
        zero = jnp.int32(0)
        return (
            jnp.where(place >= SEQ, one, zero)
            + jnp.where(place >= 2 * SEQ, one, zero)
            + jnp.where(place >= 3 * SEQ, one, zero)
        )

    return image(0) == image(1)


def halves(pair):
    low = iota(pair.shape, 1) < HEAD_DIM
    zero = jnp.zeros_like(pair)
    return jnp.concatenate([jnp.where(low, pair, zero), jnp.where(low, zero, pair)], axis=0)


def pair_probs(queries, keys, same):
    scores = jnp.where(same, dot_nt(queries, keys) * SCALE, -1e30)
    weights = jnp.exp(scores - jnp.max(scores, axis=-1, keepdims=True))
    return weights / jnp.sum(weights, axis=-1, keepdims=True)


def gains_of(block):
    turned = block.astype(F32).T
    return turned[EXPERTS : EXPERTS + 1], turned[EXPERTS + 1 : EXPERTS + 2]


def routing(second, block, routes, chunk):
    logits = dot(second, block)
    lanes = iota((ROWS, 128), 1)
    logits = jnp.where(lanes < EXPERTS, logits, -1e30)
    shifted = jnp.exp(logits - jnp.max(logits, axis=-1, keepdims=True))
    prob = shifted / jnp.sum(shifted, axis=-1, keepdims=True)
    masks = [jnp.where(lanes == routes[:, k : k + 1], 1.0, 0.0) for k in range(TOP)]
    chosen = [jnp.sum(mask * prob, axis=-1, keepdims=True) for mask in masks]
    total = jnp.where(routes[:, 0:1] >= 0, chosen[0] + chosen[1], 1.0)
    gates = [value / total for value in chosen]
    earlier = jnp.where(iota((ROWS, ROWS), 1) < iota((ROWS, ROWS), 0), 1.0, 0.0).astype(BF)
    before = dot(earlier, (masks[0] + masks[1]).astype(BF))
    places = []
    for k in range(TOP):
        slot = jnp.sum(masks[k] * before, axis=-1, keepdims=True).astype(jnp.int32)
        expert = routes[:, k : k + 1]
        base = (expert >> 1) * chunk + (expert & 1) * CAP
        places.append(jnp.where(expert >= 0, base + slot, -1))
    return prob, masks, total, gates, places


def picks(place, count):
    return jnp.where(iota((ROWS, count), 1) == place, 1.0, 0.0).astype(BF)


def columns_as_rows(columns):
    lanes = iota((ROWS, 128), 1)
    table = jnp.zeros((ROWS, 128), F32)
    for lane, column in enumerate(columns):
        table = jnp.where(lanes == lane, column.astype(F32), table)
    turned = table.T
    return [turned[lane : lane + 1].astype(jnp.int32) for lane in range(len(columns))]


def placed(place_row, count):
    return jnp.where(iota((count, ROWS), 0) == place_row, 1.0, 0.0).astype(BF)


def forward_kernel(last, *refs):
    if last:
        pieces, refs = refs[:8], refs[8:]
        (from_ref, routes_ref, grad_ref, prev_ref, ret_ref, keep_in,
         x_ref, x1_ref, qkv_ref, mixed_ref, send_ref, w_ref, rows_ref) = refs
        for place, piece in enumerate(pieces):
            rows_ref[place * 64 : (place + 1) * 64] = piece[...]
        near_ref, far_ref = rows_ref.at[: D // 2], rows_ref.at[D // 2 :]
        kept = keep_in[...]
        back = ret_ref[...]
        stream = prev_ref[...]
        for k in range(TOP):
            place = kept[:, 2 + k : 3 + k].astype(jnp.int32)
            stream = stream + kept[:, k : k + 1] * dot(picks(place, SLOTS), back)
        x_ref[...] = stream
    else:
        (near_ref, far_ref, from_ref, routes_ref, tokens_ref, x1_ref, qkv_ref, mixed_ref, send_ref, keep_ref, w_ref) = refs
        stream = tokens_ref[...].astype(F32)
    chunk = 48 if last else 24
    order = jnp.where(iota((D, D), 0) == from_ref[...], 1.0, 0.0).astype(BF)
    for left, right in ((0, 512), (512, 1024), (1024, 1536), (1536, 2048), (2048, WIDE)):
        w_ref[:, left:right] = (
            dot(order[:, : D // 2], near_ref[:, left:right]) + dot(order[:, D // 2 :], far_ref[:, left:right])
        ).astype(BF)
    block = w_ref[:, 2048:WIDE]
    gain_one, gain_two = gains_of(block)
    normed, _ = normalize(stream)
    first = (normed * gain_one).astype(BF)
    qkv_ref[...] = dot(first, w_ref[:, :1536]).astype(BF)
    same = same_image()
    low_half = iota((ROWS, 128), 1) < HEAD_DIM
    for pair in range(HEADS // 2):
        left = pair * 128
        query = qkv_ref[:, left : left + 128]
        keys = qkv_ref[:, 512 + left : 640 + left]
        values = qkv_ref[:, 1024 + left : 1152 + left]
        both = dot(pair_probs(halves(query), keys, same).astype(BF), values)
        mixed_ref[:, left : left + 128] = jnp.where(low_half, both[:ROWS], both[ROWS:]).astype(BF)
    residual = stream + dot(mixed_ref[...], w_ref[:, 1536:2048])
    x1_ref[...] = residual
    normed_two, _ = normalize(residual)
    second = (normed_two * gain_two).astype(BF)
    _, _, _, gates, places = routing(second, block, routes_ref[...], chunk)
    count = GROUPS * chunk
    place_rows = columns_as_rows(places)
    outgoing = dot(placed(place_rows[0], count) + placed(place_rows[1], count), second)
    if last:
        grad = grad_ref[...].astype(F32)
        for k in range(TOP):
            target = jnp.where(place_rows[k] >= 0, place_rows[k] + 24, -1)
            outgoing = outgoing + dot(placed(target, count), (gates[k] * grad).astype(BF))
    else:
        lanes = iota((ROWS, 128), 1)
        kept = jnp.where(lanes == 0, gates[0], jnp.where(lanes == 1, gates[1], 0.0))
        kept = jnp.where(lanes == 2, places[0].astype(F32), kept)
        keep_ref[...] = jnp.where(lanes == 3, places[1].astype(F32), kept)
    send_ref[...] = outgoing.astype(BF)


def backward_kernel(last, *refs):
    if last:
        (into_ref, w_ref, routes_ref, grad_ref, back_ref, x1_ref, x_ref, qkv_ref, mixed_ref, keep_in,
         stay_ref, give_ref, prev_ref, out_ref, send_ref, dqkv_ref) = refs
        chunk = 48
    else:
        (into_ref, w_ref, routes_ref, grad_ref, ret_ref, back_ref, x1_ref, x_ref, qkv_ref, mixed_ref,
         stay_ref, give_ref, prev_ref, dqkv_ref) = refs
        chunk = 24
    count = GROUPS * chunk
    order = jnp.where(iota((D, D), 1) == into_ref[...], 1.0, 0.0).astype(BF)

    def ordered(values):
        return dot_nt(order, values).astype(BF)

    def store(left, right, values):
        stay_ref[:, left:right] = values[: D // 2].astype(BF)
        give_ref[:, left:right] = values[D // 2 :].astype(BF)

    block = w_ref[:, 2048:WIDE]
    gain_one, gain_two = gains_of(block)
    grad = grad_ref[...].astype(F32)
    residual = x1_ref[...]
    normed_two, inverse_two = normalize(residual)
    second = (normed_two * gain_two).astype(BF)
    prob, masks, total, gates, places = routing(second, block, routes_ref[...], chunk)
    chooser = [picks(place, count) for place in places]
    back = back_ref[...]
    if last:
        returned = back
        shift = [picks(jnp.where(place >= 0, place + 24, -1), count) for place in places]
        drow = dot(shift[0] + shift[1], back)
    else:
        returned = ret_ref[...]
        drow = dot(chooser[0] + chooser[1], back)
    combined = [dot(choice, returned) for choice in chooser]
    if last:
        output = residual + (gates[0] * combined[0] + gates[1] * combined[1])
        for image in range(IMG):
            out_ref[image] = output[image * SEQ : (image + 1) * SEQ].astype(BF)
    dgate = [jnp.sum(grad * value, axis=-1, keepdims=True) for value in combined]
    inner = dgate[0] * gates[0] + dgate[1] * gates[1]
    dprob = sum((dgate[k] - inner) / total * masks[k] for k in range(TOP))
    dlogit = prob * (dprob - jnp.sum(dprob * prob, axis=-1, keepdims=True))
    logit_high, logit_low = split_low(dlogit)
    dsecond = dot_nt(logit_high, block) + dot_nt(logit_low, block) + drow
    second = ordered(second)
    small = dot(second, logit_high) + dot(second, logit_low)
    lanes = iota((ROWS, 128), 1)
    gain_grad_two = jnp.sum(dsecond * normed_two, axis=0, keepdims=True)
    grad = grad + norm_back(dsecond, normed_two, inverse_two, gain_two)
    branch = grad.astype(BF)
    store(1536, 2048, dot(ordered(mixed_ref[...]), branch))
    dmixed = dot_nt(branch, w_ref[:, 1536:2048]).astype(BF)
    same = same_image()
    low_half = lanes < HEAD_DIM
    for pair in range(HEADS // 2):
        left = pair * 128
        query = qkv_ref[:, left : left + 128]
        keys = qkv_ref[:, 512 + left : 640 + left]
        values = qkv_ref[:, 1024 + left : 1152 + left]
        queries = halves(query)
        upstream = halves(dmixed[:, left : left + 128])
        probs = pair_probs(queries, keys, same)
        dv = dot_tn(probs.astype(BF), upstream)
        dprobs = dot_nt(upstream, values)
        dscores = (probs * (dprobs - jnp.sum(dprobs * probs, axis=-1, keepdims=True))).astype(BF)
        dq = dot(dscores, keys) * SCALE
        dk = dot_tn(dscores, queries) * SCALE
        dqkv_ref[:, left : left + 128] = jnp.where(low_half, dq[:ROWS], dq[ROWS:]).astype(BF)
        dqkv_ref[:, 512 + left : 640 + left] = dk.astype(BF)
        dqkv_ref[:, 1024 + left : 1152 + left] = dv.astype(BF)
    normed, inverse = normalize(x_ref[...].astype(F32))
    first = (normed * gain_one).astype(BF)
    dqkv = dqkv_ref[...]
    first = ordered(first)
    for left in range(0, 1536, 512):
        store(left, left + 512, dot(first, dqkv[:, left : left + 512]))
    dfirst = dot_nt(dqkv, w_ref[:, :1536])
    gain_grad_one = jnp.sum(dfirst * normed, axis=0, keepdims=True)
    places = iota((128, D), 0)
    gain_grads = jnp.where(places == EXPERTS, gain_grad_one, jnp.where(places == EXPERTS + 1, gain_grad_two, 0.0))
    high, low = split_low(gain_grads)
    store(2048, WIDE, small + dot_nt(order, high) + dot_nt(order, low))
    grad = grad + norm_back(dfirst, normed, inverse, gain_one)
    if last:
        prev_ref[...] = grad
        kept = keep_in[...]
        outgoing = jnp.zeros((SLOTS, D), F32)
        place_rows = columns_as_rows([kept[:, 2 + k : 3 + k] for k in range(TOP)])
        for k in range(TOP):
            outgoing = outgoing + dot(placed(place_rows[k], SLOTS), (kept[:, k : k + 1] * grad).astype(BF))
        send_ref[...] = outgoing.astype(BF)
    else:
        for image in range(IMG):
            prev_ref[image] = grad[image * SEQ : (image + 1) * SEQ]


def arrange(chunk, shift, turned=False):
    count = GROUPS * chunk
    place = iota((1, SLOTS) if turned else (SLOTS, 1), 1 if turned else 0)
    local = jnp.where(place >= HALF, jnp.int32(1), jnp.int32(0))
    rest = place - local * HALF
    source = (rest * 171) >> 11
    target = source * chunk + local * CAP + (rest - source * CAP) + shift
    other = iota((count, SLOTS), 0) if turned else iota((SLOTS, count), 1)
    return jnp.where(other == target, 1.0, 0.0).astype(BF)


def tile_copies(packed, local, step, wide, tall, sems):
    span, part = step // SPAN, step % SPAN
    columns = pl.ds(part * FF_S, FF_S)
    shard = packed.at[step, local]
    pairs = (
        (shard.at[pl.ds(0, D)], wide.at[local, span, :, columns]),
        (shard.at[pl.ds(D, FF_S)], tall.at[local, span, columns, pl.ds(0, FF_S)]),
        (shard.at[pl.ds(D + FF_S, FF_S)], tall.at[local, span, columns, pl.ds(FF_S, FF_S)]),
    )
    return [(far, here, sems.at[local, step, place]) for place, (far, here) in enumerate(pairs)]


def load_weights(packed, wide, tall, sems):
    copies = []
    for local in range(LOCAL):
        for step in range(SHARDS):
            for far, here, sem in tile_copies(packed, local, step, wide, tall, sems):
                copy = pltpu.make_async_copy(far, here, sem)
                copy.start()
                copies.append(copy)
    return copies


def wait_span(copies, local, span):
    first = 3 * (local * SHARDS + span * SPAN)
    for copy in copies[first : first + 3 * SPAN]:
        copy.wait()


def expert_forward(recv_ref, packed, ret_ref, rows_ref, wide, tall, sems):
    copies = load_weights(packed, wide, tall, sems)
    rows_ref[...] = dot(arrange(24, 0), recv_ref[...]).astype(BF)
    totals = []
    for local in range(LOCAL):
        rows = rows_ref[local * HALF : (local + 1) * HALF]
        total = jnp.zeros((HALF, D), F32)
        for span in range(SHARDS // SPAN):
            wait_span(copies, local, span)
            pre = dot(rows, wide[local, span])
            bend = jnp.tanh(GELU_C * (pre + GELU_A * pre * pre * pre))
            hidden = (0.5 * pre * (1.0 + bend)).astype(BF)
            total = total + dot(hidden, tall[local, span])
        totals.append(total.astype(BF))
    ret_ref[...] = dot(arrange(24, 0, True), jnp.concatenate(totals, axis=0)).astype(BF)


def expert_backward(last, *refs):
    if last:
        recv_ref, packed, back_ref, grads_to, wide, tall, wide_out, tall_out, sems, out_sems = refs
    else:
        rows_ref, recv_ref, packed, back_ref, grads_to, wide, tall, wide_out, tall_out, sems, out_sems = refs
    copies = load_weights(packed, wide, tall, sems)
    recv = recv_ref[...]
    if last:
        rows_all = dot(arrange(48, 0), recv).astype(BF)
        grads_all = dot(arrange(48, 24), recv).astype(BF)
    else:
        rows_all = rows_ref[...]
        grads_all = dot(arrange(24, 0), recv).astype(BF)
    totals, back_totals, sent = [], [], []
    for local in range(LOCAL):
        rows = rows_all[local * HALF : (local + 1) * HALF]
        grads = grads_all[local * HALF : (local + 1) * HALF]
        rows_turned = rows.T
        total = jnp.zeros((HALF, D), F32)
        back_total = jnp.zeros((HALF, D), F32)
        for span in range(SHARDS // SPAN):
            wait_span(copies, local, span)
            first_use = wide[local, span]
            second_use = tall[local, span]
            pre = dot(rows, first_use)
            slope_in = dot_nt(grads, second_use)
            square = pre * pre
            bend = jnp.tanh(GELU_C * (pre + GELU_A * pre * square))
            hidden = (0.5 * pre * (1.0 + bend)).astype(BF)
            slope = 0.5 * (1.0 + bend) + (0.5 * GELU_C) * pre * (1.0 - bend * bend) * (
                1.0 + (3.0 * GELU_A) * square
            )
            dpre = (slope_in * slope).astype(BF)
            if last:
                total = total + dot(hidden, second_use)
            back_total = back_total + dot_nt(dpre, first_use)
            wide_out[local, span] = dot(rows_turned, dpre).astype(BF)
            tall_out[local, span] = dot_tn(hidden, grads).astype(BF)
            for step in range(span * SPAN, (span + 1) * SPAN):
                for far, here, sem in tile_copies(grads_to, local, step, wide_out, tall_out, out_sems):
                    copy = pltpu.make_async_copy(here, far, sem)
                    copy.start()
                    sent.append(copy)
        totals.append(total.astype(BF))
        back_totals.append(back_total.astype(BF))
    result = dot(arrange(48 if last else 24, 24 if last else 0, True), jnp.concatenate(back_totals, axis=0))
    if last:
        result = result + dot(arrange(48, 0, True), jnp.concatenate(totals, axis=0))
    back_ref[...] = result.astype(BF)
    for copy in sent:
        copy.wait()


VM = pl.BlockSpec(memory_space=pltpu.VMEM)
HM = pl.BlockSpec(memory_space=pltpu.HBM)


def shape(*dims, dtype=BF):
    return jax.ShapeDtypeStruct(dims, dtype)


def call(body, outs, in_specs, args, scratch=(), flops=1e9, moved=4e6, name=None, limit=24, out_specs=None, aliases={}):
    return pl.pallas_call(
        body,
        out_shape=outs,
        in_specs=in_specs,
        out_specs=out_specs or [VM] * len(outs),
        scratch_shapes=list(scratch),
        input_output_aliases=aliases,
        compiler_params=pltpu.CompilerParams(vmem_limit_bytes=limit * 1024 * 1024),
        cost_estimate=pl.CostEstimate(flops=int(flops), bytes_accessed=int(moved), transcendentals=0),
        name=name,
    )(*args)


WIDE_TILES = pltpu.VMEM((LOCAL, SHARDS // SPAN, D, SPAN * FF_S), BF)
TALL_TILES = pltpu.VMEM((LOCAL, SHARDS // SPAN, SPAN * FF_S, D), BF)
TILE_SEMS = pltpu.SemaphoreType.DMA((LOCAL, SHARDS, 3))


def forward_first(*args):
    def body(*refs):
        forward_kernel(False, *refs)

    outs = [shape(ROWS, D, dtype=F32), shape(ROWS, 1536), shape(ROWS, D), shape(SLOTS, D), shape(ROWS, 128, dtype=F32), shape(D, WIDE)]
    return call(body, outs, [VM] * len(args), args, name="dense_forward_first", flops=4e9)


def forward_last(*args):
    def body(*refs):
        forward_kernel(True, *refs)

    outs = [shape(ROWS, D, dtype=F32), shape(ROWS, D, dtype=F32), shape(ROWS, 1536), shape(ROWS, D), shape(2 * SLOTS, D), shape(D, WIDE)]
    return call(
        body, outs, [VM] * len(args), args, [pltpu.VMEM((D, WIDE), BF)], name="dense_forward_last", flops=4e9, limit=58
    )


DENSE_SCRATCH = (pltpu.VMEM((ROWS, 1536), BF),)


def backward_last(*args):
    def body(*refs):
        backward_kernel(True, *refs)

    outs = [shape(D // 2, WIDE)] * 2 + [shape(ROWS, D, dtype=F32), shape(IMG, SEQ, D), shape(SLOTS, D)]
    return call(body, outs, [VM] * len(args), args, DENSE_SCRATCH, name="dense_backward_last", flops=1e10)


def backward_first(*args):
    def body(*refs):
        backward_kernel(False, *refs)

    outs = [shape(D // 2, WIDE)] * 2 + [shape(IMG, SEQ, D, dtype=F32)]
    return call(body, outs, [VM] * len(args), args, DENSE_SCRATCH, name="dense_backward_first", flops=1e10)


def experts_forward(recv, source):
    outs = [shape(SLOTS, D), shape(SLOTS, D)]
    return call(
        expert_forward, outs, [VM, HM], (recv, source), (WIDE_TILES, TALL_TILES, TILE_SEMS), name="expert_forward",
        flops=4e9, moved=9e6, limit=54,
    )


def experts_backward(last, args):
    def body(*refs):
        expert_backward(last, *refs)

    outs = [shape((2 if last else 1) * SLOTS, D), shape(SHARDS, LOCAL, 2 * D, FF_S)]
    return call(
        body, outs, [VM] * (len(args) - 1) + [HM], args, (WIDE_TILES, TALL_TILES, WIDE_TILES, TALL_TILES, TILE_SEMS, TILE_SEMS),
        name="expert_backward_last" if last else "expert_backward_first", flops=1e10, moved=2e7,
        out_specs=[VM, HM], limit=54 if last else 46,
    )


def across(value, dx, dc):
    moves = [(x * 2 + c, ((x + dx) % 4) * 2 + (c + dc) % 2) for x in range(4) for c in range(2)]
    return lax.ppermute(value, "dp", moves)


def swap_experts(value, chunk):
    arrived = lax.all_to_all(value.reshape(GROUPS, chunk, D), "experts", split_axis=0, concat_axis=0, tiled=True)
    return arrived.reshape(GROUPS * chunk, D)


def add(*values):
    total = values[0].astype(F32)
    for value in values[1:]:
        total = total + value.astype(F32)
    return total


def together(*values):
    return lax.optimization_barrier(values)


def sum_shards(grads):
    return lax.psum_scatter(grads, "dp", scatter_dimension=0, tiled=False)


def unpack_experts(layer, total, earlier=()):
    def body(total_ref, *refs):
        in_ref, out_ref, packed, wide, tall, sems, out_sems = refs[len(earlier) :]
        copies, sent = [], []
        for local in range(LOCAL):
            copies.append(pltpu.make_async_copy(total_ref.at[local], packed.at[local], sems.at[local]))
            copies[-1].start()
        for local in range(LOCAL):
            copies[local].wait()
            wide[local] = packed[local, :D].astype(F32)
            tall[local, :, :FF_S] = packed[local, D : D + FF_S].astype(F32)
            tall[local, :, FF_S:] = packed[local, D + FF_S :].astype(F32)
            for place, (here, far) in enumerate(((wide, in_ref), (tall, out_ref))):
                sent.append(pltpu.make_async_copy(here.at[local], far.at[layer, local], out_sems.at[local, place]))
                sent[-1].start()
        for copy in sent:
            copy.wait()

    in_shape, out_shape = (LOCAL, D, FF_S), (LOCAL, FF_S, D)
    scratch = (
        pltpu.VMEM((LOCAL, 2 * D, FF_S), BF),
        pltpu.VMEM(in_shape, F32),
        pltpu.VMEM(out_shape, F32),
        pltpu.SemaphoreType.DMA((LOCAL,)),
        pltpu.SemaphoreType.DMA((LOCAL, 2)),
    )
    outs = [shape(LAYERS, *in_shape, dtype=F32), shape(LAYERS, *out_shape, dtype=F32)]
    return call(
        body, outs, [HM] * (1 + len(earlier)), (total, *earlier), scratch, name="unpack_experts", flops=1e6,
        moved=6e6, out_specs=[HM] * 2, aliases={1: 0, 2: 1} if earlier else {}, limit=58,
    )


def unpack_dense(arrived):
    def body(arrived_ref, gain_ref, qkv_ref, proj_ref, router_ref):
        for layer in range(LAYERS):
            total = arrived_ref[0, layer].astype(F32)
            for chip in range(1, 4):
                total = total + arrived_ref[chip, layer].astype(F32)
            qkv_ref[layer] = total[:, :1536]
            proj_ref[layer] = total[:, 1536:2048]
            small = total[:, 2048:]
            router_ref[layer] = small[:, :EXPERTS]
            turned = jnp.concatenate([small, small], axis=0).T
            gain_ref[layer] = turned[EXPERTS : EXPERTS + 2, :4]

    outs = [shape(LAYERS, 2, 4, dtype=F32)] + [shape(LAYERS, 4, width, dtype=F32) for width in (1536, 512, EXPERTS)]
    return call(body, outs, [VM], (arrived,), name="unpack_dense", flops=1e6, moved=3e5)


def pack_experts(first, second):
    return jnp.concatenate([first, second[:, :, :FF_S], second[:, :, FF_S:]], axis=1)


def along(value, dy, dz):
    moves = [(y * 4 + z, ((y + dy) % 4) * 4 + (z + dz) % 4) for y in range(4) for z in range(4)]
    return lax.ppermute(value, "experts", moves)


def source_rows(relative):
    group, rank = lax.axis_index("experts"), lax.axis_index("dp")
    place = jnp.arange(D, dtype=jnp.int32)[None]
    half, rest = place // 256, place % 256
    if relative:
        block = ((group // 4 + rest // 64) % 4) * 4 + (group % 4 + rest // 16) % 4
    else:
        block = rest // 16
    chip = (rank // 2 + (rest % 16) // 4) % 4
    return block * 32 + chip * 8 + ((rank % 2 + half) % 2) * 4 + rest % 4


def target_rows():
    core = lax.axis_index("dp") % 2
    place = jnp.arange(D, dtype=jnp.int32)[:, None]
    half, rest = place // 256, place % 256
    return rest // 4 * 8 + ((core + half) % 2) * 4 + rest % 4


def near_dense(packed):
    return jnp.concatenate([packed, across(packed, -1, 0), across(packed, 2, 0), across(packed, 1, 0)], axis=1)


def swap_dense(stay, got):
    parts = add(stay, got).astype(BF).reshape(GROUPS, 16, WIDE)
    return lax.all_to_all(parts, "experts", split_axis=0, concat_axis=0, tiled=True)


def group_sums(arrived):
    return jnp.sum(arrived.astype(F32), axis=0).astype(BF).reshape(4, 4, WIDE)


def swap_chips(parts):
    columns = [[chip * 2 + core for chip in range(4)] for core in range(2)]
    return lax.all_to_all(
        jnp.stack(parts, axis=1), "dp", split_axis=0, concat_axis=0, tiled=True, axis_index_groups=columns
    )


def local(
    tokens,
    cotangent,
    norm_gain,
    qkv_weight,
    proj_weight,
    router_weight,
    expert_in,
    expert_out,
    routes,
):
    pad = ((0, ROWS - TOK), (0, 0))
    tokens_pad = jnp.pad(tokens.reshape(TOK, D), pad)
    grad_pad = jnp.pad(cotangent.reshape(TOK, D), pad)
    routes_pad = [jnp.pad(routes[layer].reshape(TOK, TOP), pad, constant_values=-1) for layer in range(LAYERS)]
    packed = jnp.concatenate(
        [
            qkv_weight,
            proj_weight,
            router_weight,
            norm_gain.transpose(0, 2, 1),
            jnp.zeros((LAYERS, 4, WIDE - 2048 - EXPERTS - 2), BF),
        ],
        axis=2,
    )
    near = near_dense(packed)
    expert_packs = [pack_experts(expert_in[layer], expert_out[layer]) for layer in range(LAYERS)]
    rows_from = [source_rows(False), source_rows(True)]
    rows_into = target_rows()
    experts_a = lax.all_gather(expert_packs[0], "dp", axis=0, tiled=False)
    near_b = near[1]
    half_a = lax.all_to_all(
        jnp.broadcast_to(near[0][None], (GROUPS, 16, WIDE)), "experts", split_axis=0, concat_axis=0, tiled=True
    ).reshape(D // 2, WIDE)
    half_a, near_b, pack_b, tokens_pad, grad_pad, rows_into, *rest = together(
        half_a, near_b, expert_packs[1], tokens_pad, grad_pad, rows_into, *routes_pad, *rows_from
    )
    routes_pad, rows_from = rest[:LAYERS], rest[LAYERS:]
    ring = [near_b, along(near_b, 0, -1), along(near_b, 0, 2), along(near_b, 0, 1)]
    x1_a, qkv_a, mixed_a, send, keep, weights_a = forward_first(
        half_a, across(half_a, 0, 1), rows_from[0], routes_pad[0], tokens_pad
    )
    send, *ring = together(send, *ring)
    near_b = jnp.concatenate(ring, axis=0)
    ring = [near_b, along(near_b, -1, 0), along(near_b, 2, 0), along(near_b, 1, 0)]
    recv = swap_experts(send, 24)
    experts_b = lax.all_gather(pack_b, "dp", axis=0, tiled=False)
    ret, rows_a = experts_forward(recv, experts_a)
    rows_a, *ring = together(rows_a, *ring)
    others = [across(piece, 0, 1) for piece in ring]
    ret_a = swap_experts(ret, 24)
    x_b, x1_b, qkv_b, mixed_b, send, weights_b = forward_last(
        *ring, *others, rows_from[1], routes_pad[1], grad_pad, x1_a, ret_a, keep
    )
    recv = swap_experts(send, 48)
    back_b, grads_b = experts_backward(True, (recv, experts_b))
    sums_b = sum_shards(grads_b)
    back_b = swap_experts(back_b, 48)
    stay_b, give_b, grad, output, send = backward_last(
        rows_into, weights_b, routes_pad[1], grad_pad, back_b, x1_b, x_b, qkv_b, mixed_b, keep
    )
    recv, got_b = together(swap_experts(send, 24), across(give_b, 0, 1))
    arrived_b = swap_dense(stay_b, got_b)
    back_a, grads_a = experts_backward(False, (rows_a, recv, experts_a))
    back_a, grads_a, arrived_b = together(back_a, grads_a, arrived_b)
    sums_a = sum_shards(grads_a)
    back_a = swap_experts(back_a, 24)
    stay_a, give_a, grad_tokens = backward_first(
        rows_into, weights_a, routes_pad[0], grad, ret_a, back_a, x1_a, tokens_pad, qkv_a, mixed_a
    )
    part_b = group_sums(arrived_b)
    arrived_a = swap_dense(stay_a, across(give_a, 0, 1))
    arrived_a, part_b, *early = together(arrived_a, part_b, *unpack_experts(1, sums_b))
    grad_in, grad_out = unpack_experts(0, sums_a, early)
    arrived, grad_in, grad_out = together(swap_chips([group_sums(arrived_a), part_b]), grad_in, grad_out)
    grad_gain, grad_qkv, grad_proj, grad_router = unpack_dense(arrived)
    return (
        output,
        grad_tokens,
        grad_gain,
        grad_qkv,
        grad_proj,
        grad_router,
        grad_in,
        grad_out,
    )


def solution(mesh):
    placed = (
        P(("experts", "dp"), None, None),
        P(("experts", "dp"), None, None),
        P(None, None, ("experts", "dp")),
        P(None, ("experts", "dp"), None),
        P(None, ("experts", "dp"), None),
        P(None, ("experts", "dp"), None),
        P(None, "experts", None, "dp"),
        P(None, "experts", "dp", None),
        P(None, ("experts", "dp"), None, None),
    )
    return jax.shard_map(
        local,
        mesh=mesh,
        in_specs=placed,
        out_specs=(
            P(("experts", "dp"), None, None),
            P(("experts", "dp"), None, None),
            P(None, None, ("experts", "dp")),
            P(None, ("experts", "dp"), None),
            P(None, ("experts", "dp"), None),
            P(None, ("experts", "dp"), None),
            P(None, "experts", None, "dp"),
            P(None, "experts", "dp", None),
        ),
        check_vma=False,
    )
```

```python
import jax
import jax.numpy as jnp
from jax import lax
from jax.experimental import pallas as pl
from jax.experimental.pallas import tpu as pltpu
from jax.sharding import PartitionSpec as P

HEADS = 8
HEAD_DIM = 64
EXPERTS = 32
TOP = 2
LAYERS = 2
CAP = 12
D = 512
SEQ = 50
IMG = 3
TOK = 150
ROWS = 160
GROUPS = 16
LOCAL = 2
SLOTS = 384
HALF = 192
SHARDS = 8
FF_S = 256
SPAN = 4
WIDE = 2176
EPS = 1e-06
SCALE = HEAD_DIM ** (-0.5)
GELU_C = 0.7978845608028654
GELU_A = 0.044715

BF = jnp.bfloat16
F32 = jnp.float32


def dot(a, b):
    return jnp.dot(a, b, preferred_element_type=F32)


def dot_nt(a, b):
    return lax.dot_general(a, b, (((1,), (1,)), ((), ())), preferred_element_type=F32)


def dot_tn(a, b):
    return lax.dot_general(a, b, (((0,), (0,)), ((), ())), preferred_element_type=F32)


def iota(shape, dim):
    return lax.broadcasted_iota(jnp.int32, shape, dim)


def normalize(values):
    centered = values - jnp.mean(values, axis=-1, keepdims=True)
    inverse = lax.rsqrt(jnp.mean(centered * centered, axis=-1, keepdims=True) + EPS)
    return centered * inverse, inverse


def norm_back(upstream, normed, inverse, gain):
    scaled = upstream * gain
    mean_grad = jnp.mean(scaled, axis=-1, keepdims=True)
    mean_prod = jnp.mean(scaled * normed, axis=-1, keepdims=True)
    return inverse * (scaled - mean_grad - normed * mean_prod)


def split_low(values):
    high = values.astype(BF)
    return high, (values - high.astype(F32)).astype(BF)


def same_image():
    def image(dim):
        place = iota((2 * ROWS, ROWS), dim)
        if dim == 0:
            place = jnp.where(place >= ROWS, place - ROWS, place)
        one = jnp.int32(1)
        zero = jnp.int32(0)
        return (
            jnp.where(place >= SEQ, one, zero)
            + jnp.where(place >= 2 * SEQ, one, zero)
            + jnp.where(place >= 3 * SEQ, one, zero)
        )

    return image(0) == image(1)


def halves(pair):
    low = iota(pair.shape, 1) < HEAD_DIM
    zero = jnp.zeros_like(pair)
    return jnp.concatenate([jnp.where(low, pair, zero), jnp.where(low, zero, pair)], axis=0)


def pair_probs(queries, keys, same):
    scores = jnp.where(same, dot_nt(queries, keys) * SCALE, -1e30)
    weights = jnp.exp(scores - jnp.max(scores, axis=-1, keepdims=True))
    return weights / jnp.sum(weights, axis=-1, keepdims=True)


def gains_of(block):
    turned = block.astype(F32).T
    return turned[EXPERTS : EXPERTS + 1], turned[EXPERTS + 1 : EXPERTS + 2]


def routing(second, block, routes, chunk):
    logits = dot(second, block)
    lanes = iota((ROWS, 128), 1)
    logits = jnp.where(lanes < EXPERTS, logits, -1e30)
    shifted = jnp.exp(logits - jnp.max(logits, axis=-1, keepdims=True))
    prob = shifted / jnp.sum(shifted, axis=-1, keepdims=True)
    masks = [jnp.where(lanes == routes[:, k : k + 1], 1.0, 0.0) for k in range(TOP)]
    chosen = [jnp.sum(mask * prob, axis=-1, keepdims=True) for mask in masks]
    total = jnp.where(routes[:, 0:1] >= 0, chosen[0] + chosen[1], 1.0)
    gates = [value / total for value in chosen]
    earlier = jnp.where(iota((ROWS, ROWS), 1) < iota((ROWS, ROWS), 0), 1.0, 0.0).astype(BF)
    before = dot(earlier, (masks[0] + masks[1]).astype(BF))
    places = []
    for k in range(TOP):
        slot = jnp.sum(masks[k] * before, axis=-1, keepdims=True).astype(jnp.int32)
        expert = routes[:, k : k + 1]
        base = (expert >> 1) * chunk + (expert & 1) * CAP
        places.append(jnp.where(expert >= 0, base + slot, -1))
    return prob, masks, total, gates, places


def picks(place, count):
    return jnp.where(iota((ROWS, count), 1) == place, 1.0, 0.0).astype(BF)


def columns_as_rows(columns):
    lanes = iota((ROWS, 128), 1)
    table = jnp.zeros((ROWS, 128), F32)
    for lane, column in enumerate(columns):
        table = jnp.where(lanes == lane, column.astype(F32), table)
    turned = table.T
    return [turned[lane : lane + 1].astype(jnp.int32) for lane in range(len(columns))]


def placed(place_row, count):
    return jnp.where(iota((count, ROWS), 0) == place_row, 1.0, 0.0).astype(BF)


def forward_kernel(last, *refs):
    if last:
        pieces, refs = refs[:8], refs[8:]
        (from_ref, routes_ref, grad_ref, prev_ref, ret_ref, keep_in,
         x_ref, x1_ref, qkv_ref, mixed_ref, send_ref, w_ref, rows_ref) = refs
        for place, piece in enumerate(pieces):
            rows_ref[place * 64 : (place + 1) * 64] = piece[...]
        near_ref, far_ref = rows_ref.at[: D // 2], rows_ref.at[D // 2 :]
        kept = keep_in[...]
        back = ret_ref[...]
        stream = prev_ref[...]
        for k in range(TOP):
            place = kept[:, 2 + k : 3 + k].astype(jnp.int32)
            stream = stream + kept[:, k : k + 1] * dot(picks(place, SLOTS), back)
        x_ref[...] = stream
    else:
        (near_ref, far_ref, from_ref, routes_ref, tokens_ref, x1_ref, qkv_ref, mixed_ref, send_ref, keep_ref, w_ref) = refs
        stream = tokens_ref[...].astype(F32)
    chunk = 48 if last else 24
    order = jnp.where(iota((D, D), 0) == from_ref[...], 1.0, 0.0).astype(BF)
    for left, right in ((0, 512), (512, 1024), (1024, 1536), (1536, 2048), (2048, WIDE)):
        w_ref[:, left:right] = (
            dot(order[:, : D // 2], near_ref[:, left:right]) + dot(order[:, D // 2 :], far_ref[:, left:right])
        ).astype(BF)
    block = w_ref[:, 2048:WIDE]
    gain_one, gain_two = gains_of(block)
    normed, _ = normalize(stream)
    first = (normed * gain_one).astype(BF)
    qkv_ref[...] = dot(first, w_ref[:, :1536]).astype(BF)
    same = same_image()
    low_half = iota((ROWS, 128), 1) < HEAD_DIM
    for pair in range(HEADS // 2):
        left = pair * 128
        query = qkv_ref[:, left : left + 128]
        keys = qkv_ref[:, 512 + left : 640 + left]
        values = qkv_ref[:, 1024 + left : 1152 + left]
        both = dot(pair_probs(halves(query), keys, same).astype(BF), values)
        mixed_ref[:, left : left + 128] = jnp.where(low_half, both[:ROWS], both[ROWS:]).astype(BF)
    residual = stream + dot(mixed_ref[...], w_ref[:, 1536:2048])
    x1_ref[...] = residual
    normed_two, _ = normalize(residual)
    second = (normed_two * gain_two).astype(BF)
    _, _, _, gates, places = routing(second, block, routes_ref[...], chunk)
    count = GROUPS * chunk
    place_rows = columns_as_rows(places)
    outgoing = dot(placed(place_rows[0], count) + placed(place_rows[1], count), second)
    if last:
        grad = grad_ref[...].astype(F32)
        for k in range(TOP):
            target = jnp.where(place_rows[k] >= 0, place_rows[k] + 24, -1)
            outgoing = outgoing + dot(placed(target, count), (gates[k] * grad).astype(BF))
    else:
        lanes = iota((ROWS, 128), 1)
        kept = jnp.where(lanes == 0, gates[0], jnp.where(lanes == 1, gates[1], 0.0))
        kept = jnp.where(lanes == 2, places[0].astype(F32), kept)
        keep_ref[...] = jnp.where(lanes == 3, places[1].astype(F32), kept)
    send_ref[...] = outgoing.astype(BF)


def backward_kernel(last, *refs):
    if last:
        (into_ref, w_ref, routes_ref, grad_ref, back_ref, x1_ref, x_ref, qkv_ref, mixed_ref, keep_in,
         stay_ref, give_ref, prev_ref, out_ref, send_ref, dqkv_ref) = refs
        chunk = 48
    else:
        (into_ref, w_ref, routes_ref, grad_ref, ret_ref, back_ref, x1_ref, x_ref, qkv_ref, mixed_ref,
         stay_ref, give_ref, prev_ref, dqkv_ref) = refs
        chunk = 24
    count = GROUPS * chunk
    order = jnp.where(iota((D, D), 1) == into_ref[...], 1.0, 0.0).astype(BF)

    def ordered(values):
        return dot_nt(order, values).astype(BF)

    def store(left, right, values):
        stay_ref[:, left:right] = values[: D // 2].astype(BF)
        give_ref[:, left:right] = values[D // 2 :].astype(BF)

    block = w_ref[:, 2048:WIDE]
    gain_one, gain_two = gains_of(block)
    grad = grad_ref[...].astype(F32)
    residual = x1_ref[...]
    normed_two, inverse_two = normalize(residual)
    second = (normed_two * gain_two).astype(BF)
    prob, masks, total, gates, places = routing(second, block, routes_ref[...], chunk)
    chooser = [picks(place, count) for place in places]
    back = back_ref[...]
    if last:
        returned = back
        shift = [picks(jnp.where(place >= 0, place + 24, -1), count) for place in places]
        drow = dot(shift[0] + shift[1], back)
    else:
        returned = ret_ref[...]
        drow = dot(chooser[0] + chooser[1], back)
    combined = [dot(choice, returned) for choice in chooser]
    if last:
        output = residual + (gates[0] * combined[0] + gates[1] * combined[1])
        for image in range(IMG):
            out_ref[image] = output[image * SEQ : (image + 1) * SEQ].astype(BF)
    dgate = [jnp.sum(grad * value, axis=-1, keepdims=True) for value in combined]
    inner = dgate[0] * gates[0] + dgate[1] * gates[1]
    dprob = sum((dgate[k] - inner) / total * masks[k] for k in range(TOP))
    dlogit = prob * (dprob - jnp.sum(dprob * prob, axis=-1, keepdims=True))
    logit_high, logit_low = split_low(dlogit)
    dsecond = dot_nt(logit_high, block) + dot_nt(logit_low, block) + drow
    second = ordered(second)
    small = dot(second, logit_high) + dot(second, logit_low)
    lanes = iota((ROWS, 128), 1)
    gain_grad_two = jnp.sum(dsecond * normed_two, axis=0, keepdims=True)
    grad = grad + norm_back(dsecond, normed_two, inverse_two, gain_two)
    branch = grad.astype(BF)
    store(1536, 2048, dot(ordered(mixed_ref[...]), branch))
    dmixed = dot_nt(branch, w_ref[:, 1536:2048]).astype(BF)
    same = same_image()
    low_half = lanes < HEAD_DIM
    for pair in range(HEADS // 2):
        left = pair * 128
        query = qkv_ref[:, left : left + 128]
        keys = qkv_ref[:, 512 + left : 640 + left]
        values = qkv_ref[:, 1024 + left : 1152 + left]
        queries = halves(query)
        upstream = halves(dmixed[:, left : left + 128])
        probs = pair_probs(queries, keys, same)
        dv = dot_tn(probs.astype(BF), upstream)
        dprobs = dot_nt(upstream, values)
        dscores = (probs * (dprobs - jnp.sum(dprobs * probs, axis=-1, keepdims=True))).astype(BF)
        dq = dot(dscores, keys) * SCALE
        dk = dot_tn(dscores, queries) * SCALE
        dqkv_ref[:, left : left + 128] = jnp.where(low_half, dq[:ROWS], dq[ROWS:]).astype(BF)
        dqkv_ref[:, 512 + left : 640 + left] = dk.astype(BF)
        dqkv_ref[:, 1024 + left : 1152 + left] = dv.astype(BF)
    normed, inverse = normalize(x_ref[...].astype(F32))
    first = (normed * gain_one).astype(BF)
    dqkv = dqkv_ref[...]
    first = ordered(first)
    for left in range(0, 1536, 512):
        store(left, left + 512, dot(first, dqkv[:, left : left + 512]))
    dfirst = dot_nt(dqkv, w_ref[:, :1536])
    gain_grad_one = jnp.sum(dfirst * normed, axis=0, keepdims=True)
    places = iota((128, D), 0)
    gain_grads = jnp.where(places == EXPERTS, gain_grad_one, jnp.where(places == EXPERTS + 1, gain_grad_two, 0.0))
    high, low = split_low(gain_grads)
    store(2048, WIDE, small + dot_nt(order, high) + dot_nt(order, low))
    grad = grad + norm_back(dfirst, normed, inverse, gain_one)
    if last:
        prev_ref[...] = grad
        kept = keep_in[...]
        outgoing = jnp.zeros((SLOTS, D), F32)
        place_rows = columns_as_rows([kept[:, 2 + k : 3 + k] for k in range(TOP)])
        for k in range(TOP):
            outgoing = outgoing + dot(placed(place_rows[k], SLOTS), (kept[:, k : k + 1] * grad).astype(BF))
        send_ref[...] = outgoing.astype(BF)
    else:
        for image in range(IMG):
            prev_ref[image] = grad[image * SEQ : (image + 1) * SEQ]


def arrange(chunk, shift, turned=False):
    count = GROUPS * chunk
    place = iota((1, SLOTS) if turned else (SLOTS, 1), 1 if turned else 0)
    local = jnp.where(place >= HALF, jnp.int32(1), jnp.int32(0))
    rest = place - local * HALF
    source = (rest * 171) >> 11
    target = source * chunk + local * CAP + (rest - source * CAP) + shift
    other = iota((count, SLOTS), 0) if turned else iota((SLOTS, count), 1)
    return jnp.where(other == target, 1.0, 0.0).astype(BF)


def tile_copies(packed, local, step, wide, tall, sems):
    span, part = step // SPAN, step % SPAN
    columns = pl.ds(part * FF_S, FF_S)
    shard = packed.at[step, local]
    pairs = (
        (shard.at[pl.ds(0, D)], wide.at[local, span, :, columns]),
        (shard.at[pl.ds(D, FF_S)], tall.at[local, span, columns, pl.ds(0, FF_S)]),
        (shard.at[pl.ds(D + FF_S, FF_S)], tall.at[local, span, columns, pl.ds(FF_S, FF_S)]),
    )
    return [(far, here, sems.at[local, step, place]) for place, (far, here) in enumerate(pairs)]


def load_weights(packed, wide, tall, sems):
    copies = []
    for local in range(LOCAL):
        for step in range(SHARDS):
            for far, here, sem in tile_copies(packed, local, step, wide, tall, sems):
                copy = pltpu.make_async_copy(far, here, sem)
                copy.start()
                copies.append(copy)
    return copies


def wait_span(copies, local, span):
    first = 3 * (local * SHARDS + span * SPAN)
    for copy in copies[first : first + 3 * SPAN]:
        copy.wait()


def expert_forward(recv_ref, packed, ret_ref, rows_ref, wide, tall, sems):
    copies = load_weights(packed, wide, tall, sems)
    rows_ref[...] = dot(arrange(24, 0), recv_ref[...]).astype(BF)
    totals = []
    for local in range(LOCAL):
        rows = rows_ref[local * HALF : (local + 1) * HALF]
        total = jnp.zeros((HALF, D), F32)
        for span in range(SHARDS // SPAN):
            wait_span(copies, local, span)
            pre = dot(rows, wide[local, span])
            bend = jnp.tanh(GELU_C * (pre + GELU_A * pre * pre * pre))
            hidden = (0.5 * pre * (1.0 + bend)).astype(BF)
            total = total + dot(hidden, tall[local, span])
        totals.append(total.astype(BF))
    ret_ref[...] = dot(arrange(24, 0, True), jnp.concatenate(totals, axis=0)).astype(BF)


def expert_backward(last, *refs):
    if last:
        recv_ref, packed, back_ref, grads_to, wide, tall, wide_out, tall_out, sems, out_sems = refs
    else:
        rows_ref, recv_ref, packed, back_ref, grads_to, wide, tall, wide_out, tall_out, sems, out_sems = refs
    copies = load_weights(packed, wide, tall, sems)
    recv = recv_ref[...]
    if last:
        rows_all = dot(arrange(48, 0), recv).astype(BF)
        grads_all = dot(arrange(48, 24), recv).astype(BF)
    else:
        rows_all = rows_ref[...]
        grads_all = dot(arrange(24, 0), recv).astype(BF)
    totals, back_totals, sent = [], [], []
    for local in range(LOCAL):
        rows = rows_all[local * HALF : (local + 1) * HALF]
        grads = grads_all[local * HALF : (local + 1) * HALF]
        rows_turned = rows.T
        total = jnp.zeros((HALF, D), F32)
        back_total = jnp.zeros((HALF, D), F32)
        for span in range(SHARDS // SPAN):
            wait_span(copies, local, span)
            first_use = wide[local, span]
            second_use = tall[local, span]
            pre = dot(rows, first_use)
            slope_in = dot_nt(grads, second_use)
            square = pre * pre
            bend = jnp.tanh(GELU_C * (pre + GELU_A * pre * square))
            hidden = (0.5 * pre * (1.0 + bend)).astype(BF)
            slope = 0.5 * (1.0 + bend) + (0.5 * GELU_C) * pre * (1.0 - bend * bend) * (
                1.0 + (3.0 * GELU_A) * square
            )
            dpre = (slope_in * slope).astype(BF)
            if last:
                total = total + dot(hidden, second_use)
            back_total = back_total + dot_nt(dpre, first_use)
            wide_out[local, span] = dot(rows_turned, dpre).astype(BF)
            tall_out[local, span] = dot_tn(hidden, grads).astype(BF)
            for step in range(span * SPAN, (span + 1) * SPAN):
                for far, here, sem in tile_copies(grads_to, local, step, wide_out, tall_out, out_sems):
                    copy = pltpu.make_async_copy(here, far, sem)
                    copy.start()
                    sent.append(copy)
        totals.append(total.astype(BF))
        back_totals.append(back_total.astype(BF))
    result = dot(arrange(48 if last else 24, 24 if last else 0, True), jnp.concatenate(back_totals, axis=0))
    if last:
        result = result + dot(arrange(48, 0, True), jnp.concatenate(totals, axis=0))
    back_ref[...] = result.astype(BF)
    for copy in sent:
        copy.wait()


VM = pl.BlockSpec(memory_space=pltpu.VMEM)
HM = pl.BlockSpec(memory_space=pltpu.HBM)


def shape(*dims, dtype=BF):
    return jax.ShapeDtypeStruct(dims, dtype)


def call(body, outs, in_specs, args, scratch=(), flops=1e9, moved=4e6, name=None, limit=24, out_specs=None, aliases={}):
    return pl.pallas_call(
        body,
        out_shape=outs,
        in_specs=in_specs,
        out_specs=out_specs or [VM] * len(outs),
        scratch_shapes=list(scratch),
        input_output_aliases=aliases,
        compiler_params=pltpu.CompilerParams(vmem_limit_bytes=limit * 1024 * 1024),
        cost_estimate=pl.CostEstimate(flops=int(flops), bytes_accessed=int(moved), transcendentals=0),
        name=name,
    )(*args)


WIDE_TILES = pltpu.VMEM((LOCAL, SHARDS // SPAN, D, SPAN * FF_S), BF)
TALL_TILES = pltpu.VMEM((LOCAL, SHARDS // SPAN, SPAN * FF_S, D), BF)
TILE_SEMS = pltpu.SemaphoreType.DMA((LOCAL, SHARDS, 3))


def forward_first(*args):
    def body(*refs):
        forward_kernel(False, *refs)

    outs = [shape(ROWS, D, dtype=F32), shape(ROWS, 1536), shape(ROWS, D), shape(SLOTS, D), shape(ROWS, 128, dtype=F32), shape(D, WIDE)]
    return call(body, outs, [VM] * len(args), args, name="dense_forward_first", flops=4e9)


def forward_last(*args):
    def body(*refs):
        forward_kernel(True, *refs)

    outs = [shape(ROWS, D, dtype=F32), shape(ROWS, D, dtype=F32), shape(ROWS, 1536), shape(ROWS, D), shape(2 * SLOTS, D), shape(D, WIDE)]
    return call(
        body, outs, [VM] * len(args), args, [pltpu.VMEM((D, WIDE), BF)], name="dense_forward_last", flops=4e9, limit=58
    )


DENSE_SCRATCH = (pltpu.VMEM((ROWS, 1536), BF),)


def backward_last(*args):
    def body(*refs):
        backward_kernel(True, *refs)

    outs = [shape(D // 2, WIDE)] * 2 + [shape(ROWS, D, dtype=F32), shape(IMG, SEQ, D), shape(SLOTS, D)]
    return call(body, outs, [VM] * len(args), args, DENSE_SCRATCH, name="dense_backward_last", flops=1e10)


def backward_first(*args):
    def body(*refs):
        backward_kernel(False, *refs)

    outs = [shape(D // 2, WIDE)] * 2 + [shape(IMG, SEQ, D, dtype=F32)]
    return call(body, outs, [VM] * len(args), args, DENSE_SCRATCH, name="dense_backward_first", flops=1e10)


def experts_forward(recv, source):
    outs = [shape(SLOTS, D), shape(SLOTS, D)]
    return call(
        expert_forward, outs, [VM, HM], (recv, source), (WIDE_TILES, TALL_TILES, TILE_SEMS), name="expert_forward",
        flops=4e9, moved=9e6, limit=54,
    )


def experts_backward(last, args):
    def body(*refs):
        expert_backward(last, *refs)

    outs = [shape((2 if last else 1) * SLOTS, D), shape(SHARDS, LOCAL, 2 * D, FF_S)]
    return call(
        body, outs, [VM] * (len(args) - 1) + [HM], args, (WIDE_TILES, TALL_TILES, WIDE_TILES, TALL_TILES, TILE_SEMS, TILE_SEMS),
        name="expert_backward_last" if last else "expert_backward_first", flops=1e10, moved=2e7,
        out_specs=[VM, HM], limit=46,
    )


def across(value, dx, dc):
    moves = [(x * 2 + c, ((x + dx) % 4) * 2 + (c + dc) % 2) for x in range(4) for c in range(2)]
    return lax.ppermute(value, "dp", moves)


def swap_experts(value, chunk):
    arrived = lax.all_to_all(value.reshape(GROUPS, chunk, D), "experts", split_axis=0, concat_axis=0, tiled=True)
    return arrived.reshape(GROUPS * chunk, D)


def add(*values):
    total = values[0].astype(F32)
    for value in values[1:]:
        total = total + value.astype(F32)
    return total


def together(*values):
    return lax.optimization_barrier(values)


def sum_shards(grads):
    return lax.psum_scatter(grads, "dp", scatter_dimension=0, tiled=False)


def unpack_experts(layer, total, earlier=()):
    def body(total_ref, *refs):
        in_ref, out_ref, packed, wide, tall, sems, out_sems = refs[len(earlier) :]
        copies, sent = [], []
        for local in range(LOCAL):
            copies.append(pltpu.make_async_copy(total_ref.at[local], packed.at[local], sems.at[local]))
            copies[-1].start()
        for local in range(LOCAL):
            copies[local].wait()
            wide[local] = packed[local, :D].astype(F32)
            tall[local, :, :FF_S] = packed[local, D : D + FF_S].astype(F32)
            tall[local, :, FF_S:] = packed[local, D + FF_S :].astype(F32)
            for place, (here, far) in enumerate(((wide, in_ref), (tall, out_ref))):
                sent.append(pltpu.make_async_copy(here.at[local], far.at[layer, local], out_sems.at[local, place]))
                sent[-1].start()
        for copy in sent:
            copy.wait()

    in_shape, out_shape = (LOCAL, D, FF_S), (LOCAL, FF_S, D)
    scratch = (
        pltpu.VMEM((LOCAL, 2 * D, FF_S), BF),
        pltpu.VMEM(in_shape, F32),
        pltpu.VMEM(out_shape, F32),
        pltpu.SemaphoreType.DMA((LOCAL,)),
        pltpu.SemaphoreType.DMA((LOCAL, 2)),
    )
    outs = [shape(LAYERS, *in_shape, dtype=F32), shape(LAYERS, *out_shape, dtype=F32)]
    return call(
        body, outs, [HM] * (1 + len(earlier)), (total, *earlier), scratch, name="unpack_experts", flops=1e6,
        moved=6e6, out_specs=[HM] * 2, aliases={1: 0, 2: 1} if earlier else {}, limit=58,
    )


def unpack_dense(arrived):
    def body(arrived_ref, gain_ref, qkv_ref, proj_ref, router_ref):
        for layer in range(LAYERS):
            total = arrived_ref[0, layer].astype(F32)
            for chip in range(1, 4):
                total = total + arrived_ref[chip, layer].astype(F32)
            qkv_ref[layer] = total[:, :1536]
            proj_ref[layer] = total[:, 1536:2048]
            small = total[:, 2048:]
            router_ref[layer] = small[:, :EXPERTS]
            turned = jnp.concatenate([small, small], axis=0).T
            gain_ref[layer] = turned[EXPERTS : EXPERTS + 2, :4]

    outs = [shape(LAYERS, 2, 4, dtype=F32)] + [shape(LAYERS, 4, width, dtype=F32) for width in (1536, 512, EXPERTS)]
    return call(body, outs, [VM], (arrived,), name="unpack_dense", flops=1e6, moved=3e5)


def pack_experts(first, second):
    return jnp.concatenate([first, second[:, :, :FF_S], second[:, :, FF_S:]], axis=1)


def along(value, dy, dz):
    moves = [(y * 4 + z, ((y + dy) % 4) * 4 + (z + dz) % 4) for y in range(4) for z in range(4)]
    return lax.ppermute(value, "experts", moves)


def source_rows(relative):
    group, rank = lax.axis_index("experts"), lax.axis_index("dp")
    place = jnp.arange(D, dtype=jnp.int32)[None]
    half, rest = place // 256, place % 256
    if relative:
        block = ((group // 4 + rest // 64) % 4) * 4 + (group % 4 + rest // 16) % 4
    else:
        block = rest // 16
    chip = (rank // 2 + (rest % 16) // 4) % 4
    return block * 32 + chip * 8 + ((rank % 2 + half) % 2) * 4 + rest % 4


def target_rows():
    core = lax.axis_index("dp") % 2
    place = jnp.arange(D, dtype=jnp.int32)[:, None]
    half, rest = place // 256, place % 256
    return rest // 4 * 8 + ((core + half) % 2) * 4 + rest % 4


def near_dense(packed):
    return jnp.concatenate([packed, across(packed, -1, 0), across(packed, 2, 0), across(packed, 1, 0)], axis=1)


def swap_dense(stay, got):
    parts = add(stay, got).astype(BF).reshape(GROUPS, 16, WIDE)
    return lax.all_to_all(parts, "experts", split_axis=0, concat_axis=0, tiled=True)


def group_sums(arrived):
    return jnp.sum(arrived.astype(F32), axis=0).astype(BF).reshape(4, 4, WIDE)


def swap_chips(parts):
    columns = [[chip * 2 + core for chip in range(4)] for core in range(2)]
    return lax.all_to_all(
        jnp.stack(parts, axis=1), "dp", split_axis=0, concat_axis=0, tiled=True, axis_index_groups=columns
    )


def local(
    tokens,
    cotangent,
    norm_gain,
    qkv_weight,
    proj_weight,
    router_weight,
    expert_in,
    expert_out,
    routes,
):
    pad = ((0, ROWS - TOK), (0, 0))
    tokens_pad = jnp.pad(tokens.reshape(TOK, D), pad)
    grad_pad = jnp.pad(cotangent.reshape(TOK, D), pad)
    routes_pad = [jnp.pad(routes[layer].reshape(TOK, TOP), pad, constant_values=-1) for layer in range(LAYERS)]
    packed = jnp.concatenate(
        [
            qkv_weight,
            proj_weight,
            router_weight,
            norm_gain.transpose(0, 2, 1),
            jnp.zeros((LAYERS, 4, WIDE - 2048 - EXPERTS - 2), BF),
        ],
        axis=2,
    )
    near = near_dense(packed)
    expert_packs = [pack_experts(expert_in[layer], expert_out[layer]) for layer in range(LAYERS)]
    rows_from = [source_rows(False), source_rows(True)]
    rows_into = target_rows()
    experts_a = lax.all_gather(expert_packs[0], "dp", axis=0, tiled=False)
    near_b = near[1]
    half_a = lax.all_to_all(
        jnp.broadcast_to(near[0][None], (GROUPS, 16, WIDE)), "experts", split_axis=0, concat_axis=0, tiled=True
    ).reshape(D // 2, WIDE)
    half_a, near_b, pack_b, tokens_pad, grad_pad, rows_into, *rest = together(
        half_a, near_b, expert_packs[1], tokens_pad, grad_pad, rows_into, *routes_pad, *rows_from
    )
    routes_pad, rows_from = rest[:LAYERS], rest[LAYERS:]
    ring = [near_b, along(near_b, 0, -1), along(near_b, 0, 2), along(near_b, 0, 1)]
    x1_a, qkv_a, mixed_a, send, keep, weights_a = forward_first(
        half_a, across(half_a, 0, 1), rows_from[0], routes_pad[0], tokens_pad
    )
    send, *ring = together(send, *ring)
    near_b = jnp.concatenate(ring, axis=0)
    ring = [near_b, along(near_b, -1, 0), along(near_b, 2, 0), along(near_b, 1, 0)]
    recv = swap_experts(send, 24)
    experts_b = lax.all_gather(pack_b, "dp", axis=0, tiled=False)
    ret, rows_a = experts_forward(recv, experts_a)
    rows_a, *ring = together(rows_a, *ring)
    others = [across(piece, 0, 1) for piece in ring]
    ret_a = swap_experts(ret, 24)
    x_b, x1_b, qkv_b, mixed_b, send, weights_b = forward_last(
        *ring, *others, rows_from[1], routes_pad[1], grad_pad, x1_a, ret_a, keep
    )
    recv = swap_experts(send, 48)
    back_b, grads_b = experts_backward(True, (recv, experts_b))
    sums_b = sum_shards(grads_b)
    back_b = swap_experts(back_b, 48)
    stay_b, give_b, grad, output, send = backward_last(
        rows_into, weights_b, routes_pad[1], grad_pad, back_b, x1_b, x_b, qkv_b, mixed_b, keep
    )
    recv, got_b = together(swap_experts(send, 24), across(give_b, 0, 1))
    arrived_b = swap_dense(stay_b, got_b)
    back_a, grads_a = experts_backward(False, (rows_a, recv, experts_a))
    back_a, grads_a, arrived_b = together(back_a, grads_a, arrived_b)
    sums_a = sum_shards(grads_a)
    back_a = swap_experts(back_a, 24)
    stay_a, give_a, grad_tokens = backward_first(
        rows_into, weights_a, routes_pad[0], grad, ret_a, back_a, x1_a, tokens_pad, qkv_a, mixed_a
    )
    part_b = group_sums(arrived_b)
    arrived_a = swap_dense(stay_a, across(give_a, 0, 1))
    arrived_a, part_b, *early = together(arrived_a, part_b, *unpack_experts(1, sums_b))
    grad_in, grad_out = unpack_experts(0, sums_a, early)
    arrived, grad_in, grad_out = together(swap_chips([group_sums(arrived_a), part_b]), grad_in, grad_out)
    grad_gain, grad_qkv, grad_proj, grad_router = unpack_dense(arrived)
    return (
        output,
        grad_tokens,
        grad_gain,
        grad_qkv,
        grad_proj,
        grad_router,
        grad_in,
        grad_out,
    )


def solution(mesh):
    placed = (
        P(("experts", "dp"), None, None),
        P(("experts", "dp"), None, None),
        P(None, None, ("experts", "dp")),
        P(None, ("experts", "dp"), None),
        P(None, ("experts", "dp"), None),
        P(None, ("experts", "dp"), None),
        P(None, "experts", None, "dp"),
        P(None, "experts", "dp", None),
        P(None, ("experts", "dp"), None, None),
    )
    return jax.shard_map(
        local,
        mesh=mesh,
        in_specs=placed,
        out_specs=(
            P(("experts", "dp"), None, None),
            P(("experts", "dp"), None, None),
            P(None, None, ("experts", "dp")),
            P(None, ("experts", "dp"), None),
            P(None, ("experts", "dp"), None),
            P(None, ("experts", "dp"), None),
            P(None, "experts", None, "dp"),
            P(None, "experts", "dp", None),
        ),
        check_vma=False,
    )
```
